32 devices in a mesh: fsdp: 8 (over y, x, core), ctx: 4 (over z).
Axes of the slice: x: 2, y: 2, z: 4, core: 2. Of those that a mesh axis runs over, the one named last changes fastest.
Arguments:
- tokens: bfloat16 [16384, 1024], P(('fsdp', 'ctx')), may hold values from -6 to 6
- value_first: bfloat16 [16384, 1024], P(('fsdp', 'ctx')), may hold values from -6 to 6
- lengths: int32 [8, 4], P('fsdp'), may hold values from 64 to 1792, as said below
- w_query: float32 [1024, 1024], P('fsdp', 'ctx'), may hold values from -0.1875 to 0.1875
- w_key: float32 [1024, 1024], P('fsdp', 'ctx'), may hold values from -0.1875 to 0.1875
- w_value: float32 [1024, 1024], P('fsdp', 'ctx'), may hold values from -0.1875 to 0.1875
- w_out: float32 [1024, 1024], P('fsdp', 'ctx'), may hold values from -0.75 to 0.75
- w_gate: float32 [1024, 2816], P('fsdp', 'ctx'), may hold values from -0.1875 to 0.1875
- w_up: float32 [1024, 2816], P('fsdp', 'ctx'), may hold values from -0.1875 to 0.1875
- w_down: float32 [2816, 1024], P('fsdp', 'ctx'), may hold values from -0.109375 to 0.109375
- gain_attn: float32 [1024], P('fsdp'), may hold values from 0.5 to 1.5
- gain_ffn: float32 [1024], P('fsdp'), may hold values from 0.5 to 1.5
- out_grad: bfloat16 [16384, 1024], P(('fsdp', 'ctx')), may hold values from -6 to 6
- value_grad: float32 [16384, 1024], P(('fsdp', 'ctx')), may hold values from -6 to 6
Outputs:
- output: bfloat16 [16384, 1024], P(('fsdp', 'ctx'))
- input_grad: float32 [16384, 1024], P(('fsdp', 'ctx'))
- value_first_grad: float32 [16384, 1024], P(('fsdp', 'ctx'))
- grad_query: float32 [1024, 1024], P('fsdp', 'ctx')
- grad_key: float32 [1024, 1024], P('fsdp', 'ctx')
- grad_value: float32 [1024, 1024], P('fsdp', 'ctx')
- grad_out: float32 [1024, 1024], P('fsdp', 'ctx')
- grad_gate: float32 [1024, 2816], P('fsdp', 'ctx')
- grad_up: float32 [1024, 2816], P('fsdp', 'ctx')
- grad_down: float32 [2816, 1024], P('fsdp', 'ctx')
- grad_gain_attn: float32 [1024], P('fsdp')
- grad_gain_ffn: float32 [1024], P('fsdp')
The draws below stay inside these ranges and needn't reach their ends.
Inputs may be any that keep to these rules, and one draw needn't show every extreme that they name: `lengths`: row f sums to 2048; exactly one entry of each row is 1792, the others are short.
All inputs are finite; a program needn't handle non-finite values.
Results may differ from the reference program's by a relative error of at most 0.022.
Values may be sent and summed in bfloat16 or wider, within the bound.
A program may use at most 256 MiB of HBM per device.

```python
import math
import jax
import jax.numpy as jnp
from jax import lax

D = 1024
HEADS = 16
HEAD = 64
FF = 2816
TOK_DEV = 512
SHORTS = 3
MIN_LEN = 64
GROUP = 2048
TOKENS = 16384
N_FSDP = 8
N_CTX = 4


def draw_lengths(key, part):
    key = jax.random.fold_in(key, 11)
    cut_key, place_key = jax.random.split(key)
    leftover = TOK_DEV // 2 - SHORTS * MIN_LEN
    cut_points = jnp.sort(jax.random.randint(cut_key, (N_FSDP, SHORTS - 1), 0, leftover + 1), axis=1)
    boundaries = jnp.concatenate([jnp.zeros((N_FSDP, 1), jnp.int32), cut_points.astype(jnp.int32), jnp.full((N_FSDP, 1), leftover, jnp.int32)], axis=1)
    shorts_drawn = MIN_LEN + boundaries[:, 1:] - boundaries[:, :-1]
    long_place = jax.random.randint(place_key, (N_FSDP, 1), 0, SHORTS + 1)
    slot_index = jnp.arange(SHORTS + 1, dtype=jnp.int32)[None, :]
    source_slot = jnp.clip(slot_index - (slot_index > long_place).astype(jnp.int32), 0, SHORTS - 1)
    source_slot = jnp.broadcast_to(source_slot, (N_FSDP, SHORTS + 1))
    short_values = jnp.take_along_axis(shorts_drawn, source_slot, axis=1)
    return jnp.where(slot_index == long_place, N_CTX * TOK_DEV - TOK_DEV // 2, short_values).astype(jnp.int32)


def shard_levels(key, extent, cuts, low, high):
    def one(position, parts):
        steps = jax.random.uniform(jax.random.fold_in(jax.random.fold_in(key, 6), position), (parts,), jnp.float32, low / len(cuts), high / len(cuts))
        return jnp.repeat(jnp.exp(steps), extent[position] // parts).reshape((-1,) + (1,) * (len(extent) - position - 1))

    gain = one(*cuts[0])
    for cut in cuts[1:]:
        gain = gain * one(*cut)
    return gain


def gaussian(rng, shape, spread, most, pieces=(), kind=jnp.bfloat16):
    loudness = shard_levels(rng, shape, pieces, -0.22, 0.18) if pieces else 1.0
    result = jax.random.normal(rng, shape, jnp.float32) * spread * loudness
    return jnp.minimum(jnp.maximum(result, -most), most).astype(kind)


def setup_inputs(seed: int = 0) -> dict:
    seeds = jax.random.split(jax.random.key(seed), 15)
    return {
        "tokens": gaussian(seeds[0], (TOKENS, D), 1.0, 6.0, ((0, 32),)),
        "value_first": gaussian(seeds[1], (TOKENS, D), 1.0, 6.0, ((0, 32),)),
        "lengths": draw_lengths(jax.random.fold_in(seeds[14], 71), 0),
        "w_query": gaussian(seeds[3], (D, D), D ** -0.5, 0.1875, ((0, 8), (1, 4)), jnp.float32),
        "w_key": gaussian(seeds[4], (D, D), D ** -0.5, 0.1875, ((0, 8), (1, 4)), jnp.float32),
        "w_value": gaussian(seeds[5], (D, D), D ** -0.5, 0.1875, ((0, 8), (1, 4)), jnp.float32),
        "w_out": gaussian(seeds[6], (D, D), (D // 16) ** -0.5, 0.75, ((0, 8), (1, 4)), jnp.float32),
        "w_gate": gaussian(seeds[7], (D, FF), D ** -0.5, 0.1875, ((0, 8), (1, 4)), jnp.float32),
        "w_up": gaussian(seeds[8], (D, FF), D ** -0.5, 0.1875, ((0, 8), (1, 4)), jnp.float32),
        "w_down": gaussian(seeds[9], (FF, D), FF ** -0.5, 0.109375, ((0, 8), (1, 4)), jnp.float32),
        "gain_attn": jnp.clip(1.0 + 0.1 * jax.random.normal(seeds[10], (D,), jnp.float32), 0.5, 1.5),
        "gain_ffn": jnp.clip(1.0 + 0.1 * jax.random.normal(seeds[11], (D,), jnp.float32), 0.5, 1.5),
        "out_grad": gaussian(seeds[12], (TOKENS, D), 1.0, 6.0, ((0, 32),)),
        "value_grad": gaussian(seeds[13], (TOKENS, D), 1.0, 6.0, ((0, 32),), jnp.float32),
    }


@jax.custom_vjp
def low(v):
    return lax.optimization_barrier(v.astype(jnp.bfloat16)).astype(jnp.float32)

@jax.custom_vjp
def low_back(v):
    return v

def low_keep(v):
    return (low(v), None)

def low_pass(kept, grad):
    return (grad,)

def back_keep(v):
    return (v, None)

def back_low(kept, grad):
    return (low(grad),)
low.defvjp(low_keep, low_pass)
low_back.defvjp(back_keep, back_low)
HIGHEST = lax.Precision.HIGHEST
EPSILON = 1e-05
THETA = 10000.0

def normalize(vector, gain_vector):
    return vector * lax.rsqrt(lax.optimization_barrier(jnp.mean(vector * vector, axis=-1, keepdims=True)) + EPSILON) * gain_vector

def rotary(positions):
    half_size = HEAD // 2
    frequency = jnp.exp(jnp.arange(half_size).astype(jnp.float32) * (-2.0 * math.log(THETA) / HEAD))
    angles = positions.astype(jnp.float32)[:, None] * frequency[None, :]
    return (jnp.cos(angles), jnp.sin(angles))

def rotate(vector, cosine_table, sine_table):
    half_size = vector.shape[-1] // 2
    first_half = vector[..., :half_size]
    second_half = vector[..., half_size:]
    cosine_part = cosine_table[:, None, :]
    sine_part = sine_table[:, None, :]
    return jnp.concatenate([first_half * cosine_part - second_half * sine_part, first_half * sine_part + second_half * cosine_part], axis=-1)

def documents(length_row, places):
    doc_ends = jnp.cumsum(length_row).astype(jnp.int32)
    doc_starts = doc_ends - length_row
    owner_ids = lax.optimization_barrier(jnp.sum((places[:, None] >= doc_ends[None, :]).astype(jnp.int32), axis=1))
    chosen = owner_ids[:, None] == jnp.arange(length_row.shape[0], dtype=jnp.int32)[None, :]
    first_place = lax.optimization_barrier(jnp.sum(jnp.where(chosen, doc_starts[None, :], 0), axis=1)).astype(jnp.int32)
    return (owner_ids, places - first_place)

def attend_group(queries, key_rows, value_rows, owner_ids, places):
    scale_factor = 1.0 / math.sqrt(HEAD)
    scores = jnp.einsum('qhd,khd->hqk', queries, key_rows, precision=HIGHEST) * scale_factor
    scores = low_back(scores)
    allowed = (owner_ids[:, None] == owner_ids[None, :]) & (places[None, :] <= places[:, None])
    scores = jnp.where(allowed[None, :, :], scores, -jnp.inf)
    weights = low(jax.nn.softmax(scores, axis=-1))
    return jnp.einsum('hqk,khd->qhd', weights, value_rows, precision=HIGHEST)

def reference(tokens, value_first, lengths, w_query, w_key, w_value, w_out, w_gate, w_up, w_down, gain_attn, gain_ffn, out_grad, value_grad):
    places = jnp.arange(GROUP, dtype=jnp.int32)
    owners, positions = jax.vmap(lambda length_row: documents(length_row, places))(lengths)
    cosine_table, sine_table = rotary(positions.reshape(TOKENS))

    def attend_pack(group_arrays):
        return attend_group(group_arrays[0], group_arrays[1], group_arrays[2], group_arrays[3], places)

    def layer(inputs, first_values, m_query, m_key, m_value, m_out, m_gate, m_up, m_down, m_gain_one, m_gain_two):
        m_query = low(m_query)
        m_key = low(m_key)
        m_value = low(m_value)
        m_out = low(m_out)
        m_gate = low(m_gate)
        m_up = low(m_up)
        m_down = low(m_down)
        m_gain_one = low(m_gain_one)
        m_gain_two = low(m_gain_two)
        hidden_one = low(normalize(inputs, m_gain_one))
        raw_query = low_back(jnp.dot(hidden_one, m_query, precision=HIGHEST))
        raw_key = low_back(jnp.dot(hidden_one, m_key, precision=HIGHEST))
        raw_value = low_back(jnp.dot(hidden_one, m_value, precision=HIGHEST))
        queries = low(rotate(raw_query.reshape(TOKENS, HEADS, HEAD), cosine_table, sine_table))
        key_rows = low(rotate(raw_key.reshape(TOKENS, HEADS, HEAD), cosine_table, sine_table))
        mixed = low(0.5 * raw_value + 0.5 * first_values).reshape(TOKENS, HEADS, HEAD)
        attended = lax.map(jax.checkpoint(attend_pack), (queries.reshape(N_FSDP, GROUP, HEADS, HEAD), key_rows.reshape(N_FSDP, GROUP, HEADS, HEAD), mixed.reshape(N_FSDP, GROUP, HEADS, HEAD), owners))
        attended = low_back(low(attended.reshape(TOKENS, D)))
        middle = inputs + low_back(jnp.dot(attended, m_out, precision=HIGHEST))
        hidden_two = low(normalize(middle, m_gain_two))
        gate_rows = low_back(jnp.dot(hidden_two, m_gate, precision=HIGHEST))
        up_rows = low_back(jnp.dot(hidden_two, m_up, precision=HIGHEST))
        activation = low_back(low(jax.nn.silu(gate_rows) * up_rows))
        return middle + jnp.dot(activation, m_down, precision=HIGHEST)
    floats = (tokens.astype(jnp.float32), value_first.astype(jnp.float32), w_query, w_key, w_value, w_out, w_gate, w_up, w_down, gain_attn, gain_ffn)
    output, pullback = jax.vjp(layer, *floats)
    gradients = pullback(out_grad.astype(jnp.float32))
    return (output.astype(jnp.bfloat16), gradients[0], value_grad + gradients[1], gradients[2], gradients[3], gradients[4], gradients[5], gradients[6], gradients[7], gradients[8], gradients[9], gradients[10])
```

```python
import functools
import math

import jax
import jax.numpy as jnp
from jax import lax
from jax.experimental import pallas as pl
from jax.experimental.pallas import tpu as pltpu
from jax.sharding import PartitionSpec as P

HEAD = 64
EPSILON = 1e-05
THETA = 10000.0
NEGATIVE = -1e30
BLOCK = 256
VMEM_LIMIT = 58 * 1024 * 1024
MESH = pl.DeviceIdType.MESH
BF16 = jnp.bfloat16
F32 = jnp.float32


def nn(left, right):
    return lax.dot_general(left, right, (((1,), (0,)), ((), ())), preferred_element_type=F32)


def nt(left, right):
    return lax.dot_general(left, right, (((1,), (1,)), ((), ())), preferred_element_type=F32)


def tn(left, right):
    return lax.dot_general(left, right, (((0,), (0,)), ((), ())), preferred_element_type=F32)


def widen(table, width):
    return jnp.concatenate([table] * (width // table.shape[1]), axis=1)


def half_swap(rows):
    width = rows.shape[1]
    lane = lax.broadcasted_iota(jnp.int32, rows.shape, 1)
    low = lax.rem(lane, HEAD) < HEAD // 2
    return jnp.where(
        low,
        pltpu.roll(rows, width - HEAD // 2, 1),
        pltpu.roll(rows, HEAD // 2, 1),
    )


def head_lanes(shape, head):
    lane = lax.broadcasted_iota(jnp.int32, shape, 1)
    return (lane >= head * HEAD) & (lane < (head + 1) * HEAD)


def forward_kernel(
    x, vf, wqkv, gain, cos_t, sin_t, start,
    h1, q, k, vm, kt, out, att, lse,
    vt, acc, mx, tot,
):
    group = x.shape[0]
    cols = vf.shape[1]
    heads = cols // HEAD
    blocks = group // BLOCK

    def project(b, carry):
        rows = pl.ds(pl.multiple_of(b * BLOCK, BLOCK), BLOCK)
        xv = x[rows, :].astype(F32)
        rstd = lax.rsqrt(jnp.mean(xv * xv, axis=1, keepdims=True) + EPSILON)
        hv = (xv * rstd * gain[...]).astype(BF16)
        h1[rows, :] = hv
        raw = nn(hv, wqkv[...])
        cos_v = widen(cos_t[rows, :], cols)
        sin_v = widen(sin_t[rows, :], cols)
        rq = raw[:, :cols]
        rk = raw[:, cols : 2 * cols]
        rv = raw[:, 2 * cols :]
        qv = (rq * cos_v + half_swap(rq) * sin_v).astype(BF16)
        q[rows, :] = (qv.astype(F32) * (1.0 / math.sqrt(HEAD))).astype(BF16)
        kv = (rk * cos_v + half_swap(rk) * sin_v).astype(BF16)
        k[rows, :] = kv
        kt[:, rows] = kv.T
        mixed = (0.5 * rv + 0.5 * vf[rows, :].astype(F32)).astype(BF16)
        vm[rows, :] = mixed
        vt[:, rows] = mixed.T
        return carry

    lax.fori_loop(0, blocks, project, 0)

    def queries(b, carry):
        rows = pl.ds(pl.multiple_of(b * BLOCK, BLOCK), BLOCK)
        acc[...] = jnp.zeros_like(acc)
        mx[...] = jnp.full_like(mx, NEGATIVE)
        tot[...] = jnp.zeros_like(tot)
        qv = q[rows, :]
        first = start[0:1, rows]

        def keys(kb, inner):
            krows = pl.ds(pl.multiple_of(kb * BLOCK, BLOCK), BLOCK)
            kv = k[krows, :]
            key_pos = kb * BLOCK + lax.broadcasted_iota(jnp.int32, (BLOCK, BLOCK), 0)
            query_pos = b * BLOCK + lax.broadcasted_iota(jnp.int32, (BLOCK, BLOCK), 1)
            allowed = (key_pos <= query_pos) & (key_pos >= first)
            for head in range(heads):
                band = slice(head * HEAD, (head + 1) * HEAD)
                qm = jnp.where(head_lanes(qv.shape, head), qv, jnp.zeros_like(qv))
                s = jnp.where(allowed, nt(kv, qm), NEGATIVE)
                old = mx[head : head + 1, :]
                new = jnp.maximum(old, jnp.max(s, axis=0, keepdims=True))
                p = jnp.exp(s - new)
                shrink = jnp.exp(old - new)
                mx[head : head + 1, :] = new
                tot[head : head + 1, :] = tot[head : head + 1, :] * shrink + jnp.sum(
                    p, axis=0, keepdims=True
                )
                acc[band, :] = acc[band, :] * shrink + nn(vt[band, krows], p.astype(BF16))
            return inner

        lax.fori_loop(0, b + 1, keys, 0)
        for head in range(heads):
            band = slice(head * HEAD, (head + 1) * HEAD)
            acc[band, :] = acc[band, :] / tot[head : head + 1, :]
        ov = acc[...].T
        att[rows, :] = ov
        out[rows, :] = ov.astype(BF16)
        lse[:, rows] = mx[...] + jnp.log(tot[...])
        return carry

    lax.fori_loop(0, blocks, queries, 0)


def forward_attention(x, vf, wqkv, gain, cos_t, sin_t, start):
    group, depth = x.shape
    cols = vf.shape[1]
    shapes = (
        jax.ShapeDtypeStruct((group, depth), BF16),
        jax.ShapeDtypeStruct((group, cols), BF16),
        jax.ShapeDtypeStruct((group, cols), BF16),
        jax.ShapeDtypeStruct((group, cols), BF16),
        jax.ShapeDtypeStruct((cols, group), BF16),
        jax.ShapeDtypeStruct((group, cols), BF16),
        jax.ShapeDtypeStruct((group, cols), F32),
        jax.ShapeDtypeStruct((8, group), F32),
    )
    vmem = pl.BlockSpec(memory_space=pltpu.VMEM)
    return pl.pallas_call(
        forward_kernel,
        out_shape=shapes,
        in_specs=[vmem] * 7,
        out_specs=[vmem] * 8,
        scratch_shapes=[
            pltpu.VMEM((cols, group), BF16),
            pltpu.VMEM((cols, BLOCK), F32),
            pltpu.VMEM((8, BLOCK), F32),
            pltpu.VMEM((8, BLOCK), F32),
        ],
        compiler_params=pltpu.CompilerParams(vmem_limit_bytes=VMEM_LIMIT),
        name="attention_forward",
    )(x, vf, wqkv, gain, cos_t, sin_t, start)


def backward_kernel(
    x, h1, q, k, vm, kt, att, lse, do, wqkv, gain, cos_t, sin_t, start,
    part, dvm, gw, dg,
    dqt, dkv, dvv, rows_t, d3,
):
    group, depth = x.shape
    cols = vm.shape[1]
    heads = cols // HEAD
    blocks = group // BLOCK
    dqt[...] = jnp.zeros_like(dqt)

    def dots(b, carry):
        rows = pl.ds(pl.multiple_of(b * BLOCK, BLOCK), BLOCK)
        prod = do[rows, :].astype(F32) * att[rows, :]
        high = prod.astype(BF16)
        low = (prod - high.astype(F32)).astype(BF16)
        head_row = lax.broadcasted_iota(jnp.int32, (8, cols), 0)
        lane = lax.broadcasted_iota(jnp.int32, (8, cols), 1)
        pick = (lane // HEAD == head_row).astype(F32).astype(BF16)
        rows_t[:, rows] = nt(pick, high) + nt(pick, low)
        return carry

    lax.fori_loop(0, blocks, dots, 0)

    def keys(kb, carry):
        krows = pl.ds(pl.multiple_of(kb * BLOCK, BLOCK), BLOCK)
        kv = k[krows, :]
        vv = vm[krows, :]
        dkv[...] = jnp.zeros_like(dkv)
        dvv[...] = jnp.zeros_like(dvv)

        def queries(b, inner):
            rows = pl.ds(pl.multiple_of(b * BLOCK, BLOCK), BLOCK)
            qv = q[rows, :]
            dov = do[rows, :]
            first = start[0:1, rows]
            key_pos = kb * BLOCK + lax.broadcasted_iota(jnp.int32, (BLOCK, BLOCK), 0)
            query_pos = b * BLOCK + lax.broadcasted_iota(jnp.int32, (BLOCK, BLOCK), 1)
            allowed = (key_pos <= query_pos) & (key_pos >= first)
            dk_sum = jnp.zeros((BLOCK, cols), F32)
            dv_sum = jnp.zeros((BLOCK, cols), F32)
            for head in range(heads):
                band = slice(head * HEAD, (head + 1) * HEAD)
                lanes = head_lanes(qv.shape, head)
                qm = jnp.where(lanes, qv, jnp.zeros_like(qv))
                dom = jnp.where(lanes, dov, jnp.zeros_like(dov))
                s = jnp.where(allowed, nt(kv, qm), NEGATIVE)
                p = jnp.exp(s - lse[head : head + 1, rows])
                ds = (p * (nt(vv, dom) - rows_t[head : head + 1, rows])).astype(BF16)
                dv_sum = dv_sum + nn(p.astype(BF16), dom)
                dk_sum = dk_sum + nn(ds, qm)
                dqt[band, rows] = dqt[band, rows] + nn(kt[band, krows], ds)
            dkv[...] = dkv[...] + dk_sum
            dvv[...] = dvv[...] + dv_sum
            return inner

        lax.fori_loop(kb, blocks, queries, 0)
        cos_v = widen(cos_t[krows, :], cols)
        sin_v = widen(sin_t[krows, :], cols)
        dk = dkv[...]
        d3[krows, cols : 2 * cols] = (dk * cos_v - half_swap(dk) * sin_v).astype(BF16)
        dv = dvv[...]
        dvm[krows, :] = dv.astype(BF16)
        d3[krows, 2 * cols :] = (0.5 * dv).astype(BF16)
        return carry

    lax.fori_loop(0, blocks, keys, 0)
    dg[...] = jnp.zeros_like(dg)

    def finish(b, carry):
        rows = pl.ds(pl.multiple_of(b * BLOCK, BLOCK), BLOCK)
        cos_v = widen(cos_t[rows, :], cols)
        sin_v = widen(sin_t[rows, :], cols)
        dq = dqt[:, rows].T * (1.0 / math.sqrt(HEAD))
        d3[rows, :cols] = (dq * cos_v - half_swap(dq) * sin_v).astype(BF16)
        dh = nt(d3[rows, :], wqkv[...])
        xv = x[rows, :].astype(F32)
        rstd = lax.rsqrt(jnp.mean(xv * xv, axis=1, keepdims=True) + EPSILON)
        xhat = xv * rstd
        u = dh * gain[...]
        part[rows, :] = (rstd * (u - xhat * jnp.mean(u * xhat, axis=1, keepdims=True))).astype(BF16)
        dg[0:1, :] = dg[0:1, :] + jnp.sum(dh * xhat, axis=0, keepdims=True)
        return carry

    lax.fori_loop(0, blocks, finish, 0)

    def weight(b, carry):
        at = pl.ds(pl.multiple_of(b * BLOCK, BLOCK), BLOCK)
        gw[at, :] = tn(h1[:, at], d3[...]).astype(BF16)
        return carry

    lax.fori_loop(0, depth // BLOCK, weight, 0)


def backward_attention(x, h1, q, k, vm, kt, att, lse, do, wqkv, gain, cos_t, sin_t, start):
    group, depth = x.shape
    cols = vm.shape[1]
    shapes = (
        jax.ShapeDtypeStruct((group, depth), BF16),
        jax.ShapeDtypeStruct((group, cols), BF16),
        jax.ShapeDtypeStruct((depth, 3 * cols), BF16),
        jax.ShapeDtypeStruct((8, depth), F32),
    )
    vmem = pl.BlockSpec(memory_space=pltpu.VMEM)
    return pl.pallas_call(
        backward_kernel,
        out_shape=shapes,
        in_specs=[vmem] * 14,
        out_specs=[vmem] * 4,
        scratch_shapes=[
            pltpu.VMEM((cols, group), F32),
            pltpu.VMEM((BLOCK, cols), F32),
            pltpu.VMEM((BLOCK, cols), F32),
            pltpu.VMEM((8, group), F32),
            pltpu.VMEM((group, 3 * cols), BF16),
        ],
        compiler_params=pltpu.CompilerParams(vmem_limit_bytes=VMEM_LIMIT),
        name="attention_backward",
    )(x, h1, q, k, vm, kt, att, lse, do, wqkv, gain, cos_t, sin_t, start)


def feed_kernel(
    o, x, dy, wo, gain, gu, wd,
    out, dx2, do, gwo, ggu, gwd, dg,
    x2, h2, h2t, total, dh2, act, dgu,
):
    step = pl.program_id(0)
    tokens, depth = x.shape
    chunk = wd.shape[0]
    blocks = tokens // BLOCK

    @pl.when(step == 0)
    def _():
        def rows_of(b, carry):
            rows = pl.ds(pl.multiple_of(b * BLOCK, BLOCK), BLOCK)
            mid = x[rows, :].astype(F32) + nn(o[rows, :], wo[...])
            x2[rows, :] = mid
            rstd = lax.rsqrt(jnp.mean(mid * mid, axis=1, keepdims=True) + EPSILON)
            hv = (mid * rstd * gain[...]).astype(BF16)
            h2[rows, :] = hv
            h2t[:, rows] = hv.T
            total[rows, :] = mid
            dh2[rows, :] = jnp.zeros((BLOCK, depth), F32)
            return carry

        lax.fori_loop(0, blocks, rows_of, 0)

    def rows_of(b, carry):
        rows = pl.ds(pl.multiple_of(b * BLOCK, BLOCK), BLOCK)
        both = nn(h2[rows, :], gu[0])
        gate = both[:, :chunk]
        up = both[:, chunk:]
        da = nt(dy[rows, :], wd[...]).astype(BF16).astype(F32)
        sig = 1.0 / (1.0 + jnp.exp(-gate))
        silu = gate * sig
        av = (silu * up).astype(BF16)
        act[rows, :] = av
        dgate = (da * up * (sig * (1.0 + gate * (1.0 - sig)))).astype(BF16)
        dup = (da * silu).astype(BF16)
        dv = jnp.concatenate([dgate, dup], axis=1)
        dgu[rows, :] = dv
        total[rows, :] = total[rows, :] + nn(av, wd[...])
        dh2[rows, :] = dh2[rows, :] + nt(dv, gu[0])
        return carry

    lax.fori_loop(0, blocks, rows_of, 0)

    gwd[...] = tn(act[...], dy[...]).astype(BF16)

    def weight(b, carry):
        rows = pl.ds(pl.multiple_of(b * BLOCK, BLOCK), BLOCK)
        ggu[0, rows, :] = nn(h2t[rows, :], dgu[...]).astype(BF16)
        return carry

    lax.fori_loop(0, depth // BLOCK, weight, 0)

    @pl.when(step == pl.num_programs(0) - 1)
    def _():
        dg[...] = jnp.zeros_like(dg)

        def rows_of(b, carry):
            rows = pl.ds(pl.multiple_of(b * BLOCK, BLOCK), BLOCK)
            out[rows, :] = total[rows, :].astype(BF16)
            mid = x2[rows, :]
            rstd = lax.rsqrt(jnp.mean(mid * mid, axis=1, keepdims=True) + EPSILON)
            xhat = mid * rstd
            dh = dh2[rows, :]
            u = dh * gain[...]
            dm = dy[rows, :].astype(F32) + rstd * (
                u - xhat * jnp.mean(u * xhat, axis=1, keepdims=True)
            )
            dx2[rows, :] = dm
            dg[0:1, :] = dg[0:1, :] + jnp.sum(dh * xhat, axis=0, keepdims=True)
            db = dm.astype(BF16)
            h2[rows, :] = db
            do[rows, :] = nt(db, wo[...]).astype(BF16)
            return carry

        lax.fori_loop(0, blocks, rows_of, 0)

        def weight_out(b, carry):
            at = pl.ds(pl.multiple_of(b * BLOCK, BLOCK), BLOCK)
            gwo[at, :] = tn(o[:, at], h2[...]).astype(BF16)
            return carry

        lax.fori_loop(0, depth // BLOCK, weight_out, 0)


def feed_forward(o, x, dy, wo, gain, gu, wd):
    tokens, depth = x.shape
    steps, _, width = gu.shape
    chunk = width // 2
    whole = lambda shape: pl.BlockSpec(shape, lambda i: (0,) * len(shape))
    shapes = (
        jax.ShapeDtypeStruct((tokens, depth), BF16),
        jax.ShapeDtypeStruct((tokens, depth), F32),
        jax.ShapeDtypeStruct((tokens, depth), BF16),
        jax.ShapeDtypeStruct((depth, depth), BF16),
        jax.ShapeDtypeStruct(gu.shape, BF16),
        jax.ShapeDtypeStruct(wd.shape, BF16),
        jax.ShapeDtypeStruct((8, depth), F32),
    )
    return pl.pallas_call(
        feed_kernel,
        grid=(steps,),
        out_shape=shapes,
        in_specs=[
            whole((tokens, depth)),
            whole((tokens, depth)),
            whole((tokens, depth)),
            whole((depth, depth)),
            whole((1, depth)),
            pl.BlockSpec((1, depth, width), lambda i: (i, 0, 0)),
            pl.BlockSpec((chunk, depth), lambda i: (i, 0)),
        ],
        out_specs=[
            whole((tokens, depth)),
            whole((tokens, depth)),
            whole((tokens, depth)),
            whole((depth, depth)),
            pl.BlockSpec((1, depth, width), lambda i: (i, 0, 0)),
            pl.BlockSpec((chunk, depth), lambda i: (i, 0)),
            whole((8, depth)),
        ],
        scratch_shapes=[
            pltpu.VMEM((tokens, depth), F32),
            pltpu.VMEM((tokens, depth), BF16),
            pltpu.VMEM((depth, tokens), BF16),
            pltpu.VMEM((tokens, depth), F32),
            pltpu.VMEM((tokens, depth), F32),
            pltpu.VMEM((tokens, chunk), BF16),
            pltpu.VMEM((tokens, width), BF16),
        ],
        compiler_params=pltpu.CompilerParams(
            vmem_limit_bytes=VMEM_LIMIT, dimension_semantics=("arbitrary",)
        ),
        name="feed_forward",
    )(o, x, dy, wo, gain, gu, wd)


class Plan:
    def __init__(self, fsdp, ctx):
        self.fsdp, self.ctx = fsdp, ctx
        self.lines = fsdp // 2
        self.across = math.isqrt(self.lines)
        self.along = self.lines // self.across
        self.half = ctx // 2
        self.f = lax.axis_index("fsdp")
        self.c = lax.axis_index("ctx")
        self.core = lax.rem(self.f, 2)
        self.line = self.f // 2
        self.a = self.line // self.along
        self.b = lax.rem(self.line, self.along)
        self.home = self.c // self.half
        self.started = []

    def barrier(self):
        sem = pltpu.get_barrier_semaphore()
        count = 0
        for step in range(1, self.fsdp):
            dev = (lax.rem(self.f + step, self.fsdp), self.c)
            pl.semaphore_signal(sem, inc=1, device_id=dev, device_id_type=MESH)
            count += 1
        for step in range(1, self.ctx):
            for core in range(2):
                dev = (self.line * 2 + core, lax.rem(self.c + step, self.ctx))
                pl.semaphore_signal(sem, inc=1, device_id=dev, device_id_type=MESH)
                count += 1
        pl.semaphore_wait(sem, count)

    def when(self, cond, act):
        if cond is True:
            act()
        else:
            pl.when(cond)(act)

    def send(self, src, dst, send_sem, recv_sem, dev, cond=True):
        def copy():
            return pltpu.make_async_remote_copy(
                src_ref=src, dst_ref=dst, send_sem=send_sem, recv_sem=recv_sem,
                device_id=dev, device_id_type=MESH,
            )

        self.when(cond, lambda: copy().start())
        self.started.append((cond, lambda: copy().wait_send()))

    def keep(self, src, dst, sem, cond=True):
        self.when(cond, lambda: pltpu.make_async_copy(src, dst, sem).start())

    def arrive(self, dst, sem, cond=True):
        self.when(cond, lambda: pltpu.make_async_copy(dst, dst, sem).wait())

    def drain(self):
        for cond, act in self.started:
            self.when(cond, act)
        self.started = []


def both(*conds):
    out = True
    for cond in conds:
        if cond is not True:
            out = cond if out is True else jnp.logical_and(out, cond)
    return out


def gather_kernel(
    fsdp, ctx,
    x, vf, wqkv, wo, gu, wd, gains,
    xs, vs, wq, wqh, wos, gus, wds, gs,
    x_sem, x_out, v_sem, v_out, q_sem, q_out, h_sem, g_sem, g_out, w_sem, w_z, w_p, w_s,
):
    plan = Plan(fsdp, ctx)
    f, c, core, line, home, half = plan.f, plan.c, plan.core, plan.line, plan.home, plan.half
    a, b, across, along, lines = plan.a, plan.b, plan.across, plan.along, plan.lines
    cols = vs.shape[2]
    owner = core == home
    sibling = (line * 2 + 1 - core, c)
    plan.barrier()

    def spread_x(j, below, above, cond):
        src, dst = xs.at[j], xs.at[j]
        if below:
            plan.send(src, dst, x_out.at[0, j], x_sem.at[j], (f, c - 1), both(cond, c > home * half))
        if above:
            plan.send(
                src, dst, x_out.at[1, j], x_sem.at[j], (f, c + 1),
                both(cond, c < home * half + half - 1),
            )
        plan.send(src, dst, x_out.at[2, j], x_sem.at[j], sibling, cond)

    away = jnp.logical_not(owner)
    entry = jnp.where(core == 0, half - 1, half)
    plan.send(x, xs.at[c], x_out.at[0, c], x_sem.at[c], (f, entry), away)
    plan.send(x, xs.at[c], x_out.at[0, c], x_sem.at[c], (f, c - 1), both(owner, c > home * half))
    plan.send(
        x, xs.at[c], x_out.at[1, c], x_sem.at[c], (f, c + 1),
        both(owner, c < home * half + half - 1),
    )
    plan.send(x, xs.at[c], x_out.at[2, c], x_sem.at[c], sibling, owner)
    plan.keep(x, xs.at[c], x_sem.at[c], owner)

    across_ctx = lax.rem(c + half, ctx)
    plan.send(wqkv, wqh, h_sem.at[0], h_sem.at[1], (f, across_ctx))

    def items(row, j):
        return (
            wos.at[row, :, pl.ds(pl.multiple_of(j * wo.shape[1], wo.shape[1]), wo.shape[1])],
            gus.at[j, row],
            wds.at[row, :, pl.ds(pl.multiple_of(j * wd.shape[1], wd.shape[1]), wd.shape[1])],
        )

    def spread_w(srcs, j, cond, up, down):
        dsts = items(f, j)
        for i in range(3):
            if up:
                plan.send(
                    srcs[i], dsts[i], w_z.at[i, 0, j], w_sem.at[i, f, j], (f, c + 1),
                    both(cond, c < ctx - 1),
                )
            if down:
                plan.send(
                    srcs[i], dsts[i], w_z.at[i, 1, j], w_sem.at[i, f, j], (f, c - 1),
                    both(cond, c > 0),
                )
        for i in range(3):
            for step in range(1, across):
                dev = ((lax.rem(a + step, across) * along + b) * 2 + core, c)
                plan.send(
                    srcs[i], dsts[i], w_p.at[i, step - 1, line, j], w_sem.at[i, f, j], dev, cond
                )
            for step in range(1, along):
                dev = ((a * along + lax.rem(b + step, along)) * 2 + core, c)
                plan.send(
                    srcs[i], dsts[i], w_p.at[i, across + step - 2, line, j], w_sem.at[i, f, j],
                    dev, cond,
                )
            plan.send(srcs[i], dsts[i], w_s.at[i, line, j], w_sem.at[i, f, j], sibling, cond)

    for step in range(1, fsdp):
        dev = (lax.rem(f + step, fsdp), c)
        plan.send(gains, gs.at[f], g_out.at[step - 1], g_sem.at[f], dev)
    plan.keep(gains, gs.at[f], g_sem.at[f])

    own = (wo, gu, wd)
    spread_w(own, c, True, True, True)
    for src, dst, i in zip(own, items(f, c), range(3)):
        plan.keep(src, dst, w_sem.at[i, f, c])

    for at in range(lines):
        dev = (at * 2, c)
        plan.send(wqkv, wq.at[f], q_out.at[0, at], q_sem.at[f], dev, jnp.logical_not(f == at * 2))
    plan.keep(wqkv, wq.at[f], q_sem.at[f], core == 0)

    for i in range(half):
        for k in range(2):
            to = core * half + i
            rank = lax.rem(to + k * half, ctx)
            src = vf.at[:, pl.ds(pl.multiple_of(rank * cols, cols), cols)]
            mine = both(owner, c == to, core == k)
            plan.send(
                src, vs.at[c], v_out.at[i, k], v_sem.at[c], (line * 2 + k, to),
                jnp.logical_not(mine),
            )
            plan.keep(src, vs.at[c], v_sem.at[c], mine)

    pltpu.make_async_copy(wqh, wqh, h_sem.at[1]).wait()
    for at in range(lines):
        dev = (at * 2 + 1, c)
        plan.send(
            wqh, wq.at[f], q_out.at[1, at], q_sem.at[f], dev, jnp.logical_not(f == at * 2 + 1)
        )
    plan.keep(wqh, wq.at[f], q_sem.at[f], core == 1)

    for dist in range(1, ctx):
        for side in range(2):
            j = c - dist if side == 0 else c + dist
            there = j >= 0 if side == 0 else j < ctx
            at = jnp.clip(j, 0, ctx - 1)
            cond = both(owner, there)
            plan.arrive(xs.at[at], x_sem.at[at], cond)
            spread_x(at, side == 1, side == 0, cond)
        for side in range(2):
            j = c - dist if side == 0 else c + dist
            there = j >= 0 if side == 0 else j < ctx
            at = jnp.clip(j, 0, ctx - 1)
            dsts = items(f, at)
            for i in range(3):
                plan.arrive(dsts[i], w_sem.at[i, f, at], there)
            spread_w(dsts, at, there, side == 0, side == 1)

    for dist in range(ctx):
        for side in range(2 if dist else 1):
            j = c - dist if side == 0 else c + dist
            there = j >= 0 if side == 0 else j < ctx
            at = jnp.clip(j, 0, ctx - 1)
            first = at < half
            for step in range(1, across):
                from_line = lax.rem(a + across - step, across) * along + b
                row = from_line * 2 + core
                dsts = items(row, at)
                for i in range(3):
                    plan.arrive(dsts[i], w_sem.at[i, row, at], there)
                for i in range(3):
                    for hop in range(1, along):
                        dev = ((a * along + lax.rem(b + hop, along)) * 2 + core, c)
                        plan.send(
                            dsts[i], dsts[i], w_p.at[i, across + hop - 2, from_line, at],
                            w_sem.at[i, row, at], dev, both(there, first),
                        )
                    plan.send(
                        dsts[i], dsts[i], w_s.at[i, from_line, at], w_sem.at[i, row, at], sibling,
                        there,
                    )
            for step in range(1, along):
                from_line = a * along + lax.rem(b + along - step, along)
                row = from_line * 2 + core
                dsts = items(row, at)
                for i in range(3):
                    plan.arrive(dsts[i], w_sem.at[i, row, at], there)
                for i in range(3):
                    for hop in range(1, across):
                        dev = ((lax.rem(a + hop, across) * along + b) * 2 + core, c)
                        plan.send(
                            dsts[i], dsts[i], w_p.at[i, hop - 1, from_line, at],
                            w_sem.at[i, row, at], dev, both(there, jnp.logical_not(first)),
                        )
                    plan.send(
                        dsts[i], dsts[i], w_s.at[i, from_line, at], w_sem.at[i, row, at], sibling,
                        there,
                    )
    for dist in range(ctx):
        for side in range(2 if dist else 1):
            j = c - dist if side == 0 else c + dist
            there = j >= 0 if side == 0 else j < ctx
            at = jnp.clip(j, 0, ctx - 1)
            for step in range(1, across):
                for hop in range(1, along):
                    from_line = lax.rem(a + step, across) * along + lax.rem(b + hop, along)
                    row = from_line * 2 + core
                    dsts = items(row, at)
                    for i in range(3):
                        plan.arrive(dsts[i], w_sem.at[i, row, at], there)
                        plan.send(
                            dsts[i], dsts[i], w_s.at[i, from_line, at], w_sem.at[i, row, at],
                            sibling, there,
                        )

    for i in range(3):
        plan.arrive(items(f, c)[i], w_sem.at[i, f, c])

    def far(at, carry):
        row = at * 2 + 1 - core
        for j in range(ctx):
            dsts = items(row, j)
            for i in range(3):
                plan.arrive(dsts[i], w_sem.at[i, row, j])
        return carry

    lax.fori_loop(0, lines, far, 0)
    for j in range(ctx):
        plan.arrive(xs.at[j], x_sem.at[j], both(jnp.logical_or(away, c == j)))
        plan.arrive(vs.at[j], v_sem.at[j])
    for row in range(fsdp):
        plan.arrive(wq.at[row], q_sem.at[row])
        plan.arrive(gs.at[row], g_sem.at[row])
    plan.drain()


def gather(mesh, x, vf, wqkv, wo, gu, wd, gains):
    fsdp, ctx = mesh.shape["fsdp"], mesh.shape["ctx"]
    tokens, depth = x.shape
    cols = depth // ctx
    lines = fsdp // 2
    across = math.isqrt(lines)
    peers = max(across - 1 + lines // across - 1, 1)
    anywhere = pl.BlockSpec(memory_space=pl.ANY)
    dma = pltpu.SemaphoreType.DMA
    return pl.pallas_call(
        functools.partial(gather_kernel, fsdp, ctx),
        out_shape=(
            jax.ShapeDtypeStruct((ctx, tokens, depth), BF16),
            jax.ShapeDtypeStruct((ctx, tokens, cols), BF16),
            jax.ShapeDtypeStruct((fsdp,) + wqkv.shape, BF16),
            jax.ShapeDtypeStruct(wqkv.shape, BF16),
            jax.ShapeDtypeStruct((fsdp, wo.shape[0], depth), BF16),
            jax.ShapeDtypeStruct((ctx, fsdp) + gu.shape, BF16),
            jax.ShapeDtypeStruct((fsdp, wd.shape[0], depth), BF16),
            jax.ShapeDtypeStruct((fsdp,) + gains.shape, F32),
        ),
        in_specs=[anywhere] * 7,
        out_specs=[anywhere] * 8,
        scratch_shapes=[
            dma((ctx,)), dma((3, ctx)), dma((ctx,)), dma((ctx // 2, 2)),
            dma((fsdp,)), dma((2, lines)), dma((2,)), dma((fsdp,)), dma((fsdp,)),
            dma((3, fsdp, ctx)), dma((3, 2, ctx)), dma((3, peers, lines, ctx)), dma((3, lines, ctx)),
        ],
        compiler_params=pltpu.CompilerParams(collective_id=0, has_side_effects=True),
        name="gather_all",
    )(x, vf, wqkv, wo, gu, wd, gains)


def trade_kernel(fsdp, ctx, inward, src_ref, dst_ref, recv, sent):
    plan = Plan(fsdp, ctx)
    f, c, core, line, home, half = plan.f, plan.c, plan.core, plan.line, plan.home, plan.half
    cols = (src_ref if inward else dst_ref).shape[2]
    plan.barrier()

    def band(rank):
        return pl.ds(pl.multiple_of(rank * cols, cols), cols)

    if inward:
        rank = lax.rem(c + core * half, ctx)
        for step in range(ctx):
            j = lax.rem(c + step, ctx)
            src, dst = src_ref.at[j], dst_ref.at[:, band(rank)]
            dev = (line * 2 + home, j)
            mine = both(core == home) if step == 0 else False
            if step == 0:
                plan.keep(src, dst, recv.at[rank], mine)
                plan.send(src, dst, sent.at[j], recv.at[rank], dev, jnp.logical_not(mine))
            else:
                plan.send(src, dst, sent.at[j], recv.at[rank], dev)
        for rank in range(ctx):
            plan.arrive(dst_ref.at[:, band(rank)], recv.at[rank])
    else:
        for i in range(half):
            for k in range(2):
                to = core * half + i
                src = src_ref.at[:, band(lax.rem(to + k * half, ctx))]
                mine = both(core == home, c == to, core == k)
                plan.send(
                    src, dst_ref.at[c], sent.at[i * 2 + k], recv.at[c], (line * 2 + k, to),
                    jnp.logical_not(mine),
                )
                plan.keep(src, dst_ref.at[c], recv.at[c], mine)
        for j in range(ctx):
            plan.arrive(dst_ref.at[j], recv.at[j])
    plan.drain()


def trade(mesh, array, inward, ident):
    fsdp, ctx = mesh.shape["fsdp"], mesh.shape["ctx"]
    if inward:
        shape = (array.shape[1], array.shape[2] * ctx)
    else:
        shape = (ctx, array.shape[0], array.shape[1] // ctx)
    anywhere = pl.BlockSpec(memory_space=pl.ANY)
    return pl.pallas_call(
        functools.partial(trade_kernel, fsdp, ctx, inward),
        out_shape=jax.ShapeDtypeStruct(shape, BF16),
        in_specs=[anywhere],
        out_specs=anywhere,
        scratch_shapes=[pltpu.SemaphoreType.DMA((ctx,)), pltpu.SemaphoreType.DMA((ctx,))],
        compiler_params=pltpu.CompilerParams(collective_id=ident, has_side_effects=True),
        name="trade_in" if inward else "trade_out",
    )(array)


def fold_kernel(
    fsdp, ctx,
    part, dvm, out, vout,
    other, chain, summed,
    recv, sent, line_recv, line_sent, last, last_sent, v_recv, v_sent,
):
    plan = Plan(fsdp, ctx)
    f, c, core, line, home, half = plan.f, plan.c, plan.core, plan.line, plan.home, plan.half
    sibling = (line * 2 + 1 - core, c)
    low, high = home * half, home * half + half - 1
    plan.barrier()
    pairs = [jnp.where(home == 0, ctx - 2 - 2 * i, 2 * i) for i in range(half)]
    for i, base in enumerate(pairs):
        give = base + 1 - core
        plan.send(part.at[give], other.at[i], sent.at[i], recv.at[i], sibling)
    cols = dvm.shape[2]
    rank = lax.rem(c + core * half, ctx)
    for step in range(ctx):
        j = lax.rem(c + step, ctx)
        src = dvm.at[j]
        dst = vout.at[:, pl.ds(pl.multiple_of(rank * cols, cols), cols)]
        mine = core == home
        if step == 0:
            plan.keep(src, dst, v_recv.at[rank], mine)
        plan.send(
            src, dst, v_sent.at[step], v_recv.at[rank], (line * 2 + home, j),
            jnp.logical_not(mine) if step == 0 else True,
        )
    for i, base in enumerate(pairs):
        j = base + core
        plan.arrive(other.at[i], recv.at[i])
        def add(src, slot, i=i, j=j):
            def body(t, carry):
                at = pl.ds(pl.multiple_of(t * 128, 128), 128)
                summed[i, at, :] = (
                    part[j, at, :].astype(F32) + src[slot, at, :].astype(F32)
                ).astype(BF16)
                return carry

            lax.fori_loop(0, part.shape[1] // 128, body, 0)

        def more(slot, i=i):
            def body(t, carry):
                at = pl.ds(pl.multiple_of(t * 128, 128), 128)
                summed[i, at, :] = (
                    summed[i, at, :].astype(F32) + chain[slot, i, at, :].astype(F32)
                ).astype(BF16)
                return carry

            lax.fori_loop(0, part.shape[1] // 128, body, 0)

        add(other, i)
        top = jnp.minimum(j, high)
        bottom = jnp.maximum(j, low)
        from_below = both(c > low, c <= top)
        from_above = both(c < high, c >= bottom)

        @pl.when(from_below)
        def _(i=i):
            plan.arrive(chain.at[0, i], line_recv.at[0, i])
            more(0)

        @pl.when(from_above)
        def _(i=i):
            plan.arrive(chain.at[1, i], line_recv.at[1, i])
            more(1)

        plan.send(summed.at[i], chain.at[0, i], line_sent.at[0, i], line_recv.at[0, i], (f, c + 1), c < top)
        plan.send(summed.at[i], chain.at[1, i], line_sent.at[1, i], line_recv.at[1, i], (f, c - 1), c > bottom)
        end = jnp.clip(j, low, high)
        mine = both(c == end, j == c, core == home)
        plan.send(
            summed.at[i], out, last_sent.at[i], last.at[0], (line * 2 + home, j),
            both(c == end, jnp.logical_not(mine)),
        )
        plan.keep(summed.at[i], out, last.at[0], mine)
    plan.arrive(out, last.at[0])
    for at in range(ctx):
        plan.arrive(vout.at[:, pl.ds(at * cols, cols)], v_recv.at[at])
    plan.drain()


def fold(mesh, part, dvm, ident):
    fsdp, ctx = mesh.shape["fsdp"], mesh.shape["ctx"]
    _, tokens, depth = part.shape
    half = ctx // 2
    dma = pltpu.SemaphoreType.DMA
    return pl.pallas_call(
        functools.partial(fold_kernel, fsdp, ctx),
        out_shape=(
            jax.ShapeDtypeStruct((tokens, depth), BF16),
            jax.ShapeDtypeStruct((tokens, depth), BF16),
        ),
        in_specs=[
            pl.BlockSpec(memory_space=pltpu.VMEM),
            pl.BlockSpec(memory_space=pl.ANY),
        ],
        out_specs=(
            pl.BlockSpec(memory_space=pltpu.VMEM),
            pl.BlockSpec(memory_space=pl.ANY),
        ),
        scratch_shapes=[
            pltpu.VMEM((half, tokens, depth), BF16),
            pltpu.VMEM((2, half, tokens, depth), BF16),
            pltpu.VMEM((half, tokens, depth), BF16),
            dma((half,)), dma((half,)), dma((2, half)), dma((2, half)), dma((1,)), dma((half,)),
            dma((ctx,)), dma((ctx,)),
        ],
        compiler_params=pltpu.CompilerParams(
            collective_id=ident, has_side_effects=True, vmem_limit_bytes=VMEM_LIMIT
        ),
        name="fold_tokens",
    )(part, dvm)


def documents(length_row, places):
    doc_ends = jnp.cumsum(length_row)
    doc_starts = doc_ends - length_row
    owner_ids = jnp.sum((places[:, None] >= doc_ends[None, :]).astype(jnp.int32), axis=1)
    chosen = owner_ids[:, None] == jnp.arange(length_row.shape[0], dtype=jnp.int32)[None, :]
    first_place = jnp.sum(jnp.where(chosen, doc_starts[None, :], 0), axis=1)
    return first_place


def tables(length_row, group):
    places = jnp.arange(group, dtype=jnp.int32)
    first = documents(length_row, places)
    half = HEAD // 2
    frequency = jnp.exp(jnp.arange(half).astype(F32) * (-2.0 * math.log(THETA) / HEAD))
    angles = (places - first).astype(F32)[:, None] * frequency[None, :]
    cos, sin = jnp.cos(angles), jnp.sin(angles)
    return (
        jnp.concatenate([cos] * 4, axis=1),
        jnp.concatenate([-sin, sin] * 2, axis=1),
        first[None, :],
    )


def pick(array, index, axis):
    return lax.dynamic_index_in_dim(array, index, axis, keepdims=False)


def add_low(*parts):
    total = parts[0].astype(F32)
    for part in parts[1:]:
        total = total + part.astype(F32)
    return total


def sum_over(array, axis_name, axis, position, size, perm):
    parts = [pick(array, position, axis)]
    for hop in range(1, size):
        out = pick(array, lax.rem(position + hop, size), axis)
        parts.append(lax.ppermute(out, axis_name, perm(hop)))
    return add_low(*parts)


def reduce_shards(mesh, grads):
    fsdp, ctx = mesh.shape["fsdp"], mesh.shape["ctx"]
    lines = fsdp // 2
    across = math.isqrt(lines)
    along = lines // across
    f, c = lax.axis_index("fsdp"), lax.axis_index("ctx")
    core, line = lax.rem(f, 2), f // 2
    a, b = line // along, lax.rem(line, along)

    def number(aa, bb, kk):
        return (aa * along + bb) * 2 + kk

    def over_core(hop):
        return [(i, i ^ 1) for i in range(fsdp)]

    def over_along(hop):
        return [
            (number(aa, bb, kk), number(aa, (bb + hop) % along, kk))
            for aa in range(across) for bb in range(along) for kk in range(2)
        ]

    def over_across(hop):
        return [
            (number(aa, bb, kk), number((aa + hop) % across, bb, kk))
            for aa in range(across) for bb in range(along) for kk in range(2)
        ]

    def over_ctx(hop):
        return [(i, (i + hop) % ctx) for i in range(ctx)]

    out = []
    for grad in grads:
        near = sum_over(grad, "fsdp", 2, core, 2, over_core).astype(BF16)
        half = ctx // 2
        low = sum_over(near[:, :, :half], "fsdp", 1, b, along, over_along).astype(BF16)
        low = sum_over(low, "fsdp", 0, a, across, over_across).astype(BF16)
        high = sum_over(near[:, :, half:], "fsdp", 0, a, across, over_across).astype(BF16)
        high = sum_over(high, "fsdp", 0, b, along, over_along).astype(BF16)
        out.append(
            sum_over(jnp.concatenate([low, high], axis=0), "ctx", 0, c, ctx, over_ctx)
        )
    return out


def reduce_heads(mesh, grad):
    fsdp, ctx = mesh.shape["fsdp"], mesh.shape["ctx"]
    lines = fsdp // 2
    f, c = lax.axis_index("fsdp"), lax.axis_index("ctx")
    core, line = lax.rem(f, 2), f // 2

    def over_lines(hop):
        return [
            (at * 2 + k, ((at + hop) % lines) * 2 + k) for at in range(lines) for k in range(2)
        ]

    summed = sum_over(grad, "fsdp", 0, line, lines, over_lines).astype(BF16)
    half = ctx // 2
    pairs = []
    for at in range(lines):
        for z in range(ctx):
            far = (z + half) % ctx
            pairs.append(((at * 2) * ctx + z, (at * 2 + 1) * ctx + z))
            pairs.append(((at * 2 + 1) * ctx + z, (at * 2) * ctx + far))
    other = lax.ppermute(pick(summed, 1 - core, 0), ("fsdp", "ctx"), pairs)
    mine = pick(summed, core, 0)
    return other, mine, half


def reduce_heads_final(mesh, grad):
    fsdp, ctx = mesh.shape["fsdp"], mesh.shape["ctx"]
    lines, half = fsdp // 2, ctx // 2
    other, mine, _ = reduce_heads(mesh, grad)
    core = lax.rem(lax.axis_index("fsdp"), 2)
    pairs = [((at * 2 + 1) * ctx + z, (at * 2 + 1) * ctx + (z + half) % ctx)
             for at in range(lines) for z in range(ctx)]
    moved = lax.ppermute(mine, ("fsdp", "ctx"), pairs)
    return other.astype(F32) + jnp.where(core == 0, mine, moved).astype(F32)


def layer(
    mesh, tokens, value_first, lengths, w_query, w_key, w_value, w_out, w_gate, w_up, w_down,
    gain_attn, gain_ffn, out_grad, value_grad,
):
    fsdp, ctx = mesh.shape["fsdp"], mesh.shape["ctx"]
    lines = fsdp // 2
    across = math.isqrt(lines)
    along = lines // across
    count, depth = tokens.shape
    group = count * ctx
    cols = depth // ctx
    rows = depth // fsdp
    f, c = lax.axis_index("fsdp"), lax.axis_index("ctx")
    core = lax.rem(f, 2)
    home = c // (ctx // 2)

    wqkv = jnp.concatenate([w_query, w_key, w_value], axis=1).astype(BF16)
    gu = jnp.concatenate([w_gate, w_up], axis=1).astype(BF16)
    gains = jnp.stack([gain_attn, gain_ffn]).astype(BF16).astype(F32)
    gains = lax.dynamic_update_slice(
        jnp.zeros((8, depth), F32), gains, (jnp.int32(0), (f * rows).astype(jnp.int32))
    )
    other_lengths = lax.ppermute(lengths, "fsdp", [(i, i ^ 1) for i in range(fsdp)])
    length_row = jnp.where(core == home, lengths, other_lengths)[0]
    cos_t, sin_t, first = tables(length_row, group)

    xs, vs, wq, _, wos, gus, wds, gs = gather(
        mesh, tokens, value_first, wqkv, w_out.astype(BF16), gu, w_down.astype(BF16), gains
    )
    gain_full = jnp.sum(gs, axis=0)
    gain_one, gain_two = gain_full[0:1], gain_full[1:2]
    xg = xs.reshape(group, depth)
    wq = wq.reshape(depth, 3 * cols)
    h1, q, k, vm, kt, out, att, lse = forward_attention(
        xg, vs.reshape(group, cols), wq, gain_one, cos_t, sin_t, first
    )
    attended = trade(mesh, out.reshape(ctx, count, cols), True, 1)
    result, dx2, d_out, g_wo, g_gu, g_wd, dg_two = feed_forward(
        attended, tokens, out_grad, wos.reshape(depth, depth), gain_two,
        gus.reshape(ctx, depth, gu.shape[1]), wds.reshape(-1, depth),
    )
    do = trade(mesh, d_out, False, 2).reshape(group, cols)
    part, dvm, g_qkv, dg_one = backward_attention(
        xg, h1, q, k, vm, kt, att, lse, do, wq, gain_one, cos_t, sin_t, first
    )
    folded, dvm_own = fold(
        mesh, part.reshape(ctx, count, depth), dvm.reshape(ctx, count, cols), 3
    )
    ff = w_gate.shape[1]
    rows_d = w_down.shape[0]
    g_wo, g_gu, g_wd = reduce_shards(
        mesh,
        (
            g_wo.reshape(across, along, 2, rows, ctx, cols).transpose(0, 1, 2, 4, 3, 5),
            g_gu.reshape(ctx, across, along, 2, rows, 2 * ff).transpose(1, 2, 3, 0, 4, 5),
            g_wd.reshape(across, along, 2, rows_d, ctx, cols).transpose(0, 1, 2, 4, 3, 5),
        ),
    )
    g_qkv = reduce_heads_final(mesh, g_qkv.reshape(lines, 2, rows, 3 * cols))
    gain_grads = jnp.stack([dg_one[0], dg_two[0]])
    gain_grads = lax.psum(
        lax.psum_scatter(gain_grads, "fsdp", scatter_dimension=1, tiled=True), "ctx"
    )
    return (
        result,
        dx2 + folded.astype(F32),
        value_grad + 0.5 * dvm_own.astype(F32),
        g_qkv[:, :cols],
        g_qkv[:, cols : 2 * cols],
        g_qkv[:, 2 * cols :],
        g_wo,
        g_gu[:, :ff],
        g_gu[:, ff:],
        g_wd,
        gain_grads[0],
        gain_grads[1],
    )


def solution(mesh):
    rows = P(("fsdp", "ctx"), None)
    shard = P("fsdp", "ctx")
    return jax.shard_map(
        functools.partial(layer, mesh),
        mesh=mesh,
        in_specs=(rows, rows, P("fsdp", None)) + (shard,) * 7 + (P("fsdp"),) * 2 + (rows, rows),
        out_specs=(rows, rows, rows) + (shard,) * 7 + (P("fsdp"),) * 2,
        check_vma=False,
    )
```

```python
import functools
import math

import jax
import jax.numpy as jnp
from jax import lax
from jax.experimental import pallas as pl
from jax.experimental.pallas import tpu as pltpu
from jax.sharding import PartitionSpec as P

HEAD = 64
EPSILON = 1e-05
THETA = 10000.0
NEGATIVE = -1e30
BLOCK = 256
VMEM_LIMIT = 58 * 1024 * 1024
BACKWARD_LIMIT = 58 * 1024 * 1024
MESH = pl.DeviceIdType.MESH
BF16 = jnp.bfloat16
F32 = jnp.float32


def nn(left, right):
    return lax.dot_general(left, right, (((1,), (0,)), ((), ())), preferred_element_type=F32)


def nt(left, right):
    return lax.dot_general(left, right, (((1,), (1,)), ((), ())), preferred_element_type=F32)


def tn(left, right):
    return lax.dot_general(left, right, (((0,), (0,)), ((), ())), preferred_element_type=F32)


def turns(table, width):
    lane = lax.broadcasted_iota(jnp.int32, table.shape, 1)
    swapped = pltpu.roll(table, HEAD, 1)
    cos = jnp.where(lane < HEAD, table, swapped)
    sin = jnp.where(lane < HEAD, swapped, table)
    times = width // table.shape[1]
    return jnp.concatenate([cos] * times, axis=1), jnp.concatenate([sin] * times, axis=1)


def half_swap(rows):
    width = rows.shape[1]
    lane = lax.broadcasted_iota(jnp.int32, rows.shape, 1)
    low = lax.rem(lane, HEAD) < HEAD // 2
    return jnp.where(
        low,
        pltpu.roll(rows, width - HEAD // 2, 1),
        pltpu.roll(rows, HEAD // 2, 1),
    )


def head_lanes(shape, head):
    lane = lax.broadcasted_iota(jnp.int32, shape, 1)
    return (lane >= head * HEAD) & (lane < (head + 1) * HEAD)


def forward_kernel(
    x, vf, wqkv, gain, table, start,
    h1, q, k, vm, kt, out, att, lse,
    vt, acc, mx, tot,
):
    group = x.shape[0]
    cols = vf.shape[1]
    heads = cols // HEAD
    blocks = group // BLOCK

    def project(b, carry):
        rows = pl.ds(pl.multiple_of(b * BLOCK, BLOCK), BLOCK)
        xv = x[rows, :].astype(F32)
        rstd = lax.rsqrt(jnp.mean(xv * xv, axis=1, keepdims=True) + EPSILON)
        hv = (xv * rstd * gain[...]).astype(BF16)
        h1[rows, :] = hv
        raw = nn(hv, wqkv[...])
        cos_v, sin_v = turns(table[rows, :], cols)
        rq = raw[:, :cols]
        rk = raw[:, cols : 2 * cols]
        rv = raw[:, 2 * cols :]
        qv = (rq * cos_v + half_swap(rq) * sin_v).astype(BF16)
        q[rows, :] = (qv.astype(F32) * (1.0 / math.sqrt(HEAD))).astype(BF16)
        kv = (rk * cos_v + half_swap(rk) * sin_v).astype(BF16)
        k[rows, :] = kv
        kt[:, rows] = kv.T
        mixed = (0.5 * rv + 0.5 * vf[rows, :].astype(F32)).astype(BF16)
        vm[rows, :] = mixed
        vt[:, rows] = mixed.T
        return carry

    lax.fori_loop(0, blocks, project, 0)

    def queries(b, carry):
        rows = pl.ds(pl.multiple_of(b * BLOCK, BLOCK), BLOCK)
        acc[...] = jnp.zeros_like(acc)
        mx[...] = jnp.full_like(mx, NEGATIVE)
        tot[...] = jnp.zeros_like(tot)
        qv = q[rows, :]
        first = start[0:1, rows]

        def keys(kb, inner):
            krows = pl.ds(pl.multiple_of(kb * BLOCK, BLOCK), BLOCK)
            kv = k[krows, :]
            key_pos = kb * BLOCK + lax.broadcasted_iota(jnp.int32, (BLOCK, BLOCK), 0)
            query_pos = b * BLOCK + lax.broadcasted_iota(jnp.int32, (BLOCK, BLOCK), 1)
            allowed = (key_pos <= query_pos) & (key_pos >= first)
            for head in range(heads):
                band = slice(head * HEAD, (head + 1) * HEAD)
                qm = jnp.where(head_lanes(qv.shape, head), qv, jnp.zeros_like(qv))
                s = jnp.where(allowed, nt(kv, qm), NEGATIVE)
                old = mx[head : head + 1, :]
                new = jnp.maximum(old, jnp.max(s, axis=0, keepdims=True))
                p = jnp.exp(s - new)
                shrink = jnp.exp(old - new)
                mx[head : head + 1, :] = new
                tot[head : head + 1, :] = tot[head : head + 1, :] * shrink + jnp.sum(
                    p, axis=0, keepdims=True
                )
                acc[band, :] = acc[band, :] * shrink + nn(vt[band, krows], p.astype(BF16))
            return inner

        lax.fori_loop(0, b + 1, keys, 0)
        for head in range(heads):
            band = slice(head * HEAD, (head + 1) * HEAD)
            acc[band, :] = acc[band, :] / tot[head : head + 1, :]
        ov = acc[...].T
        att[rows, :] = ov
        out[rows, :] = ov.astype(BF16)
        lse[:, rows] = mx[...] + jnp.log(tot[...])
        return carry

    lax.fori_loop(0, blocks, queries, 0)


def forward_attention(x, vf, wqkv, gain, table, start):
    group, depth = x.shape
    cols = vf.shape[1]
    shapes = (
        jax.ShapeDtypeStruct((group, depth), BF16),
        jax.ShapeDtypeStruct((group, cols), BF16),
        jax.ShapeDtypeStruct((group, cols), BF16),
        jax.ShapeDtypeStruct((group, cols), BF16),
        jax.ShapeDtypeStruct((cols, group), BF16),
        jax.ShapeDtypeStruct((group, cols), BF16),
        jax.ShapeDtypeStruct((group, cols), F32),
        jax.ShapeDtypeStruct((8, group), F32),
    )
    vmem = pl.BlockSpec(memory_space=pltpu.VMEM)
    return pl.pallas_call(
        forward_kernel,
        out_shape=shapes,
        in_specs=[vmem] * 6,
        out_specs=[vmem] * 8,
        scratch_shapes=[
            pltpu.VMEM((cols, group), BF16),
            pltpu.VMEM((cols, BLOCK), F32),
            pltpu.VMEM((8, BLOCK), F32),
            pltpu.VMEM((8, BLOCK), F32),
        ],
        compiler_params=pltpu.CompilerParams(vmem_limit_bytes=VMEM_LIMIT),
        name="attention_forward",
    )(x, vf, wqkv, gain, table, start)


class Plan:
    def __init__(self, fsdp, ctx):
        self.fsdp, self.ctx = fsdp, ctx
        self.lines = fsdp // 2
        self.across = math.isqrt(self.lines)
        self.along = self.lines // self.across
        self.half = ctx // 2
        self.f = lax.axis_index("fsdp")
        self.c = lax.axis_index("ctx")
        self.core = lax.rem(self.f, 2)
        self.line = self.f // 2
        self.a = self.line // self.along
        self.b = lax.rem(self.line, self.along)
        self.home = self.c // self.half
        self.started = []
        self.draining = False

    def barrier(self):
        sem = pltpu.get_barrier_semaphore()
        count = 0
        for step in range(1, self.fsdp):
            dev = (lax.rem(self.f + step, self.fsdp), self.c)
            pl.semaphore_signal(sem, inc=1, device_id=dev, device_id_type=MESH)
            count += 1
        for step in range(1, self.ctx):
            for core in range(2):
                dev = (self.line * 2 + core, lax.rem(self.c + step, self.ctx))
                pl.semaphore_signal(sem, inc=1, device_id=dev, device_id_type=MESH)
                count += 1
        pl.semaphore_wait(sem, count)

    def when(self, cond, act):
        if cond is True:
            act()
        else:
            pl.when(cond)(act)

    def send(self, src, dst, send_sem, recv_sem, dev, cond=True):
        def copy():
            return pltpu.make_async_remote_copy(
                src_ref=src, dst_ref=dst, send_sem=send_sem, recv_sem=recv_sem,
                device_id=dev, device_id_type=MESH,
            )

        if self.draining:
            self.when(cond, lambda: copy().wait_send())
            return
        self.when(cond, lambda: copy().start())
        self.started.append((cond, lambda: copy().wait_send()))

    def keep(self, src, dst, sem, cond=True):
        if self.draining:
            return
        self.when(cond, lambda: pltpu.make_async_copy(src, dst, sem).start())

    def arrive(self, dst, sem, cond=True):
        if self.draining:
            return
        self.when(cond, lambda: pltpu.make_async_copy(dst, dst, sem).wait())

    def drain(self):
        for cond, act in self.started:
            self.when(cond, act)
        self.started = []


def both(*conds):
    out = True
    for cond in conds:
        if cond is not True:
            out = cond if out is True else jnp.logical_and(out, cond)
    return out


def gather_kernel(
    fsdp, ctx,
    x, vf, wqkv, wo, gu, wd, gains,
    xs, vs, wq, wqh, wos, gus, wds, gs,
    x_sem, x_out, v_sem, v_out, q_sem, q_out, h_sem, g_sem, g_out, w_sem, w_z, w_p, w_s,
):
    plan = Plan(fsdp, ctx)
    f, c, core, line, home, half = plan.f, plan.c, plan.core, plan.line, plan.home, plan.half
    a, b, across, along, lines = plan.a, plan.b, plan.across, plan.along, plan.lines
    cols = vs.shape[2]
    owner = core == home
    sibling = (line * 2 + 1 - core, c)
    plan.barrier()

    def spread_x(j, below, above, cond):
        src, dst = xs.at[j], xs.at[j]
        if below:
            plan.send(src, dst, x_out.at[0, j], x_sem.at[j], (f, c - 1), both(cond, c > home * half))
        if above:
            plan.send(
                src, dst, x_out.at[1, j], x_sem.at[j], (f, c + 1),
                both(cond, c < home * half + half - 1),
            )
        plan.send(src, dst, x_out.at[2, j], x_sem.at[j], sibling, cond)

    away = jnp.logical_not(owner)
    entry = jnp.where(core == 0, half - 1, half)
    plan.send(x, xs.at[c], x_out.at[0, c], x_sem.at[c], (f, entry), away)
    plan.send(x, xs.at[c], x_out.at[0, c], x_sem.at[c], (f, c - 1), both(owner, c > home * half))
    plan.send(
        x, xs.at[c], x_out.at[1, c], x_sem.at[c], (f, c + 1),
        both(owner, c < home * half + half - 1),
    )
    plan.send(x, xs.at[c], x_out.at[2, c], x_sem.at[c], sibling, owner)
    plan.keep(x, xs.at[c], x_sem.at[c], owner)

    across_ctx = lax.rem(c + half, ctx)
    plan.send(wqkv, wqh, h_sem.at[0], h_sem.at[1], (f, across_ctx))

    def items(row, j):
        return (
            wos.at[row, :, pl.ds(pl.multiple_of(j * wo.shape[1], wo.shape[1]), wo.shape[1])],
            gus.at[j, row],
            wds.at[row, :, pl.ds(pl.multiple_of(j * wd.shape[1], wd.shape[1]), wd.shape[1])],
        )

    def spread_w(srcs, j, cond, up, down):
        dsts = items(f, j)
        for i in range(3):
            if up:
                plan.send(
                    srcs[i], dsts[i], w_z.at[i, 0, j], w_sem.at[i, f, j], (f, c + 1),
                    both(cond, c < ctx - 1),
                )
            if down:
                plan.send(
                    srcs[i], dsts[i], w_z.at[i, 1, j], w_sem.at[i, f, j], (f, c - 1),
                    both(cond, c > 0),
                )
        for i in range(3):
            for step in range(1, across):
                dev = ((lax.rem(a + step, across) * along + b) * 2 + core, c)
                plan.send(
                    srcs[i], dsts[i], w_p.at[i, step - 1, line, j], w_sem.at[i, f, j], dev, cond
                )
            for step in range(1, along):
                dev = ((a * along + lax.rem(b + step, along)) * 2 + core, c)
                plan.send(
                    srcs[i], dsts[i], w_p.at[i, across + step - 2, line, j], w_sem.at[i, f, j],
                    dev, cond,
                )
            plan.send(srcs[i], dsts[i], w_s.at[i, line, j], w_sem.at[i, f, j], sibling, cond)

    for step in range(1, fsdp):
        dev = (lax.rem(f + step, fsdp), c)
        plan.send(gains, gs.at[f], g_out.at[step - 1], g_sem.at[f], dev)
    plan.keep(gains, gs.at[f], g_sem.at[f])

    own = (wo, gu, wd)
    spread_w(own, c, True, True, True)
    for src, dst, i in zip(own, items(f, c), range(3)):
        plan.keep(src, dst, w_sem.at[i, f, c])

    for at in range(lines):
        dev = (at * 2, c)
        plan.send(wqkv, wq.at[f], q_out.at[0, at], q_sem.at[f], dev, jnp.logical_not(f == at * 2))
    plan.keep(wqkv, wq.at[f], q_sem.at[f], core == 0)

    for i in range(half):
        for k in range(2):
            to = core * half + i
            rank = lax.rem(to + k * half, ctx)
            src = vf.at[:, pl.ds(pl.multiple_of(rank * cols, cols), cols)]
            mine = both(owner, c == to, core == k)
            plan.send(
                src, vs.at[c], v_out.at[i, k], v_sem.at[c], (line * 2 + k, to),
                jnp.logical_not(mine),
            )
            plan.keep(src, vs.at[c], v_sem.at[c], mine)

    pltpu.make_async_copy(wqh, wqh, h_sem.at[1]).wait()
    for at in range(lines):
        dev = (at * 2 + 1, c)
        plan.send(
            wqh, wq.at[f], q_out.at[1, at], q_sem.at[f], dev, jnp.logical_not(f == at * 2 + 1)
        )
    plan.keep(wqh, wq.at[f], q_sem.at[f], core == 1)

    for dist in range(1, ctx):
        for side in range(2):
            j = c - dist if side == 0 else c + dist
            there = j >= 0 if side == 0 else j < ctx
            at = jnp.clip(j, 0, ctx - 1)
            cond = both(owner, there)
            plan.arrive(xs.at[at], x_sem.at[at], cond)
            spread_x(at, side == 1, side == 0, cond)
        for side in range(2):
            j = c - dist if side == 0 else c + dist
            there = j >= 0 if side == 0 else j < ctx
            at = jnp.clip(j, 0, ctx - 1)
            dsts = items(f, at)
            for i in range(3):
                plan.arrive(dsts[i], w_sem.at[i, f, at], there)
            spread_w(dsts, at, there, side == 0, side == 1)

    for dist in range(ctx):
        for side in range(2 if dist else 1):
            j = c - dist if side == 0 else c + dist
            there = j >= 0 if side == 0 else j < ctx
            at = jnp.clip(j, 0, ctx - 1)
            first = at < half
            for step in range(1, across):
                from_line = lax.rem(a + across - step, across) * along + b
                row = from_line * 2 + core
                dsts = items(row, at)
                for i in range(3):
                    plan.arrive(dsts[i], w_sem.at[i, row, at], there)
                for i in range(3):
                    for hop in range(1, along):
                        dev = ((a * along + lax.rem(b + hop, along)) * 2 + core, c)
                        plan.send(
                            dsts[i], dsts[i], w_p.at[i, across + hop - 2, from_line, at],
                            w_sem.at[i, row, at], dev, both(there, first),
                        )
                    plan.send(
                        dsts[i], dsts[i], w_s.at[i, from_line, at], w_sem.at[i, row, at], sibling,
                        there,
                    )
            for step in range(1, along):
                from_line = a * along + lax.rem(b + along - step, along)
                row = from_line * 2 + core
                dsts = items(row, at)
                for i in range(3):
                    plan.arrive(dsts[i], w_sem.at[i, row, at], there)
                for i in range(3):
                    for hop in range(1, across):
                        dev = ((lax.rem(a + hop, across) * along + b) * 2 + core, c)
                        plan.send(
                            dsts[i], dsts[i], w_p.at[i, hop - 1, from_line, at],
                            w_sem.at[i, row, at], dev, both(there, jnp.logical_not(first)),
                        )
                    plan.send(
                        dsts[i], dsts[i], w_s.at[i, from_line, at], w_sem.at[i, row, at], sibling,
                        there,
                    )
    for dist in range(ctx):
        for side in range(2 if dist else 1):
            j = c - dist if side == 0 else c + dist
            there = j >= 0 if side == 0 else j < ctx
            at = jnp.clip(j, 0, ctx - 1)
            for step in range(1, across):
                for hop in range(1, along):
                    from_line = lax.rem(a + step, across) * along + lax.rem(b + hop, along)
                    row = from_line * 2 + core
                    dsts = items(row, at)
                    for i in range(3):
                        plan.arrive(dsts[i], w_sem.at[i, row, at], there)
                        plan.send(
                            dsts[i], dsts[i], w_s.at[i, from_line, at], w_sem.at[i, row, at],
                            sibling, there,
                        )

    for i in range(3):
        plan.arrive(items(f, c)[i], w_sem.at[i, f, c])

    def far(at, carry):
        row = at * 2 + 1 - core
        for j in range(ctx):
            dsts = items(row, j)
            for i in range(3):
                plan.arrive(dsts[i], w_sem.at[i, row, j])
        return carry

    lax.fori_loop(0, lines, far, 0)
    for j in range(ctx):
        plan.arrive(xs.at[j], x_sem.at[j], both(jnp.logical_or(away, c == j)))
        plan.arrive(vs.at[j], v_sem.at[j])
    for row in range(fsdp):
        plan.arrive(wq.at[row], q_sem.at[row])
        plan.arrive(gs.at[row], g_sem.at[row])
    plan.drain()


def gather(mesh, x, vf, wqkv, wo, gu, wd, gains):
    fsdp, ctx = mesh.shape["fsdp"], mesh.shape["ctx"]
    tokens, depth = x.shape
    cols = depth // ctx
    lines = fsdp // 2
    across = math.isqrt(lines)
    peers = max(across - 1 + lines // across - 1, 1)
    anywhere = pl.BlockSpec(memory_space=pl.ANY)
    dma = pltpu.SemaphoreType.DMA
    return pl.pallas_call(
        functools.partial(gather_kernel, fsdp, ctx),
        out_shape=(
            jax.ShapeDtypeStruct((ctx, tokens, depth), BF16),
            jax.ShapeDtypeStruct((ctx, tokens, cols), BF16),
            jax.ShapeDtypeStruct((fsdp,) + wqkv.shape, BF16),
            jax.ShapeDtypeStruct(wqkv.shape, BF16),
            jax.ShapeDtypeStruct((fsdp, wo.shape[0], depth), BF16),
            jax.ShapeDtypeStruct((ctx, fsdp) + gu.shape, BF16),
            jax.ShapeDtypeStruct((fsdp, wd.shape[0], depth), BF16),
            jax.ShapeDtypeStruct((fsdp,) + gains.shape, F32),
        ),
        in_specs=[anywhere] * 7,
        out_specs=[anywhere] * 8,
        scratch_shapes=[
            dma((ctx,)), dma((3, ctx)), dma((ctx,)), dma((ctx // 2, 2)),
            dma((fsdp,)), dma((2, lines)), dma((2,)), dma((fsdp,)), dma((fsdp,)),
            dma((3, fsdp, ctx)), dma((3, 2, ctx)), dma((3, peers, lines, ctx)), dma((3, lines, ctx)),
        ],
        compiler_params=pltpu.CompilerParams(collective_id=0, has_side_effects=True),
        name="gather_all",
    )(x, vf, wqkv, wo, gu, wd, gains)


def trade_kernel(fsdp, ctx, inward, src_ref, dst_ref, recv, sent):
    plan = Plan(fsdp, ctx)
    f, c, core, line, home, half = plan.f, plan.c, plan.core, plan.line, plan.home, plan.half
    cols = (src_ref if inward else dst_ref).shape[2]
    plan.barrier()

    def band(rank):
        return pl.ds(pl.multiple_of(rank * cols, cols), cols)

    if inward:
        rank = lax.rem(c + core * half, ctx)
        for step in range(ctx):
            j = lax.rem(c + step, ctx)
            src, dst = src_ref.at[j], dst_ref.at[:, band(rank)]
            dev = (line * 2 + home, j)
            mine = both(core == home) if step == 0 else False
            if step == 0:
                plan.keep(src, dst, recv.at[rank], mine)
                plan.send(src, dst, sent.at[j], recv.at[rank], dev, jnp.logical_not(mine))
            else:
                plan.send(src, dst, sent.at[j], recv.at[rank], dev)
        for rank in range(ctx):
            plan.arrive(dst_ref.at[:, band(rank)], recv.at[rank])
    else:
        for i in range(half):
            for k in range(2):
                to = core * half + i
                src = src_ref.at[:, band(lax.rem(to + k * half, ctx))]
                mine = both(core == home, c == to, core == k)
                plan.send(
                    src, dst_ref.at[c], sent.at[i * 2 + k], recv.at[c], (line * 2 + k, to),
                    jnp.logical_not(mine),
                )
                plan.keep(src, dst_ref.at[c], recv.at[c], mine)
        for j in range(ctx):
            plan.arrive(dst_ref.at[j], recv.at[j])
    plan.drain()


def trade(mesh, array, inward, ident):
    fsdp, ctx = mesh.shape["fsdp"], mesh.shape["ctx"]
    if inward:
        shape = (array.shape[1], array.shape[2] * ctx)
    else:
        shape = (ctx, array.shape[0], array.shape[1] // ctx)
    anywhere = pl.BlockSpec(memory_space=pl.ANY)
    return pl.pallas_call(
        functools.partial(trade_kernel, fsdp, ctx, inward),
        out_shape=jax.ShapeDtypeStruct(shape, BF16),
        in_specs=[anywhere],
        out_specs=anywhere,
        scratch_shapes=[pltpu.SemaphoreType.DMA((ctx,)), pltpu.SemaphoreType.DMA((ctx,))],
        compiler_params=pltpu.CompilerParams(collective_id=ident, has_side_effects=True),
        name="trade_in" if inward else "trade_out",
    )(array)


def feed_kernel(
    fsdp, ctx,
    o, x, dy, wo, gain, gu, wd,
    out, dx2, do, dg, s_wo, s_gu, s_wd,
    x2, h2, h2t, total, dh2, act, dgu,
    my_gu, my_wd, my_wo, got_gu, got_wd, got_wo,
    gu_sem, gu_out, wd_sem, wd_out, wo_sem, wo_out,
):
    plan = Plan(fsdp, ctx)
    core = plan.core
    sibling = (plan.line * 2 + 1 - core, plan.c)
    step = pl.program_id(0)
    last = pl.num_programs(0) - 1
    tokens, depth = x.shape
    chunk = wd.shape[0]
    blocks = tokens // BLOCK
    lines = plan.lines
    shard = depth // fsdp
    row_lines = my_wd.shape[1]
    row_count = my_wd.shape[3]
    slot = lax.rem(step, 2)

    def give(at):
        place = lax.rem(at, 2)
        for i in range(lines):
            plan.send(
                my_gu.at[place, i, 1 - core], got_gu.at[at, i], gu_out.at[place, i],
                gu_sem.at[at, i], sibling,
            )
        for i in range(row_lines):
            plan.send(
                my_wd.at[place, i, 1 - core], got_wd.at[at, i], wd_out.at[place, i],
                wd_sem.at[at, i], sibling,
            )

    def given(at):
        plan.draining = True
        give(at)
        plan.draining = False

    @pl.when(step == 0)
    def _():
        sem = pltpu.get_barrier_semaphore()
        pl.semaphore_signal(sem, inc=1, device_id=sibling, device_id_type=MESH)
        pl.semaphore_wait(sem, 1)

        def rows_of(b, carry):
            rows = pl.ds(pl.multiple_of(b * BLOCK, BLOCK), BLOCK)
            mid = x[rows, :].astype(F32) + nn(o[rows, :], wo[...])
            x2[rows, :] = mid
            rstd = lax.rsqrt(jnp.mean(mid * mid, axis=1, keepdims=True) + EPSILON)
            hv = (mid * rstd * gain[...]).astype(BF16)
            h2[rows, :] = hv
            h2t[:, rows] = hv.T
            total[rows, :] = mid
            dh2[rows, :] = jnp.zeros((BLOCK, depth), F32)
            return carry

        lax.fori_loop(0, blocks, rows_of, 0)

    @pl.when(jnp.logical_and(step >= 2, step < last))
    def _():
        given(step - 2)

    @pl.when(step < last)
    def _():
        def rows_of(b, carry):
            rows = pl.ds(pl.multiple_of(b * BLOCK, BLOCK), BLOCK)
            both_ = nn(h2[rows, :], gu[0])
            gate = both_[:, :chunk]
            up = both_[:, chunk:]
            da = nt(dy[rows, :], wd[...]).astype(BF16).astype(F32)
            sig = 1.0 / (1.0 + jnp.exp(-gate))
            silu = gate * sig
            av = (silu * up).astype(BF16)
            act[rows, :] = av
            dgate = (da * up * (sig * (1.0 + gate * (1.0 - sig)))).astype(BF16)
            dup = (da * silu).astype(BF16)
            dv = jnp.concatenate([dgate, dup], axis=1)
            dgu[rows, :] = dv
            total[rows, :] = total[rows, :] + nn(av, wd[...])
            dh2[rows, :] = dh2[rows, :] + nt(dv, gu[0])
            return carry

        lax.fori_loop(0, blocks, rows_of, 0)

        for part in range(depth // 512):
            at = slice(part * 512, (part + 1) * 512)
            val = tn(act[...], dy[:, at])
            for r in range(row_lines * 2):
                my_wd[slot, r // 2, r % 2, :, at] = val[
                    r * row_count : (r + 1) * row_count
                ].astype(BF16)

        rows_each = BLOCK // shard

        def weight(b, carry):
            rows = pl.ds(pl.multiple_of(b * BLOCK, BLOCK), BLOCK)
            val = nn(h2t[rows, :], dgu[...]).astype(BF16)
            for r in range(rows_each):
                my_gu[slot, b * (rows_each // 2) + r // 2, r % 2] = val[
                    r * shard : (r + 1) * shard
                ]
            return carry

        lax.fori_loop(0, depth // BLOCK, weight, 0)
        give(step)

    def collect(at):
        place = lax.rem(at, 2)
        for i in range(lines):
            plan.arrive(got_gu.at[at, i], gu_sem.at[at, i])
            add_rows(s_gu.at[0, i], [my_gu.at[place, i, core], got_gu.at[at, i]])
        for i in range(row_lines):
            plan.arrive(got_wd.at[at, i], wd_sem.at[at, i])
            add_rows(s_wd.at[i], [my_wd.at[place, i, core], got_wd.at[at, i]])

    @pl.when(jnp.logical_and(step >= 1, step < last))
    def _():
        collect(step - 1)

    @pl.when(step == last)
    def _():
        dg[...] = jnp.zeros_like(dg)

        def rows_of(b, carry):
            rows = pl.ds(pl.multiple_of(b * BLOCK, BLOCK), BLOCK)
            out[rows, :] = total[rows, :].astype(BF16)
            mid = x2[rows, :]
            rstd = lax.rsqrt(jnp.mean(mid * mid, axis=1, keepdims=True) + EPSILON)
            xhat = mid * rstd
            dh = dh2[rows, :]
            u = dh * gain[...]
            dm = dy[rows, :].astype(F32) + rstd * (
                u - xhat * jnp.mean(u * xhat, axis=1, keepdims=True)
            )
            dx2[rows, :] = dm
            dg[0:1, :] = dg[0:1, :] + jnp.sum(dh * xhat, axis=0, keepdims=True)
            h2[rows, :] = dm.astype(BF16)
            return carry

        lax.fori_loop(0, blocks, rows_of, 0)
        rows_each = BLOCK // shard

        def weight_out(b, carry):
            at = pl.ds(pl.multiple_of(b * BLOCK, BLOCK), BLOCK)
            val = tn(o[:, at], h2[...]).astype(BF16)
            for r in range(rows_each):
                my_wo[b * (rows_each // 2) + r // 2, r % 2] = val[r * shard : (r + 1) * shard]
            return carry

        lax.fori_loop(0, depth // BLOCK, weight_out, 0)
        for i in range(lines):
            plan.send(my_wo.at[i, 1 - core], got_wo.at[i], wo_out.at[i], wo_sem.at[i], sibling)

        def rows_out(b, carry):
            rows = pl.ds(pl.multiple_of(b * BLOCK, BLOCK), BLOCK)
            do[rows, :] = nt(h2[rows, :], wo[...]).astype(BF16)
            return carry

        lax.fori_loop(0, blocks, rows_out, 0)
        collect(last - 1)
        for i in range(lines):
            plan.arrive(got_wo.at[i], wo_sem.at[i])
            add_rows(s_wo.at[i], [my_wo.at[i, core], got_wo.at[i]])
        for at in (last - 2, last - 1):
            given(at)
        plan.draining = True
        for i in range(lines):
            plan.send(my_wo.at[i, 1 - core], got_wo.at[i], wo_out.at[i], wo_sem.at[i], sibling)
        plan.draining = False


def feed_forward(mesh, o, x, dy, wo, gain, gu, wd):
    fsdp, ctx = mesh.shape["fsdp"], mesh.shape["ctx"]
    tokens, depth = x.shape
    steps, _, width = gu.shape
    chunk = width // 2
    lines = fsdp // 2
    shard = depth // fsdp
    row_count = wd.shape[0] // fsdp
    row_lines = fsdp // ctx // 2
    once = pl.Buffered(1)

    def whole(shape):
        return pl.BlockSpec(shape, lambda i: (0,) * len(shape), pipeline_mode=once)

    def whole_out(shape):
        return pl.BlockSpec(shape, lambda i: (0,) * len(shape), pipeline_mode=once)

    shapes = (
        jax.ShapeDtypeStruct((tokens, depth), BF16),
        jax.ShapeDtypeStruct((tokens, depth), F32),
        jax.ShapeDtypeStruct((tokens, depth), BF16),
        jax.ShapeDtypeStruct((8, depth), F32),
        jax.ShapeDtypeStruct((lines, shard, depth), BF16),
        jax.ShapeDtypeStruct((ctx, lines, shard, width), BF16),
        jax.ShapeDtypeStruct((lines, row_count, depth), BF16),
    )
    dma = pltpu.SemaphoreType.DMA
    return pl.pallas_call(
        functools.partial(feed_kernel, fsdp, ctx),
        grid=(steps + 1,),
        out_shape=shapes,
        in_specs=[
            whole((tokens, depth)),
            whole((tokens, depth)),
            whole((tokens, depth)),
            whole((depth, depth)),
            whole((1, depth)),
            pl.BlockSpec((1, depth, width), lambda i: (jnp.minimum(i, steps - 1), 0, 0)),
            pl.BlockSpec((chunk, depth), lambda i: (jnp.minimum(i, steps - 1), 0)),
        ],
        out_specs=[
            whole_out((tokens, depth)),
            whole_out((tokens, depth)),
            whole_out((tokens, depth)),
            whole_out((8, depth)),
            whole_out((lines, shard, depth)),
            pl.BlockSpec((1, lines, shard, width), lambda i: (jnp.maximum(i - 1, 0), 0, 0, 0)),
            pl.BlockSpec((row_lines, row_count, depth), lambda i: (jnp.maximum(i - 1, 0), 0, 0)),
        ],
        scratch_shapes=[
            pltpu.VMEM((tokens, depth), F32),
            pltpu.VMEM((tokens, depth), BF16),
            pltpu.VMEM((depth, tokens), BF16),
            pltpu.VMEM((tokens, depth), F32),
            pltpu.VMEM((tokens, depth), F32),
            pltpu.VMEM((tokens, chunk), BF16),
            pltpu.VMEM((tokens, width), BF16),
            pltpu.VMEM((2, lines, 2, shard, width), BF16),
            pltpu.VMEM((2, row_lines, 2, row_count, depth), BF16),
            pltpu.VMEM((lines, 2, shard, depth), BF16),
            pltpu.VMEM((steps, lines, shard, width), BF16),
            pltpu.VMEM((steps, row_lines, row_count, depth), BF16),
            pltpu.VMEM((lines, shard, depth), BF16),
            dma((steps, lines)), dma((2, lines)), dma((steps, row_lines)), dma((2, row_lines)),
            dma((lines,)), dma((lines,)),
        ],
        compiler_params=pltpu.CompilerParams(
            vmem_limit_bytes=VMEM_LIMIT, dimension_semantics=("arbitrary",), collective_id=4,
            has_side_effects=True,
        ),
        name="feed_forward",
    )(o, x, dy, wo, gain, gu, wd)


def chunk_rows(count):
    return 32 if count % 32 == 0 else count


def add_rows(dst, parts):
    count = dst.shape[0]
    rows = chunk_rows(count)

    def body(t, carry):
        at = pl.ds(pl.multiple_of(t * rows, rows), rows)
        total = parts[0][at, :].astype(F32)
        for part in parts[1:]:
            total = total + part[at, :].astype(F32)
        dst[at, :] = total.astype(dst.dtype)
        return carry

    lax.fori_loop(0, count // rows, body, 0)


class Reduction:
    def __init__(self, plan, sources, own, near, next_, last, outs, sems):
        self.plan = plan
        self.sources, self.own, self.near, self.next, self.last, self.outs = (
            sources, own, near, next_, last, outs,
        )
        (
            self.own_sem, self.near_sem, self.near_out, self.next_sem, self.next_out,
            self.last_sem, self.last_out,
        ) = sems
        self.side = plan.across

    def line_of(self, low, first, second):
        return second * self.plan.along + first if low else first * self.plan.along + second

    def places(self, j):
        plan = self.plan
        low = j < plan.half
        return (low, plan.b if low else plan.a, plan.a if low else plan.b)

    def piece(self, i, line, j):
        src = self.sources[i]
        if i == 1:
            return src.at[j, line]
        width = src.shape[2] // self.plan.ctx
        return src.at[line, :, pl.ds(j * width, width)]

    def start(self, order):
        plan = self.plan
        for j in order:
            low, first, second = self.places(j)
            for hop in range(1, self.side):
                to = lax.rem(first + hop, self.side)
                dev = (self.line_of(low, to, second) * 2 + plan.core, plan.c)
                for i in range(3):
                    for inner in range(self.side):
                        plan.send(
                            self.piece(i, self.line_of(low, to, inner), j),
                            self.near[i].at[j, hop - 1, inner],
                            self.near_out.at[i, j, hop - 1, inner],
                            self.near_sem.at[i, j, hop - 1, inner],
                            dev,
                        )
            for i in range(3):
                for inner in range(self.side):
                    plan.keep(
                        self.piece(i, self.line_of(low, first, inner), j),
                        self.own[i].at[j, inner],
                        self.own_sem.at[i, j, inner],
                    )

    def step_near(self, j):
        plan = self.plan
        low, first, second = self.places(j)
        for i in range(3):
            for inner in range(self.side):
                plan.arrive(self.own[i].at[j, inner], self.own_sem.at[i, j, inner])
                for hop in range(1, self.side):
                    plan.arrive(
                        self.near[i].at[j, hop - 1, inner], self.near_sem.at[i, j, hop - 1, inner]
                    )
                if not plan.draining:
                    add_rows(
                        self.own[i].at[j, inner],
                        [self.own[i].at[j, inner]]
                        + [self.near[i].at[j, hop - 1, inner] for hop in range(1, self.side)],
                    )
        for hop in range(1, self.side):
            to = lax.rem(second + hop, self.side)
            dev = (self.line_of(low, first, to) * 2 + plan.core, plan.c)
            for i in range(3):
                plan.send(
                    self.own[i].at[j, to],
                    self.next[i].at[j, hop - 1],
                    self.next_out.at[i, j, hop - 1],
                    self.next_sem.at[i, j, hop - 1],
                    dev,
                )

    def step_next(self, j):
        plan = self.plan
        low, first, second = self.places(j)
        mine = plan.c == j
        for i in range(3):
            for hop in range(1, self.side):
                plan.arrive(self.next[i].at[j, hop - 1], self.next_sem.at[i, j, hop - 1])
            if not plan.draining:
                add_rows(
                    self.own[i].at[j, second],
                    [self.own[i].at[j, second]]
                    + [self.next[i].at[j, hop - 1] for hop in range(1, self.side)],
                )
            plan.send(
                self.own[i].at[j, second],
                self.last[i].at[plan.c],
                self.last_out.at[i, j],
                self.last_sem.at[i, plan.c],
                (plan.f, j),
                jnp.logical_not(mine),
            )
            plan.keep(
                self.own[i].at[j, second], self.last[i].at[plan.c], self.last_sem.at[i, plan.c],
                mine,
            )

    def finish(self):
        plan = self.plan
        for i in range(3):
            for j in range(plan.ctx):
                plan.arrive(self.last[i].at[j], self.last_sem.at[i, j])
            add_rows(self.outs[i], [self.last[i].at[j] for j in range(plan.ctx)])


def backward_kernel(
    fsdp, ctx,
    d_out, x_in, q_in, k_in, vm_in, kt_in, att_in, lse, wqkv_in, gain, table_in, start,
    dg_two, s_wo, s_gu, s_wd,
    folded, vout, g_wo, g_gu, g_wd, g_qkv, dg_all,
    part, q, k, vm, kt, att, do, wqkv, table,
    dqt, dkk, dvv, rows_t, d3, gw_full, gw,
    other, chain, gw_near, gw_sum, gw_last, dg, dg_near, dg_sum, dg_last,
    o_wo, o_gu, o_wd, n_wo, n_gu, n_wd, x_wo, x_gu, x_wd, l_wo, l_gu, l_wd,
    load_sem, do_sem, do_out, v_sem, v_out,
    sib_sem, sib_out, chain_sem, chain_out, end_sem, end_out,
    gw_sem, gw_out, gl_sem, gl_out, dn_sem, dn_out, dl_sem, dl_out,
    own_sem, near_sem, near_out, next_sem, next_out, last_sem, last_out,
):
    plan = Plan(fsdp, ctx)
    f, c, core, line, home, half = plan.f, plan.c, plan.core, plan.line, plan.home, plan.half
    lines = plan.lines
    sibling = (line * 2 + 1 - core, c)
    low, high = home * half, home * half + half - 1
    blocks, _, depth = part.shape
    group = blocks * BLOCK
    cols = vm.shape[1]
    heads = cols // HEAD
    tokens = group // ctx
    per = tokens // BLOCK
    pairs = blocks // 2
    plan.barrier()

    for i in range(half):
        for kk in range(2):
            to = core * half + i
            rank = lax.rem(to + kk * half, ctx)
            src = d_out.at[:, pl.ds(pl.multiple_of(rank * cols, cols), cols)]
            mine = both(core == home, c == to, core == kk)
            plan.send(
                src, do.at[c], do_out.at[i * 2 + kk], do_sem.at[c], (line * 2 + kk, to),
                jnp.logical_not(mine),
            )
            plan.keep(src, do.at[c], do_sem.at[c], mine)
    loads = (
        (q_in, q), (k_in, k), (vm_in, vm), (kt_in, kt), (att_in, att), (table_in, table),
        (wqkv_in, wqkv), (x_in, part),
    )
    for i, (src, dst) in enumerate(loads):
        plan.keep(src, dst, load_sem.at[i])
    reduction = Reduction(
        plan, (s_wo, s_gu, s_wd), (o_wo, o_gu, o_wd), (n_wo, n_gu, n_wd), (x_wo, x_gu, x_wd),
        (l_wo, l_gu, l_wd), (g_wo, g_gu, g_wd),
        (own_sem, near_sem, near_out, next_sem, next_out, last_sem, last_out),
    )
    order = []
    for i in range(half):
        order += [i, half + i]
    reduction.start(order)

    dqt[...] = jnp.zeros_like(dqt)
    dkk[...] = jnp.zeros_like(dkk)
    dvv[...] = jnp.zeros_like(dvv)
    gw_full[...] = jnp.zeros_like(gw_full)
    dg[...] = jnp.zeros_like(dg)
    dg[1:2, :] = dg_two[0:1, :]
    for i, (src, dst) in enumerate(loads):
        plan.arrive(dst, load_sem.at[i])
    for j in range(ctx):
        plan.arrive(do.at[j], do_sem.at[j])

    def grads_of(b):
        return do[b // per, pl.ds(pl.multiple_of(lax.rem(b, per) * BLOCK, BLOCK), BLOCK), :]

    def dots(b, carry):
        rows = pl.ds(pl.multiple_of(b * BLOCK, BLOCK), BLOCK)
        prod = grads_of(b).astype(F32) * att[rows, :]
        upper = prod.astype(BF16)
        lower = (prod - upper.astype(F32)).astype(BF16)
        head_row = lax.broadcasted_iota(jnp.int32, (8, cols), 0)
        lane = lax.broadcasted_iota(jnp.int32, (8, cols), 1)
        choose = (lane // HEAD == head_row).astype(F32).astype(BF16)
        rows_t[:, rows] = nt(choose, upper) + nt(choose, lower)
        return carry

    lax.fori_loop(0, blocks, dots, 0)

    def tile(kb, qb):
        krows = pl.ds(pl.multiple_of(kb * BLOCK, BLOCK), BLOCK)
        rows = pl.ds(pl.multiple_of(qb * BLOCK, BLOCK), BLOCK)
        kv = k[krows, :]
        vv = vm[krows, :]
        qv = q[rows, :]
        dov = grads_of(qb)
        key_pos = kb * BLOCK + lax.broadcasted_iota(jnp.int32, (BLOCK, BLOCK), 0)
        query_pos = qb * BLOCK + lax.broadcasted_iota(jnp.int32, (BLOCK, BLOCK), 1)
        allowed = (key_pos <= query_pos) & (key_pos >= start[0:1, rows])
        dk_sum = dkk[krows, :]
        dv_sum = dvv[krows, :]
        for head in range(heads):
            band = slice(head * HEAD, (head + 1) * HEAD)
            lanes = head_lanes(qv.shape, head)
            qm = jnp.where(lanes, qv, jnp.zeros_like(qv))
            dom = jnp.where(lanes, dov, jnp.zeros_like(dov))
            s = jnp.where(allowed, nt(kv, qm), NEGATIVE)
            p = jnp.exp(s - lse[head : head + 1, rows])
            ds = (p * (nt(vv, dom) - rows_t[head : head + 1, rows])).astype(BF16)
            dv_sum = dv_sum + nn(p.astype(BF16), dom)
            dk_sum = dk_sum + nn(ds, qm)
            dqt[band, rows] = dqt[band, rows] + nn(kt[band, krows], ds)
        dkk[krows, :] = dk_sum
        dvv[krows, :] = dv_sum

    def unit_of(t):
        return jnp.where(home == 0, blocks - 1 - t, t)

    def finish(o):
        rows = pl.ds(pl.multiple_of(o * BLOCK, BLOCK), BLOCK)
        cos_v, sin_v = turns(table[rows, :], cols)
        dq = dqt[:, rows].T * (1.0 / math.sqrt(HEAD))
        d3[rows, :cols] = (dq * cos_v - half_swap(dq) * sin_v).astype(BF16)
        dk = dkk[rows, :]
        d3[rows, cols : 2 * cols] = (dk * cos_v - half_swap(dk) * sin_v).astype(BF16)
        d3[rows, 2 * cols :] = (0.5 * dvv[rows, :]).astype(BF16)
        dh = nt(d3[rows, :], wqkv[...])
        xv = part[o].astype(F32)
        rstd = lax.rsqrt(jnp.mean(xv * xv, axis=1, keepdims=True) + EPSILON)
        xhat = xv * rstd
        h1 = (xhat * gain[...]).astype(BF16)
        u = dh * gain[...]
        part[o] = (rstd * (u - xhat * jnp.mean(u * xhat, axis=1, keepdims=True))).astype(BF16)
        dg[0:1, :] = dg[0:1, :] + jnp.sum(dh * xhat, axis=0, keepdims=True)
        gw_full[...] = gw_full[...] + tn(h1, d3[rows, :])

    def give(t):
        o = unit_of(t)
        slot = t // 2
        plan.send(
            part.at[o], other.at[slot], sib_out.at[slot], sib_sem.at[slot], sibling,
            lax.rem(o, 2) != core,
        )

    def pair_unit(i):
        return jnp.where(home == 0, blocks - 2 - 2 * i, 2 * i) + core

    def add_unit(o, src):
        def body(t, carry):
            at = pl.ds(pl.multiple_of(t * 32, 32), 32)
            part[o, at, :] = (part[o, at, :].astype(F32) + src[at, :].astype(F32)).astype(BF16)
            return carry

        lax.fori_loop(0, BLOCK // 32, body, 0)

    def sum_pair(i):
        plan.arrive(other.at[i], sib_sem.at[i])
        if not plan.draining:
            add_unit(pair_unit(i), other.at[i])

    def pass_pair(i, hears):
        o = pair_unit(i)
        j = o // per
        top = jnp.minimum(j, high)
        bottom = jnp.maximum(j, low)
        from_below = both(c > low, c <= top)
        from_above = both(c < high, c >= bottom)
        now = jnp.logical_or(from_below, from_above) == hears
        spot = jnp.where(j == c, pairs, i)
        if hears and not plan.draining:

            @pl.when(from_below)
            def _():
                plan.arrive(chain.at[i], chain_sem.at[i])
                add_unit(o, chain.at[i])

            @pl.when(from_above)
            def _():
                plan.arrive(chain.at[spot], chain_sem.at[spot])
                add_unit(o, chain.at[spot])

        plan.send(
            part.at[o], chain.at[i], chain_out.at[0, i], chain_sem.at[i], (f, c + 1),
            both(now, c < top),
        )
        below = jnp.where(j == c - 1, pairs, i)
        plan.send(
            part.at[o], chain.at[below], chain_out.at[1, i], chain_sem.at[below], (f, c - 1),
            both(now, c > bottom),
        )
        end = jnp.clip(j, low, high)
        mine = both(c == end, j == c, core == home)
        where = lax.rem(o, per)
        dst = folded.at[pl.ds(pl.multiple_of(where * BLOCK, BLOCK), BLOCK), :]
        plan.send(
            part.at[o], dst, end_out.at[i], end_sem.at[where], (line * 2 + home, j),
            both(now, c == end, jnp.logical_not(mine)),
        )
        plan.keep(part.at[o], dst, end_sem.at[where], both(now, mine))

    rank = lax.rem(c + core * half, ctx)

    def give_values(i):
        j = jnp.where(home == 0, ctx - 1 - i, i)
        src = d3.at[pl.ds(pl.multiple_of(j * tokens, tokens), tokens), 2 * cols : 3 * cols]
        dst = vout.at[:, pl.ds(pl.multiple_of(rank * cols, cols), cols)]
        mine = both(core == home, c == j)
        plan.send(
            src, dst, v_out.at[i], v_sem.at[rank], (line * 2 + home, j), jnp.logical_not(mine)
        )
        plan.keep(src, dst, v_sem.at[rank], mine)

    schedule = {}

    def at_step(t, act):
        schedule.setdefault(t, []).append(act)

    scale = blocks // 8
    for j in order[:half]:
        at_step(NEAR_A * scale, lambda j=j: reduction.step_near(j))
        at_step(NEXT_A * scale, lambda j=j: reduction.step_next(j))
    for j in order[half:]:
        at_step(NEAR_B * scale, lambda j=j: reduction.step_near(j))
        at_step(NEXT_B * scale, lambda j=j: reduction.step_next(j))
    for i in range(pairs - 1):
        at_step(2 * i + 1, lambda i=i: give_values(i))
        at_step(2 * i + 2, lambda i=i: sum_pair(i))
        at_step(2 * i + 2, lambda i=i: pass_pair(i, False))
        if i < pairs - 2:
            at_step(2 * i + 4, lambda i=i: pass_pair(i, True))
    at_step(blocks - 1, lambda: give_values(pairs - 1))

    def step(t, carry):
        o = unit_of(t)

        def inner(i, carry2):
            tile(jnp.where(home == 0, i, o), jnp.where(home == 0, o, o + i))
            return carry2

        lax.fori_loop(0, blocks - t, inner, 0)
        finish(o)
        give(t)
        for s in sorted(schedule):

            @pl.when(t == s)
            def _(s=s):
                for act in schedule[s]:
                    act()

        return carry

    plan.started_at_top = plan.started
    plan.started = []
    lax.fori_loop(0, blocks, step, 0)
    plan.started = plan.started_at_top

    for hop in range(1, fsdp):
        dev = (lax.rem(f + hop, fsdp), c)
        plan.send(dg, dg_near.at[f], dn_out.at[hop - 1], dn_sem.at[f], dev)
    plan.keep(dg, dg_near.at[f], dn_sem.at[f])

    pass_pair(pairs - 2, True)
    sum_pair(pairs - 1)
    pass_pair(pairs - 1, False)
    shard = depth // fsdp
    rows_each = BLOCK // shard

    def weight(b, carry):
        at = pl.ds(pl.multiple_of(b * BLOCK, BLOCK), BLOCK)
        val = gw_full[at, :].astype(BF16)
        for r in range(rows_each):
            gw[b * (rows_each // 2) + r // 2, r % 2] = val[r * shard : (r + 1) * shard]
        return carry

    lax.fori_loop(0, depth // BLOCK, weight, 0)
    for hop in range(1, lines):
        to = lax.rem(line + hop, lines)
        plan.send(
            gw.at[to], gw_near.at[hop - 1], gw_out.at[hop - 1], gw_sem.at[hop - 1],
            (to * 2 + core, c),
        )
    pass_pair(pairs - 1, True)

    for at in range(fsdp):
        plan.arrive(dg_near.at[at], dn_sem.at[at])
    total = dg_near[0]
    for at in range(1, fsdp):
        total = total + dg_near[at]
    dg_sum[...] = total
    for hop in range(1, ctx):
        plan.send(
            dg_sum, dg_last.at[c], dl_out.at[hop - 1], dl_sem.at[c], (f, lax.rem(c + hop, ctx))
        )
    plan.keep(dg_sum, dg_last.at[c], dl_sem.at[c])

    for hop in range(1, lines):
        plan.arrive(gw_near.at[hop - 1], gw_sem.at[hop - 1])
    for kk in range(2):
        add_rows(
            gw_sum.at[kk], [gw.at[line, kk]] + [gw_near.at[hop - 1, kk] for hop in range(1, lines)]
        )
    plane = jnp.where(core == 0, c, lax.rem(c + half, ctx))
    for kk in range(2):
        mine = both(core == 0, kk == 0)
        plan.send(
            gw_sum.at[kk], gw_last.at[core], gl_out.at[kk], gl_sem.at[core], (line * 2 + kk, plane),
            jnp.logical_not(mine),
        )
        plan.keep(gw_sum.at[kk], gw_last.at[core], gl_sem.at[core], mine)

    reduction.finish()
    for at in range(ctx):
        plan.arrive(dg_last.at[at], dl_sem.at[at])
    total = dg_last[0]
    for at in range(1, ctx):
        total = total + dg_last[at]
    dg_all[...] = total
    for kk in range(2):
        plan.arrive(gw_last.at[kk], gl_sem.at[kk])
    add_rows(g_qkv, [gw_last.at[0], gw_last.at[1]])
    for at in range(per):
        plan.arrive(folded.at[pl.ds(at * BLOCK, BLOCK), :], end_sem.at[at])
    for at in range(ctx):
        plan.arrive(vout.at[:, pl.ds(at * cols, cols)], v_sem.at[at])
    plan.drain()
    plan.draining = True
    for t in range(blocks):
        give(t)
    for s in sorted(schedule):
        for act in schedule[s]:
            act()


NEAR_A, NEAR_B, NEXT_A, NEXT_B = 1, 3, 4, 6


def backward(mesh, d_out, x, q, k, vm, kt, att, lse, wqkv, gain, table, start, dg_two, sums):
    fsdp, ctx = mesh.shape["fsdp"], mesh.shape["ctx"]
    group, depth = x.shape
    cols = vm.shape[1]
    tokens = group // ctx
    blocks = group // BLOCK
    x = x.reshape(blocks, BLOCK, depth)
    pairs = blocks // 2
    half = ctx // 2
    lines = fsdp // 2
    side = math.isqrt(lines)
    shard = depth // fsdp
    s_wo, s_gu, s_wd = sums
    shapes = (
        (s_wo.shape[1], s_wo.shape[2] // ctx),
        (s_gu.shape[2], s_gu.shape[3]),
        (s_wd.shape[1], s_wd.shape[2] // ctx),
    )
    anywhere = pl.BlockSpec(memory_space=pl.ANY)
    vmem = pl.BlockSpec(memory_space=pltpu.VMEM)
    dma = pltpu.SemaphoreType.DMA
    hops = max(side - 1, 1)

    def low(*shape):
        return pltpu.VMEM(shape, BF16)

    def full(*shape):
        return pltpu.VMEM(shape, F32)

    return pl.pallas_call(
        functools.partial(backward_kernel, fsdp, ctx),
        out_shape=(
            jax.ShapeDtypeStruct((tokens, depth), BF16),
            jax.ShapeDtypeStruct((tokens, depth), BF16),
            jax.ShapeDtypeStruct(shapes[0], F32),
            jax.ShapeDtypeStruct(shapes[1], F32),
            jax.ShapeDtypeStruct(shapes[2], F32),
            jax.ShapeDtypeStruct((shard, 3 * cols), F32),
            jax.ShapeDtypeStruct((8, depth), F32),
        ),
        in_specs=[anywhere] * 7 + [vmem, anywhere, vmem] + [anywhere] + [vmem] * 2 + [anywhere] * 3,
        out_specs=[anywhere] * 2 + [vmem] * 5,
        scratch_shapes=[
            low(blocks, BLOCK, depth), low(group, cols), low(group, cols), low(group, cols),
            low(cols, group), full(group, cols), low(ctx, tokens, cols), low(depth, 3 * cols),
            full(group, table.shape[1]),
            full(cols, group), full(group, cols), full(group, cols),
            full(8, group), low(group, 3 * cols), full(depth, 3 * cols), low(lines, 2, shard, 3 * cols),
            low(pairs, BLOCK, depth), low(pairs + 1, BLOCK, depth),
            low(max(lines - 1, 1), 2, shard, 3 * cols), low(2, shard, 3 * cols),
            low(2, shard, 3 * cols),
            full(8, depth), full(fsdp, 8, depth), full(8, depth), full(ctx, 8, depth),
        ]
        + [low(ctx, side, *shape) for shape in shapes]
        + [low(ctx, hops, side, *shape) for shape in shapes]
        + [low(ctx, hops, *shape) for shape in shapes]
        + [low(ctx, *shape) for shape in shapes]
        + [
            dma((8,)), dma((ctx,)), dma((ctx,)), dma((ctx,)), dma((ctx,)),
            dma((pairs,)), dma((pairs,)), dma((pairs + 1,)), dma((2, pairs)),
            dma((tokens // BLOCK,)), dma((pairs,)),
            dma((lines,)), dma((lines,)), dma((2,)), dma((2,)),
            dma((fsdp,)), dma((fsdp,)), dma((ctx,)), dma((ctx,)),
            dma((3, ctx, side)), dma((3, ctx, hops, side)), dma((3, ctx, hops, side)),
            dma((3, ctx, hops)), dma((3, ctx, hops)), dma((3, ctx)), dma((3, ctx)),
        ],
        compiler_params=pltpu.CompilerParams(
            collective_id=3, has_side_effects=True, vmem_limit_bytes=BACKWARD_LIMIT
        ),
        name="backward",
    )(d_out, x, q, k, vm, kt, att, lse, wqkv, gain, table, start, dg_two, *sums)


def documents(length_row, places):
    doc_ends = jnp.cumsum(length_row)
    doc_starts = doc_ends - length_row
    owner_ids = jnp.sum((places[:, None] >= doc_ends[None, :]).astype(jnp.int32), axis=1)
    chosen = owner_ids[:, None] == jnp.arange(length_row.shape[0], dtype=jnp.int32)[None, :]
    first_place = jnp.sum(jnp.where(chosen, doc_starts[None, :], 0), axis=1)
    return first_place


def tables(length_row, group):
    places = jnp.arange(group, dtype=jnp.int32)
    first = documents(length_row, places)
    half = HEAD // 2
    frequency = jnp.exp(jnp.arange(half).astype(F32) * (-2.0 * math.log(THETA) / HEAD))
    angles = (places - first).astype(F32)[:, None] * frequency[None, :]
    cos, sin = jnp.cos(angles), jnp.sin(angles)
    return jnp.concatenate([cos, cos, -sin, sin], axis=1), first[None, :]


def layer(
    mesh, tokens, value_first, lengths, w_query, w_key, w_value, w_out, w_gate, w_up, w_down,
    gain_attn, gain_ffn, out_grad, value_grad,
):
    fsdp, ctx = mesh.shape["fsdp"], mesh.shape["ctx"]
    count, depth = tokens.shape
    group = count * ctx
    cols = depth // ctx
    rows = depth // fsdp
    f, c = lax.axis_index("fsdp"), lax.axis_index("ctx")
    core = lax.rem(f, 2)
    home = c // (ctx // 2)

    wqkv = jnp.concatenate([w_query, w_key, w_value], axis=1).astype(BF16)
    gu = jnp.concatenate([w_gate, w_up], axis=1).astype(BF16)
    gains = jnp.stack([gain_attn, gain_ffn]).astype(BF16).astype(F32)
    gains = lax.dynamic_update_slice(
        jnp.zeros((8, depth), F32), gains, (jnp.int32(0), (f * rows).astype(jnp.int32))
    )
    other_lengths = lax.ppermute(lengths, "fsdp", [(i, i ^ 1) for i in range(fsdp)])
    length_row = jnp.where(core == home, lengths, other_lengths)[0]
    table, first = tables(length_row, group)

    xs, vs, wq, _, wos, gus, wds, gs = gather(
        mesh, tokens, value_first, wqkv, w_out.astype(BF16), gu, w_down.astype(BF16), gains
    )
    gain_full = jnp.sum(gs, axis=0)
    gain_one, gain_two = gain_full[0:1], gain_full[1:2]
    xg = xs.reshape(group, depth)
    wq = wq.reshape(depth, 3 * cols)
    _, q, k, vm, kt, out, att, lse = forward_attention(
        xg, vs.reshape(group, cols), wq, gain_one, table, first
    )
    attended = trade(mesh, out.reshape(ctx, count, cols), True, 1)
    result, dx2, d_out, dg_two, s_wo, s_gu, s_wd = feed_forward(
        mesh, attended, tokens, out_grad, wos.reshape(depth, depth), gain_two,
        gus.reshape(ctx, depth, gu.shape[1]), wds.reshape(-1, depth),
    )
    folded, dvr, g_wo, g_gu, g_wd, g_qkv, gain_grads = backward(
        mesh, d_out, xg, q, k, vm, kt, att, lse, wq, gain_one, table, first, dg_two,
        (s_wo, s_gu, s_wd),
    )
    gain_grads = lax.dynamic_slice(
        gain_grads, (jnp.int32(0), (f * rows).astype(jnp.int32)), (2, rows)
    )
    ff = w_gate.shape[1]
    return (
        result,
        dx2 + folded.astype(F32),
        value_grad + dvr.astype(F32),
        g_qkv[:, :cols],
        g_qkv[:, cols : 2 * cols],
        g_qkv[:, 2 * cols :],
        g_wo,
        g_gu[:, :ff],
        g_gu[:, ff:],
        g_wd,
        gain_grads[0],
        gain_grads[1],
    )


def solution(mesh):
    rows = P(("fsdp", "ctx"), None)
    shard = P("fsdp", "ctx")
    return jax.shard_map(
        functools.partial(layer, mesh),
        mesh=mesh,
        in_specs=(rows, rows, P("fsdp", None)) + (shard,) * 7 + (P("fsdp"),) * 2 + (rows, rows),
        out_specs=(rows, rows, rows) + (shard,) * 7 + (P("fsdp"),) * 2,
        check_vma=False,
    )
```

```python
import functools
import math

import jax
import jax.numpy as jnp
from jax import lax
from jax.experimental import pallas as pl
from jax.experimental.pallas import tpu as pltpu
from jax.sharding import PartitionSpec as P

HEAD = 64
EPSILON = 1e-05
THETA = 10000.0
NEGATIVE = -1e30
BLOCK = 256
VMEM_LIMIT = 58 * 1024 * 1024
BACKWARD_LIMIT = 58 * 1024 * 1024
MESH = pl.DeviceIdType.MESH
BF16 = jnp.bfloat16
F32 = jnp.float32


def nn(left, right):
    return lax.dot_general(left, right, (((1,), (0,)), ((), ())), preferred_element_type=F32)


def nt(left, right):
    return lax.dot_general(left, right, (((1,), (1,)), ((), ())), preferred_element_type=F32)


def tn(left, right):
    return lax.dot_general(left, right, (((0,), (0,)), ((), ())), preferred_element_type=F32)


def turns(table, width):
    lane = lax.broadcasted_iota(jnp.int32, table.shape, 1)
    swapped = pltpu.roll(table, HEAD, 1)
    cos = jnp.where(lane < HEAD, table, swapped)
    sin = jnp.where(lane < HEAD, swapped, table)
    times = width // table.shape[1]
    return jnp.concatenate([cos] * times, axis=1), jnp.concatenate([sin] * times, axis=1)


def half_swap(rows):
    width = rows.shape[1]
    lane = lax.broadcasted_iota(jnp.int32, rows.shape, 1)
    low = lax.rem(lane, HEAD) < HEAD // 2
    return jnp.where(
        low,
        pltpu.roll(rows, width - HEAD // 2, 1),
        pltpu.roll(rows, HEAD // 2, 1),
    )


def head_lanes(shape, head):
    lane = lax.broadcasted_iota(jnp.int32, shape, 1)
    return (lane >= head * HEAD) & (lane < (head + 1) * HEAD)


class Plan:
    def __init__(self, fsdp, ctx):
        self.fsdp, self.ctx = fsdp, ctx
        self.lines = fsdp // 2
        self.across = math.isqrt(self.lines)
        self.along = self.lines // self.across
        self.half = ctx // 2
        self.f = lax.axis_index("fsdp")
        self.c = lax.axis_index("ctx")
        self.core = lax.rem(self.f, 2)
        self.line = self.f // 2
        self.a = self.line // self.along
        self.b = lax.rem(self.line, self.along)
        self.home = self.c // self.half
        self.started = []
        self.draining = False

    def barrier(self):
        sem = pltpu.get_barrier_semaphore()
        count = 0
        for step in range(1, self.fsdp):
            dev = (lax.rem(self.f + step, self.fsdp), self.c)
            pl.semaphore_signal(sem, inc=1, device_id=dev, device_id_type=MESH)
            count += 1
        for step in range(1, self.ctx):
            for core in range(2):
                dev = (self.line * 2 + core, lax.rem(self.c + step, self.ctx))
                pl.semaphore_signal(sem, inc=1, device_id=dev, device_id_type=MESH)
                count += 1
        pl.semaphore_wait(sem, count)

    def greet_plane(self):
        sem = pltpu.get_barrier_semaphore()
        for step in range(1, self.fsdp):
            dev = (lax.rem(self.f + step, self.fsdp), self.c)
            pl.semaphore_signal(sem, inc=1, device_id=dev, device_id_type=MESH)
        pl.semaphore_wait(sem, self.fsdp - 1)

    def when(self, cond, act):
        if cond is True:
            act()
        else:
            pl.when(cond)(act)

    def send(self, src, dst, send_sem, recv_sem, dev, cond=True):
        def copy():
            return pltpu.make_async_remote_copy(
                src_ref=src, dst_ref=dst, send_sem=send_sem, recv_sem=recv_sem,
                device_id=dev, device_id_type=MESH,
            )

        if self.draining:
            self.when(cond, lambda: copy().wait_send())
            return
        self.when(cond, lambda: copy().start())
        self.started.append((cond, lambda: copy().wait_send()))

    def keep(self, src, dst, sem, cond=True):
        if self.draining:
            return
        self.when(cond, lambda: pltpu.make_async_copy(src, dst, sem).start())

    def arrive(self, dst, sem, cond=True):
        if self.draining:
            return
        self.when(cond, lambda: pltpu.make_async_copy(dst, dst, sem).wait())

    def drain(self):
        for cond, act in self.started:
            self.when(cond, act)
        self.started = []


def both(*conds):
    out = True
    for cond in conds:
        if cond is not True:
            out = cond if out is True else jnp.logical_and(out, cond)
    return out


class Gathering:
    def __init__(self, plan, own, whole, sems):
        self.plan, self.own, self.whole = plan, own, whole
        self.sem, self.z_out, self.p_out, self.s_out = sems
        self.widths = (own[0].shape[1], None, own[2].shape[1])

    def spots(self, row, j):
        wos, gus, wds = self.whole

        def band(width):
            return pl.ds(pl.multiple_of(j * width, width), width)

        return (
            wos.at[row, :, band(self.widths[0])], gus.at[j, row], wds.at[row, :, band(self.widths[2])],
        )

    def along_ctx(self, srcs, j, cond, up, down, items=(0, 1, 2)):
        plan = self.plan
        dsts = self.spots(plan.f, j)
        for i in items:
            if up:
                plan.send(
                    srcs[i], dsts[i], self.z_out.at[i, 0, j], self.sem.at[i, plan.f, j],
                    (plan.f, plan.c + 1), both(cond, plan.c < plan.ctx - 1),
                )
            if down:
                plan.send(
                    srcs[i], dsts[i], self.z_out.at[i, 1, j], self.sem.at[i, plan.f, j],
                    (plan.f, plan.c - 1), both(cond, plan.c > 0),
                )

    def on_plane(self, srcs, row, line, j, cond, over_a, over_b, items=(0, 1, 2)):
        plan = self.plan
        dsts = self.spots(row, j)
        for i in items:
            if over_a is not False:
                for hop in range(1, plan.across):
                    to = (lax.rem(plan.a + hop, plan.across) * plan.along + plan.b) * 2 + plan.core
                    plan.send(
                        srcs[i], dsts[i], self.p_out.at[i, hop - 1, line, j],
                        self.sem.at[i, row, j], (to, plan.c), both(cond, over_a),
                    )
            if over_b is not False:
                for hop in range(1, plan.along):
                    to = (plan.a * plan.along + lax.rem(plan.b + hop, plan.along)) * 2 + plan.core
                    plan.send(
                        srcs[i], dsts[i], self.p_out.at[i, plan.across + hop - 2, line, j],
                        self.sem.at[i, row, j], (to, plan.c), both(cond, over_b),
                    )
            plan.send(
                srcs[i], dsts[i], self.s_out.at[i, line, j], self.sem.at[i, row, j],
                (plan.line * 2 + 1 - plan.core, plan.c), cond,
            )

    def near(self, dist):
        plan = self.plan
        for side in range(2 if dist else 1):
            j = plan.c - dist if side == 0 else plan.c + dist
            there = True if dist == 0 else (j >= 0 if side == 0 else j < plan.ctx)
            yield jnp.clip(j, 0, plan.ctx - 1), there, side

    def start_ctx(self):
        self.along_ctx(self.own, self.plan.c, True, True, True)

    def start_plane(self):
        plan = self.plan
        self.on_plane(self.own, plan.f, plan.line, plan.c, True, True, True)
        for src, dst, i in zip(self.own, self.spots(plan.f, plan.c), range(3)):
            plan.keep(src, dst, self.sem.at[i, plan.f, plan.c])

    def wait(self, row, j, cond=True, items=(0, 1, 2)):
        dsts = self.spots(row, j)
        for i in items:
            self.plan.arrive(dsts[i], self.sem.at[i, row, j], cond)
        return dsts

    def from_ctx(self, dist):
        plan = self.plan
        for j, there, side in self.near(dist):
            for i in ORDER:
                dsts = self.wait(plan.f, j, there, (i,))
                self.along_ctx(dsts, j, there, side == 0, side == 1, (i,))
                self.on_plane(dsts, plan.f, plan.line, j, there, True, True, (i,))

    def from_plane(self, dist):
        plan = self.plan
        for j, there, _ in self.near(dist):
            first = j < plan.half
            for hop in range(1, plan.across):
                line = lax.rem(plan.a + plan.across - hop, plan.across) * plan.along + plan.b
                row = line * 2 + plan.core
                for i in ORDER:
                    dsts = self.wait(row, j, there, (i,))
                    self.on_plane(dsts, row, line, j, there, False, first, (i,))
            for hop in range(1, plan.along):
                line = plan.a * plan.along + lax.rem(plan.b + plan.along - hop, plan.along)
                row = line * 2 + plan.core
                for i in ORDER:
                    dsts = self.wait(row, j, there, (i,))
                    self.on_plane(
                        dsts, row, line, j, there, jnp.logical_not(first), False, (i,)
                    )

    def from_far(self, dist):
        plan = self.plan
        for j, there, _ in self.near(dist):
            for hop in range(1, plan.across):
                for hop2 in range(1, plan.along):
                    line = lax.rem(plan.a + hop, plan.across) * plan.along + lax.rem(
                        plan.b + hop2, plan.along
                    )
                    row = line * 2 + plan.core
                    for i in ORDER:
                        dsts = self.wait(row, j, there, (i,))
                        self.on_plane(dsts, row, line, j, there, False, False, (i,))

    def finish(self):
        plan = self.plan
        self.wait(plan.f, plan.c)

        def other(line, carry):
            for j in range(plan.ctx):
                self.wait(line * 2 + 1 - plan.core, j)
            return carry

        lax.fori_loop(0, plan.lines, other, 0)


def forward_kernel(
    fsdp, ctx,
    x, vf, w_q, w_k, w_v, w_o, w_g, w_u, w_d, small,
    attended, wos, gus, wds, x_out_ref, q_ref, k_ref, vm_ref, kt_ref, att_ref, wq_ref,
    lse, table, start, gain,
    xs, vs, wq, wqh, own_q, own_o, own_g, own_d, gs, q, k, vm, kt, vt, att, out, acc, mx, tot,
    x_sem, x_out, v_sem, v_out, q_sem, q_out, h_sem, g_sem, g_out,
    w_sem, w_z, w_p, w_s, o_sem, o_out, save_sem,
):
    plan = Plan(fsdp, ctx)
    f, c, core, line, home, half = plan.f, plan.c, plan.core, plan.line, plan.home, plan.half
    tokens, depth = x.shape
    group = tokens * ctx
    cols = depth // ctx
    heads = cols // HEAD
    blocks = group // BLOCK
    per = tokens // BLOCK
    owner = core == home
    away = jnp.logical_not(owner)
    sibling = (line * 2 + 1 - core, c)

    own_o[...] = w_o[...].astype(BF16)
    own_g[...] = jnp.concatenate([w_g[...].astype(BF16), w_u[...].astype(BF16)], axis=1)
    own_d[...] = w_d[...].astype(BF16)
    own_q[...] = jnp.concatenate(
        [w_q[...].astype(BF16), w_k[...].astype(BF16), w_v[...].astype(BF16)], axis=1
    )
    plan.barrier()
    gathering = Gathering(
        plan, (own_o, own_g, own_d), (wos, gus, wds), (w_sem, w_z, w_p, w_s)
    )

    for hop in range(1, fsdp):
        plan.send(small, gs.at[f], g_out.at[hop - 1], g_sem.at[f], (lax.rem(f + hop, fsdp), c))
    plan.keep(small, gs.at[f], g_sem.at[f])
    plan.send(own_q, wqh, h_sem.at[0], h_sem.at[1], (f, lax.rem(c + half, ctx)))

    piece = tokens // PIECES

    def part_of(ref, i):
        return ref.at[pl.ds(i * piece, piece), :]

    def spread_x(src, j, i, below, above, cond):
        dst = part_of(xs.at[j], i)
        if below:
            plan.send(
                src, dst, x_out.at[0, j, i], x_sem.at[j, i], (f, c - 1),
                both(cond, c > home * half),
            )
        if above:
            plan.send(
                src, dst, x_out.at[1, j, i], x_sem.at[j, i], (f, c + 1),
                both(cond, c < home * half + half - 1),
            )
        plan.send(src, dst, x_out.at[2, j, i], x_sem.at[j, i], sibling, cond)

    entry = jnp.where(core == 0, half - 1, half)
    for i in range(PIECES):
        src = part_of(x, i)
        plan.send(
            src, part_of(xs.at[c], i), x_out.at[0, c, i], x_sem.at[c, i], (f, entry), away
        )
        spread_x(src, c, i, True, True, owner)
        plan.keep(src, part_of(xs.at[c], i), x_sem.at[c, i], owner)
    for at in range(plan.lines):
        plan.send(
            own_q, wq.at[f], q_out.at[0, at], q_sem.at[f], (at * 2, c),
            jnp.logical_not(f == at * 2),
        )
    plan.keep(own_q, wq.at[f], q_sem.at[f], core == 0)
    for i in range(half):
        for kk in range(2):
            to = core * half + i
            rank = lax.rem(to + kk * half, ctx)
            src = vf.at[:, pl.ds(pl.multiple_of(rank * cols, cols), cols)]
            mine = both(owner, c == to, core == kk)
            plan.send(
                src, vs.at[c], v_out.at[i, kk], v_sem.at[c], (line * 2 + kk, to),
                jnp.logical_not(mine),
            )
            plan.keep(src, vs.at[c], v_sem.at[c], mine)
    gathering.start_plane()

    for row in range(fsdp):
        plan.arrive(gs.at[row], g_sem.at[row])
    total = gs[0]
    for row in range(1, fsdp):
        total = total + gs[row]
    gain[...] = total
    lens = gs[line * 2 + home]
    doc_count = SHORTS_AND_LONG

    def firsts(places):
        end = jnp.zeros((1, 1), F32)
        first = jnp.zeros(places.shape, F32)
        for d in range(doc_count):
            size = lens[2:3, d : d + 1]
            end = end + size
            first = first + jnp.where(places >= end, size, 0.0)
        return first

    places = lax.broadcasted_iota(jnp.int32, (1, group), 1).astype(F32)
    start[...] = firsts(places).astype(jnp.int32)

    def angles(b, carry):
        rows = pl.ds(pl.multiple_of(b * BLOCK, BLOCK), BLOCK)
        at = (b * BLOCK + lax.broadcasted_iota(jnp.int32, (BLOCK, 128), 0)).astype(F32)
        lane = lax.broadcasted_iota(jnp.int32, (BLOCK, 128), 1)
        pair = lax.rem(lane, HEAD // 2).astype(F32)
        angle = (at - firsts(at)) * jnp.exp(pair * (-2.0 * math.log(THETA) / HEAD))
        sine = jnp.sin(angle)
        table[rows, :] = jnp.where(
            lane < HEAD, jnp.cos(angle), jnp.where(lane < HEAD + HEAD // 2, -sine, sine)
        )
        return carry

    lax.fori_loop(0, blocks, angles, 0)

    plan.arrive(wqh, h_sem.at[1])
    for at in range(plan.lines):
        plan.send(
            wqh, wq.at[f], q_out.at[1, at], q_sem.at[f], (at * 2 + 1, c),
            jnp.logical_not(f == at * 2 + 1),
        )
    plan.keep(wqh, wq.at[f], q_sem.at[f], core == 1)

    def project(j):
        def body(i, carry):
            rows = pl.ds(pl.multiple_of(j * tokens + i * BLOCK, BLOCK), BLOCK)
            xv = xs[j, pl.ds(pl.multiple_of(i * BLOCK, BLOCK), BLOCK), :].astype(F32)
            rstd = lax.rsqrt(jnp.mean(xv * xv, axis=1, keepdims=True) + EPSILON)
            hv = (xv * rstd * gain[0:1, :]).astype(BF16)
            raw = nn(hv, wq[...].reshape(depth, 3 * cols))
            cos_v, sin_v = turns(table[rows, :], cols)
            rq = raw[:, :cols]
            rk = raw[:, cols : 2 * cols]
            qv = (rq * cos_v + half_swap(rq) * sin_v).astype(BF16)
            q[rows, :] = (qv.astype(F32) * (1.0 / math.sqrt(HEAD))).astype(BF16)
            kv = (rk * cos_v + half_swap(rk) * sin_v).astype(BF16)
            k[rows, :] = kv
            kt[:, rows] = kv.T
            att[rows, :] = 0.5 * raw[:, 2 * cols :]
            return carry

        lax.fori_loop(0, per, body, 0)

    def actions(place):
        out = [gathering.start_ctx] if place == START else []
        for kind in ("from_ctx", "from_plane", "from_far"):
            for dist in range(ctx):
                if (kind, dist) != ("from_ctx", 0) and place == spot_of(kind, dist, ctx, blocks):
                    out.append(functools.partial(getattr(gathering, kind), dist))
        return out

    for dist in range(ctx):
        for i in range(PIECES):
            for j, there, side in gathering.near(dist):
                spot = part_of(xs.at[j], i)
                plan.arrive(spot, x_sem.at[j, i], there)
                if dist:
                    spread_x(spot, j, i, side == 1, side == 0, both(owner, there))
        for act in actions(("x", dist)):
            act()
    for row in range(fsdp):
        plan.arrive(wq.at[row], q_sem.at[row])
    for act in actions("q"):
        act()
    for j in range(ctx):
        project(j)
    for act in actions("p"):
        act()
    saves = [(xs, x_out_ref), (q, q_ref), (k, k_ref), (kt, kt_ref), (wq, wq_ref)]
    for i, (src, dst) in enumerate(saves):
        plan.keep(src, dst, save_sem.at[i])
    for j in range(ctx):
        plan.arrive(vs.at[j], v_sem.at[j])

    def mix(b, carry):
        rows = pl.ds(pl.multiple_of(b * BLOCK, BLOCK), BLOCK)
        first = vs[b // per, pl.ds(pl.multiple_of(lax.rem(b, per) * BLOCK, BLOCK), BLOCK), :]
        mixed = (att[rows, :] + 0.5 * first.astype(F32)).astype(BF16)
        vm[rows, :] = mixed
        vt[:, rows] = mixed.T
        return carry

    lax.fori_loop(0, blocks, mix, 0)
    plan.keep(vm, vm_ref, save_sem.at[5])

    rank = lax.rem(c + core * half, ctx)

    def give(b):
        j = b // per
        where = lax.rem(b, per)
        src = out.at[pl.ds(pl.multiple_of(b * BLOCK, BLOCK), BLOCK), :]
        dst = attended.at[
            pl.ds(pl.multiple_of(where * BLOCK, BLOCK), BLOCK),
            pl.ds(pl.multiple_of(rank * cols, cols), cols),
        ]
        mine = both(owner, c == j)
        plan.send(
            src, dst, o_out.at[b], o_sem.at[rank, where], (line * 2 + home, j),
            jnp.logical_not(mine),
        )
        plan.keep(src, dst, o_sem.at[rank, where], mine)

    schedule = {}

    def at_step(t, act):
        schedule.setdefault(min(t, blocks - 1), []).append(act)

    for place in range(blocks):
        for act in actions(("t", place)):
            at_step(place, act)

    def unit(t, carry):
        b = blocks - 1 - t
        rows = pl.ds(pl.multiple_of(b * BLOCK, BLOCK), BLOCK)
        acc[...] = jnp.zeros_like(acc)
        mx[...] = jnp.full_like(mx, NEGATIVE)
        tot[...] = jnp.zeros_like(tot)
        qv = q[rows, :]
        first = start[0:1, rows]

        def keys(kb, inner):
            krows = pl.ds(pl.multiple_of(kb * BLOCK, BLOCK), BLOCK)
            kv = k[krows, :]
            key_pos = kb * BLOCK + lax.broadcasted_iota(jnp.int32, (BLOCK, BLOCK), 0)
            query_pos = b * BLOCK + lax.broadcasted_iota(jnp.int32, (BLOCK, BLOCK), 1)
            allowed = (key_pos <= query_pos) & (key_pos >= first)
            for head in range(heads):
                band = slice(head * HEAD, (head + 1) * HEAD)
                qm = jnp.where(head_lanes(qv.shape, head), qv, jnp.zeros_like(qv))
                s = jnp.where(allowed, nt(kv, qm), NEGATIVE)
                old = mx[head : head + 1, :]
                new = jnp.maximum(old, jnp.max(s, axis=0, keepdims=True))
                p = jnp.exp(s - new)
                shrink = jnp.exp(old - new)
                mx[head : head + 1, :] = new
                tot[head : head + 1, :] = tot[head : head + 1, :] * shrink + jnp.sum(
                    p, axis=0, keepdims=True
                )
                acc[band, :] = acc[band, :] * shrink + nn(vt[band, krows], p.astype(BF16))
            return inner

        lax.fori_loop(0, b + 1, keys, 0)
        for head in range(heads):
            band = slice(head * HEAD, (head + 1) * HEAD)
            acc[band, :] = acc[band, :] / tot[head : head + 1, :]
        ov = acc[...].T
        att[rows, :] = ov
        out[rows, :] = ov.astype(BF16)
        lse[:, rows] = mx[...] + jnp.log(tot[...])
        give(b)
        for s in sorted(schedule):

            @pl.when(t == s)
            def _(s=s):
                for act in schedule[s]:
                    act()

        return carry

    kept = plan.started
    plan.started = []
    lax.fori_loop(0, blocks, unit, 0)
    plan.started = kept
    plan.keep(att, att_ref, save_sem.at[6])
    for act in actions("late"):
        act()
    gathering.finish()
    for at in range(ctx):
        for where in range(per):
            plan.arrive(
                attended.at[pl.ds(where * BLOCK, BLOCK), pl.ds(at * cols, cols)],
                o_sem.at[at, where],
            )
    for i, (src, dst) in enumerate(saves + [(vm, vm_ref), (att, att_ref)]):
        plan.arrive(dst, save_sem.at[i])
    plan.drain()
    plan.draining = True
    for b in range(blocks):
        give(b)
    for s in sorted(schedule):
        for act in schedule[s]:
            act()


ORDER = (0, 1, 2)
PIECES = 4
START = ('x', 0)
SHORTS_AND_LONG = 4
SPOTS = {
    "from_ctx": (None, ('x', 2), ('x', 3), 'q'),
    "from_plane": (('x', 2), ('x', 3), 'p', ('t', 2)),
    "from_far": (('t', 0), ('t', 2), ('t', 4), 'late'),
}


def spot_of(kind, dist, ctx, blocks):
    if dist >= 4:
        return "p" if kind == "from_ctx" else "late"
    spot = SPOTS[kind][dist]
    return ("t", spot[1] * (blocks // 8)) if spot[0] == "t" else spot


def forward(mesh, x, vf, weights, small):
    fsdp, ctx = mesh.shape["fsdp"], mesh.shape["ctx"]
    tokens, depth = x.shape
    cols = depth // ctx
    group = tokens * ctx
    blocks = group // BLOCK
    per = tokens // BLOCK
    lines = fsdp // 2
    across = math.isqrt(lines)
    peers = max(across - 1 + lines // across - 1, 1)
    shard = depth // fsdp
    out_shape = weights[3].shape
    up_shape = (weights[4].shape[0], 2 * weights[4].shape[1])
    down_shape = weights[6].shape
    anywhere = pl.BlockSpec(memory_space=pl.ANY)
    vmem = pl.BlockSpec(memory_space=pltpu.VMEM)
    dma = pltpu.SemaphoreType.DMA

    def low(*shape):
        return pltpu.VMEM(shape, BF16)

    def full(*shape):
        return pltpu.VMEM(shape, F32)

    def array(dtype, *shape):
        return jax.ShapeDtypeStruct(shape, dtype)

    return pl.pallas_call(
        functools.partial(forward_kernel, fsdp, ctx),
        out_shape=(
            array(BF16, tokens, depth),
            array(BF16, fsdp, out_shape[0], depth),
            array(BF16, ctx, fsdp, *up_shape),
            array(BF16, fsdp, down_shape[0], depth),
            array(BF16, ctx, tokens, depth),
            array(BF16, group, cols),
            array(BF16, group, cols),
            array(BF16, group, cols),
            array(BF16, cols, group),
            array(F32, group, cols),
            array(BF16, fsdp, shard, 3 * cols),
            array(F32, 8, group),
            array(F32, group, 128),
            array(jnp.int32, 1, group),
            array(F32, 8, depth),
        ),
        in_specs=[anywhere] * 2 + [vmem] * 8,
        out_specs=[anywhere] * 11 + [vmem] * 4,
        scratch_shapes=[
            low(ctx, tokens, depth), low(ctx, tokens, cols), low(fsdp, shard, 3 * cols),
            low(shard, 3 * cols), low(shard, 3 * cols), low(*out_shape), low(*up_shape),
            low(*down_shape), full(fsdp, 8, depth),
            low(group, cols), low(group, cols), low(group, cols), low(cols, group),
            low(cols, group), full(group, cols), low(group, cols),
            full(cols, BLOCK), full(8, BLOCK), full(8, BLOCK),
            dma((ctx, PIECES)), dma((3, ctx, PIECES)), dma((ctx,)), dma((ctx // 2, 2)),
            dma((fsdp,)), dma((2, lines)), dma((2,)), dma((fsdp,)), dma((fsdp,)),
            dma((3, fsdp, ctx)), dma((3, 2, ctx)), dma((3, peers, lines, ctx)), dma((3, lines, ctx)),
            dma((ctx, per)), dma((blocks,)), dma((7,)),
        ],
        compiler_params=pltpu.CompilerParams(
            collective_id=0, has_side_effects=True, vmem_limit_bytes=VMEM_LIMIT
        ),
        name="forward",
    )(x, vf, *weights, small)


def chunk_order(i, ctx):
    return i % 2 * (ctx // 2) + i // 2


def reduce_line(plan, low, first, second):
    return second * plan.along + first if low else first * plan.along + second


def reduce_places(plan, j):
    low = j < plan.half
    return (low, plan.b if low else plan.a, plan.a if low else plan.b)


def feed_kernel(
    fsdp, ctx,
    o, x, dy, wo, gain, gu, wd,
    out, dx2, do, dg, s_wo, s_gu, s_wd, early,
    x2, h2, h2t, total, act, dgu,
    my_gu, my_wd, my_wo, got_gu, got_wd, got_wo, near_gu,
    gu_sem, gu_out, wd_sem, wd_out, wo_sem, wo_out, near_sem, near_out,
):
    plan = Plan(fsdp, ctx)
    core = plan.core
    sibling = (plan.line * 2 + 1 - core, plan.c)
    step = pl.program_id(0)
    last = pl.num_programs(0) - 1
    tokens, depth = x.shape
    chunk = wd.shape[0]
    blocks = tokens // BLOCK
    lines = plan.lines
    shard = depth // fsdp
    row_lines = my_wd.shape[1]
    row_count = my_wd.shape[3]
    slot = lax.rem(step, 2)
    half, side = plan.half, plan.across

    def give(at):
        place = lax.rem(at, 2)
        for i in range(lines):
            plan.send(
                my_gu.at[place, i, 1 - core], got_gu.at[at, i], gu_out.at[place, i],
                gu_sem.at[at, i], sibling,
            )
        for i in range(row_lines):
            plan.send(
                my_wd.at[place, i, 1 - core], got_wd.at[at, i], wd_out.at[place, i],
                wd_sem.at[at, i], sibling,
            )

    def given(at):
        plan.draining = True
        give(at)
        plan.draining = False

    @pl.when(step == 0)
    def _():
        plan.greet_plane()

        def rows_of(b, carry):
            rows = pl.ds(pl.multiple_of(b * BLOCK, BLOCK), BLOCK)
            mid = x[rows, :].astype(F32) + nn(o[rows, :], wo[...])
            x2[rows, :] = mid
            rstd = lax.rsqrt(jnp.mean(mid * mid, axis=1, keepdims=True) + EPSILON)
            hv = (mid * rstd * gain[...]).astype(BF16)
            h2[rows, :] = hv
            h2t[:, rows] = hv.T
            total[rows, :] = mid
            dx2[rows, :] = jnp.zeros((BLOCK, depth), F32)
            return carry

        lax.fori_loop(0, blocks, rows_of, 0)

    @pl.when(jnp.logical_and(step >= 2, step < last))
    def _():
        given(step - 2)

    @pl.when(step < last)
    def _():
        def rows_of(b, carry):
            rows = pl.ds(pl.multiple_of(b * BLOCK, BLOCK), BLOCK)
            both_ = nn(h2[rows, :], gu[0])
            gate = both_[:, :chunk]
            up = both_[:, chunk:]
            da = nt(dy[rows, :], wd[...]).astype(BF16).astype(F32)
            sig = 1.0 / (1.0 + jnp.exp(-gate))
            silu = gate * sig
            av = (silu * up).astype(BF16)
            act[rows, :] = av
            dgate = (da * up * (sig * (1.0 + gate * (1.0 - sig)))).astype(BF16)
            dup = (da * silu).astype(BF16)
            dv = jnp.concatenate([dgate, dup], axis=1)
            dgu[rows, :] = dv
            total[rows, :] = total[rows, :] + nn(av, wd[...])
            dx2[rows, :] = dx2[rows, :] + nt(dv, gu[0])
            return carry

        lax.fori_loop(0, blocks, rows_of, 0)

        for part in range(depth // 512):
            at = slice(part * 512, (part + 1) * 512)
            val = tn(act[...], dy[:, at])
            for r in range(row_lines * 2):
                my_wd[slot, r // 2, r % 2, :, at] = val[
                    r * row_count : (r + 1) * row_count
                ].astype(BF16)

        rows_each = BLOCK // shard

        def weight(b, carry):
            rows = pl.ds(pl.multiple_of(b * BLOCK, BLOCK), BLOCK)
            val = nn(h2t[rows, :], dgu[...]).astype(BF16)
            for r in range(rows_each):
                my_gu[slot, b * (rows_each // 2) + r // 2, r % 2] = val[
                    r * shard : (r + 1) * shard
                ]
            return carry

        lax.fori_loop(0, depth // BLOCK, weight, 0)
        give(step)

    def over_plane(at):
        j = chunk_order(at, ctx)
        low, first, second = reduce_places(plan, j)
        for hop in range(1, side):
            to = lax.rem(first + hop, side)
            dev = (reduce_line(plan, low, to, second) * 2 + core, plan.c)
            for inner in range(side):
                plan.send(
                    got_gu.at[at, reduce_line(plan, low, to, inner)],
                    near_gu.at[at, hop - 1, inner], near_out.at[at, hop - 1, inner],
                    near_sem.at[at, hop - 1, inner], dev,
                )

    def collect(at):
        place = lax.rem(at, 2)
        for i in range(lines):
            plan.arrive(got_gu.at[at, i], gu_sem.at[at, i])

            @pl.when(at >= half)
            def _(i=i):
                add_rows(s_gu.at[0, i], [my_gu.at[place, i, core], got_gu.at[at, i]])

            @pl.when(at < half)
            def _(i=i):
                add_rows(got_gu.at[at, i], [my_gu.at[place, i, core], got_gu.at[at, i]])

        for early_at in range(half):

            @pl.when(at == early_at)
            def _(early_at=early_at):
                over_plane(early_at)

        for i in range(row_lines):
            plan.arrive(got_wd.at[at, i], wd_sem.at[at, i])
            add_rows(s_wd.at[i], [my_wd.at[place, i, core], got_wd.at[at, i]])

    @pl.when(jnp.logical_and(step >= 1, step < last))
    def _():
        collect(step - 1)

    @pl.when(step == last)
    def _():
        dg[...] = jnp.zeros_like(dg)

        def rows_of(b, carry):
            rows = pl.ds(pl.multiple_of(b * BLOCK, BLOCK), BLOCK)
            out[rows, :] = total[rows, :].astype(BF16)
            mid = x2[rows, :]
            rstd = lax.rsqrt(jnp.mean(mid * mid, axis=1, keepdims=True) + EPSILON)
            xhat = mid * rstd
            dh = dx2[rows, :]
            u = dh * gain[...]
            dm = dy[rows, :].astype(F32) + rstd * (
                u - xhat * jnp.mean(u * xhat, axis=1, keepdims=True)
            )
            dx2[rows, :] = dm
            dg[0:1, :] = dg[0:1, :] + jnp.sum(dh * xhat, axis=0, keepdims=True)
            h2[rows, :] = dm.astype(BF16)
            return carry

        lax.fori_loop(0, blocks, rows_of, 0)
        rows_each = BLOCK // shard

        def weight_out(b, carry):
            at = pl.ds(pl.multiple_of(b * BLOCK, BLOCK), BLOCK)
            val = tn(o[:, at], h2[...]).astype(BF16)
            for r in range(rows_each):
                my_wo[b * (rows_each // 2) + r // 2, r % 2] = val[r * shard : (r + 1) * shard]
            return carry

        lax.fori_loop(0, depth // BLOCK, weight_out, 0)
        for i in range(lines):
            plan.send(my_wo.at[i, 1 - core], got_wo.at[i], wo_out.at[i], wo_sem.at[i], sibling)

        def rows_out(b, carry):
            rows = pl.ds(pl.multiple_of(b * BLOCK, BLOCK), BLOCK)
            do[rows, :] = nt(h2[rows, :], wo[...]).astype(BF16)
            return carry

        lax.fori_loop(0, blocks, rows_out, 0)
        collect(last - 1)
        for i in range(lines):
            plan.arrive(got_wo.at[i], wo_sem.at[i])
            add_rows(s_wo.at[i], [my_wo.at[i, core], got_wo.at[i]])
        for at in (last - 2, last - 1):
            given(at)
        for at in range(half):
            low, first, _ = reduce_places(plan, chunk_order(at, ctx))
            for inner in range(side):
                for hop in range(1, side):
                    plan.arrive(near_gu.at[at, hop - 1, inner], near_sem.at[at, hop - 1, inner])
                add_rows(
                    early.at[at, inner],
                    [got_gu.at[at, reduce_line(plan, low, first, inner)]]
                    + [near_gu.at[at, hop - 1, inner] for hop in range(1, side)],
                )
        plan.draining = True
        for at in range(half):
            over_plane(at)
        for i in range(lines):
            plan.send(my_wo.at[i, 1 - core], got_wo.at[i], wo_out.at[i], wo_sem.at[i], sibling)
        plan.draining = False


def feed_forward(mesh, o, x, dy, wo, gain, gu, wd):
    fsdp, ctx = mesh.shape["fsdp"], mesh.shape["ctx"]
    tokens, depth = x.shape
    steps, _, width = gu.shape
    chunk = width // 2
    lines = fsdp // 2
    shard = depth // fsdp
    row_count = wd.shape[0] // fsdp
    row_lines = fsdp // ctx // 2
    half = ctx // 2
    side = math.isqrt(lines)
    hops = max(side - 1, 1)
    once = pl.Buffered(1)

    def chunk_of(i):
        return chunk_order(jnp.minimum(i, steps - 1), ctx)

    def chunk_before(i):
        return chunk_order(jnp.maximum(i - 1, 0), ctx)

    def whole(shape):
        return pl.BlockSpec(shape, lambda i: (0,) * len(shape), pipeline_mode=once)

    def whole_out(shape):
        return pl.BlockSpec(shape, lambda i: (0,) * len(shape), pipeline_mode=once)

    shapes = (
        jax.ShapeDtypeStruct((tokens, depth), BF16),
        jax.ShapeDtypeStruct((tokens, depth), F32),
        jax.ShapeDtypeStruct((tokens, depth), BF16),
        jax.ShapeDtypeStruct((8, depth), F32),
        jax.ShapeDtypeStruct((lines, shard, depth), BF16),
        jax.ShapeDtypeStruct((ctx - half, lines, shard, width), BF16),
        jax.ShapeDtypeStruct((lines, row_count, depth), BF16),
        jax.ShapeDtypeStruct((half, side, shard, width), BF16),
    )
    dma = pltpu.SemaphoreType.DMA
    return pl.pallas_call(
        functools.partial(feed_kernel, fsdp, ctx),
        grid=(steps + 1,),
        out_shape=shapes,
        in_specs=[
            whole((tokens, depth)),
            whole((tokens, depth)),
            whole((tokens, depth)),
            whole((depth, depth)),
            whole((1, depth)),
            pl.BlockSpec((1, depth, width), lambda i: (chunk_of(i), 0, 0)),
            pl.BlockSpec((chunk, depth), lambda i: (chunk_of(i), 0)),
        ],
        out_specs=[
            whole_out((tokens, depth)),
            whole_out((tokens, depth)),
            whole_out((tokens, depth)),
            whole_out((8, depth)),
            whole_out((lines, shard, depth)),
            pl.BlockSpec(
                (1, lines, shard, width), lambda i: (jnp.maximum(i - 1 - half, 0), 0, 0, 0)
            ),
            pl.BlockSpec((row_lines, row_count, depth), lambda i: (chunk_before(i), 0, 0)),
            whole_out((half, side, shard, width)),
        ],
        scratch_shapes=[
            pltpu.VMEM((tokens, depth), F32),
            pltpu.VMEM((tokens, depth), BF16),
            pltpu.VMEM((depth, tokens), BF16),
            pltpu.VMEM((tokens, depth), F32),
            pltpu.VMEM((tokens, chunk), BF16),
            pltpu.VMEM((tokens, width), BF16),
            pltpu.VMEM((2, lines, 2, shard, width), BF16),
            pltpu.VMEM((2, row_lines, 2, row_count, depth), BF16),
            pltpu.VMEM((lines, 2, shard, depth), BF16),
            pltpu.VMEM((steps, lines, shard, width), BF16),
            pltpu.VMEM((steps, row_lines, row_count, depth), BF16),
            pltpu.VMEM((lines, shard, depth), BF16),
            pltpu.VMEM((half, hops, side, shard, width), BF16),
            dma((steps, lines)), dma((2, lines)), dma((steps, row_lines)), dma((2, row_lines)),
            dma((lines,)), dma((lines,)), dma((half, hops, side)), dma((half, hops, side)),
        ],
        compiler_params=pltpu.CompilerParams(
            vmem_limit_bytes=VMEM_LIMIT, dimension_semantics=("arbitrary",), collective_id=4,
            has_side_effects=True,
        ),
        name="feed_forward",
    )(o, x, dy, wo, gain, gu, wd)


def chunk_rows(count):
    return 32 if count % 32 == 0 else count


def add_rows(dst, parts):
    count = dst.shape[0]
    rows = chunk_rows(count)

    def body(t, carry):
        at = pl.ds(pl.multiple_of(t * rows, rows), rows)
        total = parts[0][at, :].astype(F32)
        for part in parts[1:]:
            total = total + part[at, :].astype(F32)
        dst[at, :] = total.astype(dst.dtype)
        return carry

    lax.fori_loop(0, count // rows, body, 0)


class Reduction:
    def __init__(self, plan, sources, early, own, near, next_, last, outs, sems):
        self.plan = plan
        self.sources, self.early, self.own, self.near, self.next, self.last, self.outs = (
            sources, early, own, near, next_, last, outs,
        )
        (
            self.own_sem, self.near_sem, self.near_out, self.next_sem, self.next_out,
            self.last_sem, self.last_out,
        ) = sems
        self.side = plan.across
        half, ctx = plan.half, plan.ctx
        self.chunks = [chunk_order(i, ctx) for i in range(ctx)]
        self.first_set = [(1, j) for j in self.chunks[:half]]
        self.second_set = [(1, j) for j in self.chunks[half:]]
        self.third_set = [(i, j) for i in (0, 2) for j in self.chunks]

    def piece(self, i, line, j):
        src = self.sources[i]
        if i == 1:
            return src.at[self.chunks.index(j) - self.plan.half, line]
        width = src.shape[2] // self.plan.ctx
        return src.at[line, :, pl.ds(j * width, width)]

    def send_next(self, i, j, source):
        plan = self.plan
        low, first, second = reduce_places(plan, j)
        for hop in range(1, self.side):
            to = lax.rem(second + hop, self.side)
            plan.send(
                source(to),
                self.next[i].at[j, hop - 1],
                self.next_out.at[i, j, hop - 1],
                self.next_sem.at[i, j, hop - 1],
                (reduce_line(plan, low, first, to) * 2 + plan.core, plan.c),
            )

    def start_early(self):
        plan = self.plan
        for at, (i, j) in enumerate(self.first_set):
            self.send_next(i, j, lambda to, at=at: self.early.at[at, to])
            for inner in range(self.side):
                plan.keep(
                    self.early.at[at, inner], self.own[i].at[j, inner], self.own_sem.at[i, j, inner]
                )

    def start(self, pairs):
        plan = self.plan
        for i, j in pairs:
            low, first, second = reduce_places(plan, j)
            for hop in range(1, self.side):
                to = lax.rem(first + hop, self.side)
                dev = (reduce_line(plan, low, to, second) * 2 + plan.core, plan.c)
                for inner in range(self.side):
                    plan.send(
                        self.piece(i, reduce_line(plan, low, to, inner), j),
                        self.near[i].at[j, hop - 1, inner],
                        self.near_out.at[i, j, hop - 1, inner],
                        self.near_sem.at[i, j, hop - 1, inner],
                        dev,
                    )
            for inner in range(self.side):
                plan.keep(
                    self.piece(i, reduce_line(plan, low, first, inner), j),
                    self.own[i].at[j, inner],
                    self.own_sem.at[i, j, inner],
                )

    def step_near(self, pairs):
        plan = self.plan
        for i, j in pairs:
            for inner in range(self.side):
                plan.arrive(self.own[i].at[j, inner], self.own_sem.at[i, j, inner])
                for hop in range(1, self.side):
                    plan.arrive(
                        self.near[i].at[j, hop - 1, inner], self.near_sem.at[i, j, hop - 1, inner]
                    )
                if not plan.draining:
                    add_rows(
                        self.own[i].at[j, inner],
                        [self.own[i].at[j, inner]]
                        + [self.near[i].at[j, hop - 1, inner] for hop in range(1, self.side)],
                    )
            self.send_next(i, j, lambda to, i=i, j=j: self.own[i].at[j, to])

    def step_next(self, pairs):
        plan = self.plan
        for i, j in pairs:
            _, _, second = reduce_places(plan, j)
            if (i, j) in self.first_set:
                for inner in range(self.side):
                    plan.arrive(self.own[i].at[j, inner], self.own_sem.at[i, j, inner])
            for hop in range(1, self.side):
                plan.arrive(self.next[i].at[j, hop - 1], self.next_sem.at[i, j, hop - 1])
            if not plan.draining:
                add_rows(
                    self.own[i].at[j, second],
                    [self.own[i].at[j, second]]
                    + [self.next[i].at[j, hop - 1] for hop in range(1, self.side)],
                )
            self.send_last(i, j, second, both(plan.c == 0, j > 0), both(plan.c == plan.ctx - 1, j < plan.ctx - 1))

    def send_last(self, i, j, second, up, down):
        plan = self.plan
        if up is not None:
            plan.send(
                self.own[i].at[j, second], self.last[i].at[j], self.last_out.at[i, j],
                self.last_sem.at[i, j], (plan.f, plan.c + 1), up,
            )
        if down is not None:
            slot = jnp.where(plan.c - 1 == j, plan.ctx, j)
            plan.send(
                self.own[i].at[j, second], self.last[i].at[slot], self.last_out.at[i, j],
                self.last_sem.at[i, slot], (plan.f, plan.c - 1), down,
            )

    def step_pass(self, pairs, hop):
        plan = self.plan
        for i, j in pairs:
            _, _, second = reduce_places(plan, j)
            up = both(plan.c == hop, plan.c < j) if hop < j else None
            down = both(plan.c == plan.ctx - 1 - hop, plan.c > j) if plan.ctx - 1 - hop > j else None
            for cond in (up, down):
                if cond is not None and not plan.draining:

                    @pl.when(cond)
                    def _(i=i, j=j, second=second):
                        plan.arrive(self.last[i].at[j], self.last_sem.at[i, j])
                        add_rows(
                            self.own[i].at[j, second],
                            [self.own[i].at[j, second], self.last[i].at[j]],
                        )

            self.send_last(i, j, second, up, down)

    def finish(self):
        plan = self.plan
        for i in range(3):
            count = self.outs[i].shape[0]
            rows = chunk_rows(count)
            slots = ((plan.c > 0, plan.c), (plan.c < plan.ctx - 1, plan.ctx))
            for there, slot in slots:
                plan.arrive(self.last[i].at[slot], self.last_sem.at[i, slot], there)

            def body(t, carry, i=i, rows=rows):
                at = pl.ds(pl.multiple_of(t * rows, rows), rows)
                for j in range(plan.ctx):
                    _, _, second = reduce_places(plan, j)

                    @pl.when(plan.c == j)
                    def _(j=j, second=second):
                        total = self.own[i][j, second, at, :].astype(F32)
                        if j > 0:
                            total = total + self.last[i][j, at, :].astype(F32)
                        if j < plan.ctx - 1:
                            total = total + self.last[i][plan.ctx, at, :].astype(F32)
                        self.outs[i][at, :] = total

                return carry

            lax.fori_loop(0, count // rows, body, 0)


def backward_kernel(
    fsdp, ctx,
    d_out, x_in, q_in, k_in, vm_in, kt_in, att_in, lse, wqkv_in, gain, table_in, start,
    dg_two, s_wo, s_gu, s_wd, early,
    folded, vout, g_wo, g_gu, g_wd, g_qkv, dg_all,
    part, q, k, vm, kt, att, do, wqkv, table,
    dqt, dkk, dvv, rows_t, d3, gw_full, gw,
    other, chain, gw_near, gw_sum, gw_last, dg, dg_near, dg_sum, dg_last,
    o_wo, o_gu, o_wd, n_wo, n_gu, n_wd, x_wo, x_gu, x_wd, l_wo, l_gu, l_wd,
    load_sem, do_sem, do_out, v_sem, v_out,
    sib_sem, sib_out, chain_sem, chain_out, end_sem, end_out,
    gw_sem, gw_out, gl_sem, gl_out, dn_sem, dn_out, dl_sem, dl_out,
    own_sem, near_sem, near_out, next_sem, next_out, last_sem, last_out,
):
    plan = Plan(fsdp, ctx)
    f, c, core, line, home, half = plan.f, plan.c, plan.core, plan.line, plan.home, plan.half
    lines = plan.lines
    sibling = (line * 2 + 1 - core, c)
    low, high = home * half, home * half + half - 1
    blocks, _, depth = part.shape
    group = blocks * BLOCK
    cols = vm.shape[1]
    heads = cols // HEAD
    tokens = group // ctx
    per = tokens // BLOCK
    pairs = blocks // 2
    plan.barrier()

    for i in range(half):
        for kk in range(2):
            to = core * half + i
            rank = lax.rem(to + kk * half, ctx)
            src = d_out.at[:, pl.ds(pl.multiple_of(rank * cols, cols), cols)]
            mine = both(core == home, c == to, core == kk)
            plan.send(
                src, do.at[c], do_out.at[i * 2 + kk], do_sem.at[c], (line * 2 + kk, to),
                jnp.logical_not(mine),
            )
            plan.keep(src, do.at[c], do_sem.at[c], mine)
    loads = (
        (q_in, q), (k_in, k), (vm_in, vm), (kt_in, kt), (att_in, att), (table_in, table),
        (wqkv_in, wqkv), (x_in, part),
    )
    for i, (src, dst) in enumerate(loads):
        plan.keep(src, dst, load_sem.at[i])
    reduction = Reduction(
        plan, (s_wo, s_gu, s_wd), early, (o_wo, o_gu, o_wd), (n_wo, n_gu, n_wd), (x_wo, x_gu, x_wd),
        (l_wo, l_gu, l_wd), (g_wo, g_gu, g_wd),
        (own_sem, near_sem, near_out, next_sem, next_out, last_sem, last_out),
    )
    reduction.start_early()
    reduction.start(reduction.second_set)
    reduction.start(reduction.third_set)

    dqt[...] = jnp.zeros_like(dqt)
    dkk[...] = jnp.zeros_like(dkk)
    dvv[...] = jnp.zeros_like(dvv)
    gw_full[...] = jnp.zeros_like(gw_full)
    dg[...] = jnp.zeros_like(dg)
    dg[1:2, :] = dg_two[0:1, :]
    for i, (src, dst) in enumerate(loads):
        plan.arrive(dst, load_sem.at[i])
    for j in range(ctx):
        plan.arrive(do.at[j], do_sem.at[j])

    def grads_of(b):
        return do[b // per, pl.ds(pl.multiple_of(lax.rem(b, per) * BLOCK, BLOCK), BLOCK), :]

    def dots(b, carry):
        rows = pl.ds(pl.multiple_of(b * BLOCK, BLOCK), BLOCK)
        prod = grads_of(b).astype(F32) * att[rows, :]
        upper = prod.astype(BF16)
        lower = (prod - upper.astype(F32)).astype(BF16)
        head_row = lax.broadcasted_iota(jnp.int32, (8, cols), 0)
        lane = lax.broadcasted_iota(jnp.int32, (8, cols), 1)
        choose = (lane // HEAD == head_row).astype(F32).astype(BF16)
        rows_t[:, rows] = nt(choose, upper) + nt(choose, lower)
        return carry

    lax.fori_loop(0, blocks, dots, 0)

    def tile(kb, qb):
        krows = pl.ds(pl.multiple_of(kb * BLOCK, BLOCK), BLOCK)
        rows = pl.ds(pl.multiple_of(qb * BLOCK, BLOCK), BLOCK)
        kv = k[krows, :]
        vv = vm[krows, :]
        qv = q[rows, :]
        dov = grads_of(qb)
        key_pos = kb * BLOCK + lax.broadcasted_iota(jnp.int32, (BLOCK, BLOCK), 0)
        query_pos = qb * BLOCK + lax.broadcasted_iota(jnp.int32, (BLOCK, BLOCK), 1)
        allowed = (key_pos <= query_pos) & (key_pos >= start[0:1, rows])
        dk_sum = dkk[krows, :]
        dv_sum = dvv[krows, :]
        for head in range(heads):
            band = slice(head * HEAD, (head + 1) * HEAD)
            lanes = head_lanes(qv.shape, head)
            qm = jnp.where(lanes, qv, jnp.zeros_like(qv))
            dom = jnp.where(lanes, dov, jnp.zeros_like(dov))
            s = jnp.where(allowed, nt(kv, qm), NEGATIVE)
            p = jnp.exp(s - lse[head : head + 1, rows])
            ds = (p * (nt(vv, dom) - rows_t[head : head + 1, rows])).astype(BF16)
            dv_sum = dv_sum + nn(p.astype(BF16), dom)
            dk_sum = dk_sum + nn(ds, qm)
            dqt[band, rows] = dqt[band, rows] + nn(kt[band, krows], ds)
        dkk[krows, :] = dk_sum
        dvv[krows, :] = dv_sum

    def unit_of(t):
        return jnp.where(home == 0, blocks - 1 - t, t)

    def finish(o):
        rows = pl.ds(pl.multiple_of(o * BLOCK, BLOCK), BLOCK)
        cos_v, sin_v = turns(table[rows, :], cols)
        dq = dqt[:, rows].T * (1.0 / math.sqrt(HEAD))
        d3[rows, :cols] = (dq * cos_v - half_swap(dq) * sin_v).astype(BF16)
        dk = dkk[rows, :]
        d3[rows, cols : 2 * cols] = (dk * cos_v - half_swap(dk) * sin_v).astype(BF16)
        d3[rows, 2 * cols :] = (0.5 * dvv[rows, :]).astype(BF16)
        dh = nt(d3[rows, :], wqkv[...])
        xv = part[o].astype(F32)
        rstd = lax.rsqrt(jnp.mean(xv * xv, axis=1, keepdims=True) + EPSILON)
        xhat = xv * rstd
        h1 = (xhat * gain[...]).astype(BF16)
        u = dh * gain[...]
        part[o] = (rstd * (u - xhat * jnp.mean(u * xhat, axis=1, keepdims=True))).astype(BF16)
        dg[0:1, :] = dg[0:1, :] + jnp.sum(dh * xhat, axis=0, keepdims=True)
        gw_full[...] = gw_full[...] + tn(h1, d3[rows, :])

    def give(t):
        o = unit_of(t)
        slot = t // 2
        plan.send(
            part.at[o], other.at[slot], sib_out.at[slot], sib_sem.at[slot], sibling,
            lax.rem(o, 2) != core,
        )

    def pair_unit(i):
        return jnp.where(home == 0, blocks - 2 - 2 * i, 2 * i) + core

    def add_unit(o, src):
        def body(t, carry):
            at = pl.ds(pl.multiple_of(t * 32, 32), 32)
            part[o, at, :] = (part[o, at, :].astype(F32) + src[at, :].astype(F32)).astype(BF16)
            return carry

        lax.fori_loop(0, BLOCK // 32, body, 0)

    def sum_pair(i):
        plan.arrive(other.at[i], sib_sem.at[i])
        if not plan.draining:
            add_unit(pair_unit(i), other.at[i])

    def pass_pair(i, hears):
        o = pair_unit(i)
        j = o // per
        top = jnp.minimum(j, high)
        bottom = jnp.maximum(j, low)
        from_below = both(c > low, c <= top)
        from_above = both(c < high, c >= bottom)
        now = jnp.logical_or(from_below, from_above) == hears
        spot = jnp.where(j == c, pairs, i)
        if hears and not plan.draining:

            @pl.when(from_below)
            def _():
                plan.arrive(chain.at[i], chain_sem.at[i])
                add_unit(o, chain.at[i])

            @pl.when(from_above)
            def _():
                plan.arrive(chain.at[spot], chain_sem.at[spot])
                add_unit(o, chain.at[spot])

        plan.send(
            part.at[o], chain.at[i], chain_out.at[0, i], chain_sem.at[i], (f, c + 1),
            both(now, c < top),
        )
        below = jnp.where(j == c - 1, pairs, i)
        plan.send(
            part.at[o], chain.at[below], chain_out.at[1, i], chain_sem.at[below], (f, c - 1),
            both(now, c > bottom),
        )
        end = jnp.clip(j, low, high)
        mine = both(c == end, j == c, core == home)
        where = lax.rem(o, per)
        dst = folded.at[pl.ds(pl.multiple_of(where * BLOCK, BLOCK), BLOCK), :]
        plan.send(
            part.at[o], dst, end_out.at[i], end_sem.at[where], (line * 2 + home, j),
            both(now, c == end, jnp.logical_not(mine)),
        )
        plan.keep(part.at[o], dst, end_sem.at[where], both(now, mine))

    rank = lax.rem(c + core * half, ctx)

    def give_values(i):
        j = jnp.where(home == 0, ctx - 1 - i, i)
        src = d3.at[pl.ds(pl.multiple_of(j * tokens, tokens), tokens), 2 * cols : 3 * cols]
        dst = vout.at[:, pl.ds(pl.multiple_of(rank * cols, cols), cols)]
        mine = both(core == home, c == j)
        plan.send(
            src, dst, v_out.at[i], v_sem.at[rank], (line * 2 + home, j), jnp.logical_not(mine)
        )
        plan.keep(src, dst, v_sem.at[rank], mine)

    schedule = {}
    schedule_last = []

    def at_step(t, act):
        schedule.setdefault(t, []).append(act)

    scale = blocks // 8
    for kind, which, place in REDUCE_STEPS:
        pairs_of = getattr(reduction, which)
        if kind != "step_pass":
            at_step(place * scale, functools.partial(getattr(reduction, kind), pairs_of))
            continue
        for hop in range(1, ctx - 1):
            act = functools.partial(reduction.step_pass, pairs_of, hop)
            when = place + PASS_GAP * (hop - 1)
            if when < 8 and hop < 3:
                at_step(when * scale, act)
            else:
                schedule_last.append(act)
    for i in range(pairs - 1):
        at_step(2 * i + 1, lambda i=i: give_values(i))
        at_step(2 * i + 2, lambda i=i: sum_pair(i))
        at_step(2 * i + 2, lambda i=i: pass_pair(i, False))
        if i < pairs - 2:
            at_step(2 * i + 4, lambda i=i: pass_pair(i, True))
    at_step(blocks - 1, lambda: give_values(pairs - 1))

    def step(t, carry):
        o = unit_of(t)

        def inner(i, carry2):
            tile(jnp.where(home == 0, i, o), jnp.where(home == 0, o, o + i))
            return carry2

        lax.fori_loop(0, blocks - t, inner, 0)
        finish(o)
        give(t)
        for s in sorted(schedule):

            @pl.when(t == s)
            def _(s=s):
                for act in schedule[s]:
                    act()

        return carry

    kept = plan.started
    plan.started = []
    lax.fori_loop(0, blocks, step, 0)
    plan.started = kept

    for hop in range(1, fsdp):
        dev = (lax.rem(f + hop, fsdp), c)
        plan.send(dg, dg_near.at[f], dn_out.at[hop - 1], dn_sem.at[f], dev)
    plan.keep(dg, dg_near.at[f], dn_sem.at[f])

    pass_pair(pairs - 2, True)
    sum_pair(pairs - 1)
    pass_pair(pairs - 1, False)
    shard = depth // fsdp
    rows_each = BLOCK // shard

    def weight(b, carry):
        at = pl.ds(pl.multiple_of(b * BLOCK, BLOCK), BLOCK)
        val = gw_full[at, :].astype(BF16)
        for r in range(rows_each):
            gw[b * (rows_each // 2) + r // 2, r % 2] = val[r * shard : (r + 1) * shard]
        return carry

    lax.fori_loop(0, depth // BLOCK, weight, 0)
    for i in range(3):
        for hop in range(1, lines):
            to = lax.rem(line + hop, lines)
            plan.send(
                gw.at[to, :, :, pl.ds(i * cols, cols)],
                gw_near.at[hop - 1, :, :, pl.ds(i * cols, cols)],
                gw_out.at[i, hop - 1], gw_sem.at[i, hop - 1], (to * 2 + core, c),
            )
    pass_pair(pairs - 1, True)

    for at in range(fsdp):
        plan.arrive(dg_near.at[at], dn_sem.at[at])
    total = dg_near[0]
    for at in range(1, fsdp):
        total = total + dg_near[at]
    dg_sum[...] = total
    for hop in range(1, ctx):
        plan.send(
            dg_sum, dg_last.at[c], dl_out.at[hop - 1], dl_sem.at[c], (f, lax.rem(c + hop, ctx))
        )
    plan.keep(dg_sum, dg_last.at[c], dl_sem.at[c])

    plane = jnp.where(core == 0, c, lax.rem(c + half, ctx))
    for i in range(3):
        band = pl.ds(i * cols, cols)
        for hop in range(1, lines):
            plan.arrive(gw_near.at[hop - 1, :, :, band], gw_sem.at[i, hop - 1])
        for kk in range(2):
            add_rows(
                gw_sum.at[kk, :, band],
                [gw.at[line, kk, :, band]]
                + [gw_near.at[hop - 1, kk, :, band] for hop in range(1, lines)],
            )
            mine = both(core == 0, kk == 0)
            src, dst = gw_sum.at[kk, :, band], gw_last.at[core, :, band]
            plan.send(
                src, dst, gl_out.at[kk, i], gl_sem.at[core, i], (line * 2 + kk, plane),
                jnp.logical_not(mine),
            )
            plan.keep(src, dst, gl_sem.at[core, i], mine)

    for act in schedule_last:
        act()
    reduction.finish()
    for at in range(ctx):
        plan.arrive(dg_last.at[at], dl_sem.at[at])
    total = dg_last[0]
    for at in range(1, ctx):
        total = total + dg_last[at]
    dg_all[...] = total
    for kk in range(2):
        for i in range(3):
            plan.arrive(gw_last.at[kk, :, pl.ds(i * cols, cols)], gl_sem.at[kk, i])
    add_rows(g_qkv, [gw_last.at[0], gw_last.at[1]])
    for at in range(per):
        plan.arrive(folded.at[pl.ds(at * BLOCK, BLOCK), :], end_sem.at[at])
    for at in range(ctx):
        plan.arrive(vout.at[:, pl.ds(at * cols, cols)], v_sem.at[at])
    plan.drain()
    plan.draining = True
    for t in range(blocks):
        give(t)
    for s in sorted(schedule):
        for act in schedule[s]:
            act()


PASS_GAP = 1
REDUCE_STEPS = (
    ("step_near", "second_set", 0),
    ("step_next", "first_set", 0),
    ("step_near", "third_set", 1),
    ("step_next", "second_set", 2),
    ("step_pass", "first_set", 2),
    ("step_next", "third_set", 3),
    ("step_pass", "second_set", 4),
    ("step_pass", "third_set", 6),
)


def backward(mesh, d_out, x, q, k, vm, kt, att, lse, wqkv, gain, table, start, dg_two, sums):
    fsdp, ctx = mesh.shape["fsdp"], mesh.shape["ctx"]
    group, depth = x.shape
    cols = vm.shape[1]
    tokens = group // ctx
    blocks = group // BLOCK
    x = x.reshape(blocks, BLOCK, depth)
    pairs = blocks // 2
    half = ctx // 2
    lines = fsdp // 2
    side = math.isqrt(lines)
    shard = depth // fsdp
    s_wo, s_gu, s_wd, _ = sums
    shapes = (
        (s_wo.shape[1], s_wo.shape[2] // ctx),
        (s_gu.shape[2], s_gu.shape[3]),
        (s_wd.shape[1], s_wd.shape[2] // ctx),
    )
    anywhere = pl.BlockSpec(memory_space=pl.ANY)
    vmem = pl.BlockSpec(memory_space=pltpu.VMEM)
    dma = pltpu.SemaphoreType.DMA
    hops = max(side - 1, 1)

    def low(*shape):
        return pltpu.VMEM(shape, BF16)

    def full(*shape):
        return pltpu.VMEM(shape, F32)

    return pl.pallas_call(
        functools.partial(backward_kernel, fsdp, ctx),
        out_shape=(
            jax.ShapeDtypeStruct((tokens, depth), BF16),
            jax.ShapeDtypeStruct((tokens, depth), BF16),
            jax.ShapeDtypeStruct(shapes[0], F32),
            jax.ShapeDtypeStruct(shapes[1], F32),
            jax.ShapeDtypeStruct(shapes[2], F32),
            jax.ShapeDtypeStruct((shard, 3 * cols), F32),
            jax.ShapeDtypeStruct((8, depth), F32),
        ),
        in_specs=[anywhere] * 7 + [vmem, anywhere, vmem] + [anywhere] + [vmem] * 2 + [anywhere] * 4,
        out_specs=[anywhere] * 2 + [vmem] * 5,
        scratch_shapes=[
            low(blocks, BLOCK, depth), low(group, cols), low(group, cols), low(group, cols),
            low(cols, group), full(group, cols), low(ctx, tokens, cols), low(depth, 3 * cols),
            full(group, table.shape[1]),
            full(cols, group), full(group, cols), full(group, cols),
            full(8, group), low(group, 3 * cols), full(depth, 3 * cols), low(lines, 2, shard, 3 * cols),
            low(pairs, BLOCK, depth), low(pairs + 1, BLOCK, depth),
            low(max(lines - 1, 1), 2, shard, 3 * cols), low(2, shard, 3 * cols),
            low(2, shard, 3 * cols),
            full(8, depth), full(fsdp, 8, depth), full(8, depth), full(ctx, 8, depth),
        ]
        + [low(ctx, side, *shape) for shape in shapes]
        + [low(ctx, hops, side, *shape) for shape in shapes]
        + [low(ctx, hops, *shape) for shape in shapes]
        + [low(ctx + 1, *shape) for shape in shapes]
        + [
            dma((8,)), dma((ctx,)), dma((ctx,)), dma((ctx,)), dma((ctx,)),
            dma((pairs,)), dma((pairs,)), dma((pairs + 1,)), dma((2, pairs)),
            dma((tokens // BLOCK,)), dma((pairs,)),
            dma((3, lines)), dma((3, lines)), dma((2, 3)), dma((2, 3)),
            dma((fsdp,)), dma((fsdp,)), dma((ctx,)), dma((ctx,)),
            dma((3, ctx, side)), dma((3, ctx, hops, side)), dma((3, ctx, hops, side)),
            dma((3, ctx, hops)), dma((3, ctx, hops)), dma((3, ctx + 1)), dma((3, ctx)),
        ],
        compiler_params=pltpu.CompilerParams(
            collective_id=3, has_side_effects=True, vmem_limit_bytes=BACKWARD_LIMIT
        ),
        name="backward",
    )(d_out, x, q, k, vm, kt, att, lse, wqkv, gain, table, start, dg_two, *sums)


def layer(
    mesh, tokens, value_first, lengths, w_query, w_key, w_value, w_out, w_gate, w_up, w_down,
    gain_attn, gain_ffn, out_grad, value_grad,
):
    fsdp, ctx = mesh.shape["fsdp"], mesh.shape["ctx"]
    count, depth = tokens.shape
    group = count * ctx
    cols = depth // ctx
    rows = depth // fsdp
    f, c = lax.axis_index("fsdp"), lax.axis_index("ctx")
    small = jnp.stack([gain_attn, gain_ffn]).astype(BF16).astype(F32)
    small = lax.dynamic_update_slice(
        jnp.zeros((8, depth), F32), small, (jnp.int32(0), (f * rows).astype(jnp.int32))
    )
    small = lax.dynamic_update_slice(small, lengths.astype(F32), (2, 0))
    (
        attended, wos, gus, wds, xs, q, k, vm, kt, att, wq, lse, table, first, gains
    ) = forward(
        mesh, tokens, value_first, (w_query, w_key, w_value, w_out, w_gate, w_up, w_down), small
    )
    gain_one, gain_two = gains[0:1], gains[1:2]
    wq = wq.reshape(depth, 3 * cols)
    result, dx2, d_out, dg_two, *sums = feed_forward(
        mesh, attended, tokens, out_grad, wos.reshape(depth, depth), gain_two,
        gus.reshape(ctx, depth, -1), wds.reshape(-1, depth),
    )
    folded, dvr, g_wo, g_gu, g_wd, g_qkv, gain_grads = backward(
        mesh, d_out, xs.reshape(group, depth), q, k, vm, kt, att, lse, wq, gain_one, table, first, dg_two,
        sums,
    )
    gain_grads = lax.dynamic_slice(
        gain_grads, (jnp.int32(0), (f * rows).astype(jnp.int32)), (2, rows)
    )
    ff = w_gate.shape[1]
    return (
        result,
        dx2 + folded.astype(F32),
        value_grad + dvr.astype(F32),
        g_qkv[:, :cols],
        g_qkv[:, cols : 2 * cols],
        g_qkv[:, 2 * cols :],
        g_wo,
        g_gu[:, :ff],
        g_gu[:, ff:],
        g_wd,
        gain_grads[0],
        gain_grads[1],
    )


def solution(mesh):
    rows = P(("fsdp", "ctx"), None)
    shard = P("fsdp", "ctx")
    return jax.shard_map(
        functools.partial(layer, mesh),
        mesh=mesh,
        in_specs=(rows, rows, P("fsdp", None)) + (shard,) * 7 + (P("fsdp"),) * 2 + (rows, rows),
        out_specs=(rows, rows, rows) + (shard,) * 7 + (P("fsdp"),) * 2,
        check_vma=False,
    )
```

```python
import functools
import math

import jax
import jax.numpy as jnp
from jax import lax
from jax.experimental import pallas as pl
from jax.experimental.pallas import tpu as pltpu
from jax.sharding import PartitionSpec as P

HEAD = 64
EPSILON = 1e-05
THETA = 10000.0
NEGATIVE = -1e30
BLOCK = 256
VMEM_LIMIT = 58 * 1024 * 1024
BACKWARD_LIMIT = 58 * 1024 * 1024
MESH = pl.DeviceIdType.MESH
BF16 = jnp.bfloat16
F32 = jnp.float32


def nn(left, right):
    return lax.dot_general(left, right, (((1,), (0,)), ((), ())), preferred_element_type=F32)


def nt(left, right):
    return lax.dot_general(left, right, (((1,), (1,)), ((), ())), preferred_element_type=F32)


def tn(left, right):
    return lax.dot_general(left, right, (((0,), (0,)), ((), ())), preferred_element_type=F32)


def turns(table, width):
    lane = lax.broadcasted_iota(jnp.int32, table.shape, 1)
    swapped = pltpu.roll(table, HEAD, 1)
    cos = jnp.where(lane < HEAD, table, swapped)
    sin = jnp.where(lane < HEAD, swapped, table)
    times = width // table.shape[1]
    return jnp.concatenate([cos] * times, axis=1), jnp.concatenate([sin] * times, axis=1)


def half_swap(rows):
    width = rows.shape[1]
    lane = lax.broadcasted_iota(jnp.int32, rows.shape, 1)
    low = lax.rem(lane, HEAD) < HEAD // 2
    return jnp.where(
        low,
        pltpu.roll(rows, width - HEAD // 2, 1),
        pltpu.roll(rows, HEAD // 2, 1),
    )


def head_lanes(shape, head):
    lane = lax.broadcasted_iota(jnp.int32, shape, 1)
    return (lane >= head * HEAD) & (lane < (head + 1) * HEAD)


def early_chunks(ctx):
    return max(ctx // 2, 1)


class Plan:
    def __init__(self, fsdp, ctx):
        self.fsdp, self.ctx = fsdp, ctx
        self.lines = fsdp // 2
        self.across = math.isqrt(self.lines)
        self.along = self.lines // self.across
        self.half = ctx // 2
        self.early = early_chunks(ctx)
        self.f = lax.axis_index("fsdp")
        self.c = lax.axis_index("ctx")
        self.core = lax.rem(self.f, 2)
        self.line = self.f // 2
        self.a = self.line // self.along
        self.b = lax.rem(self.line, self.along)
        self.home = self.c // self.half
        self.started = []
        self.draining = False

    def barrier(self):
        sem = pltpu.get_barrier_semaphore()
        count = 0
        for step in range(1, self.fsdp):
            dev = (lax.rem(self.f + step, self.fsdp), self.c)
            pl.semaphore_signal(sem, inc=1, device_id=dev, device_id_type=MESH)
            count += 1
        for step in range(1, self.ctx):
            for core in range(2):
                dev = (self.line * 2 + core, lax.rem(self.c + step, self.ctx))
                pl.semaphore_signal(sem, inc=1, device_id=dev, device_id_type=MESH)
                count += 1
        pl.semaphore_wait(sem, count)

    def greet_plane(self):
        sem = pltpu.get_barrier_semaphore()
        for step in range(1, self.fsdp):
            dev = (lax.rem(self.f + step, self.fsdp), self.c)
            pl.semaphore_signal(sem, inc=1, device_id=dev, device_id_type=MESH)
        pl.semaphore_wait(sem, self.fsdp - 1)

    def when(self, cond, act):
        if cond is True:
            act()
        else:
            pl.when(cond)(act)

    def send(self, src, dst, send_sem, recv_sem, dev, cond=True):
        def copy():
            return pltpu.make_async_remote_copy(
                src_ref=src, dst_ref=dst, send_sem=send_sem, recv_sem=recv_sem,
                device_id=dev, device_id_type=MESH,
            )

        if self.draining:
            self.when(cond, lambda: copy().wait_send())
            return
        self.when(cond, lambda: copy().start())
        self.started.append((cond, lambda: copy().wait_send()))

    def keep(self, src, dst, sem, cond=True):
        if self.draining:
            return
        self.when(cond, lambda: pltpu.make_async_copy(src, dst, sem).start())

    def arrive(self, dst, sem, cond=True):
        if self.draining:
            return
        self.when(cond, lambda: pltpu.make_async_copy(dst, dst, sem).wait())

    def drain(self):
        for cond, act in self.started:
            self.when(cond, act)
        self.started = []


def both(*conds):
    out = True
    for cond in conds:
        if cond is not True:
            out = cond if out is True else jnp.logical_and(out, cond)
    return out


class Gathering:
    def __init__(self, plan, own, whole, sems):
        self.plan, self.own, self.whole = plan, own, whole
        self.sem, self.z_out, self.p_out, self.s_out = sems
        self.widths = (own[0].shape[1], None, own[2].shape[1])

    def spots(self, row, j):
        wos, gus, wds = self.whole

        def band(width):
            return pl.ds(pl.multiple_of(j * width, width), width)

        return (
            wos.at[row, :, band(self.widths[0])], gus.at[j, row], wds.at[row, :, band(self.widths[2])],
        )

    def along_ctx(self, srcs, j, cond, up, down, items=(0, 1, 2)):
        plan = self.plan
        dsts = self.spots(plan.f, j)
        for i in items:
            if up:
                plan.send(
                    srcs[i], dsts[i], self.z_out.at[i, 0, j], self.sem.at[i, plan.f, j],
                    (plan.f, plan.c + 1), both(cond, plan.c < plan.ctx - 1),
                )
            if down:
                plan.send(
                    srcs[i], dsts[i], self.z_out.at[i, 1, j], self.sem.at[i, plan.f, j],
                    (plan.f, plan.c - 1), both(cond, plan.c > 0),
                )

    def on_plane(self, srcs, row, line, j, cond, over_a, over_b, items=(0, 1, 2)):
        plan = self.plan
        dsts = self.spots(row, j)
        for i in items:
            if over_a is not False:
                for hop in range(1, plan.across):
                    to = (lax.rem(plan.a + hop, plan.across) * plan.along + plan.b) * 2 + plan.core
                    plan.send(
                        srcs[i], dsts[i], self.p_out.at[i, hop - 1, line, j],
                        self.sem.at[i, row, j], (to, plan.c), both(cond, over_a),
                    )
            if over_b is not False:
                for hop in range(1, plan.along):
                    to = (plan.a * plan.along + lax.rem(plan.b + hop, plan.along)) * 2 + plan.core
                    plan.send(
                        srcs[i], dsts[i], self.p_out.at[i, plan.across + hop - 2, line, j],
                        self.sem.at[i, row, j], (to, plan.c), both(cond, over_b),
                    )
            plan.send(
                srcs[i], dsts[i], self.s_out.at[i, line, j], self.sem.at[i, row, j],
                (plan.line * 2 + 1 - plan.core, plan.c), cond,
            )

    def near(self, dist):
        plan = self.plan
        for side in range(2 if dist else 1):
            j = plan.c - dist if side == 0 else plan.c + dist
            there = True if dist == 0 else (j >= 0 if side == 0 else j < plan.ctx)
            yield jnp.clip(j, 0, plan.ctx - 1), there, side

    def start_ctx(self):
        self.along_ctx(self.own, self.plan.c, True, True, True)

    def start_plane(self):
        plan = self.plan
        self.on_plane(self.own, plan.f, plan.line, plan.c, True, True, True)
        for src, dst, i in zip(self.own, self.spots(plan.f, plan.c), range(3)):
            plan.keep(src, dst, self.sem.at[i, plan.f, plan.c])

    def wait(self, row, j, cond=True, items=(0, 1, 2)):
        dsts = self.spots(row, j)
        for i in items:
            self.plan.arrive(dsts[i], self.sem.at[i, row, j], cond)
        return dsts

    def from_ctx(self, dist):
        plan = self.plan
        for j, there, side in self.near(dist):
            for i in ORDER:
                dsts = self.wait(plan.f, j, there, (i,))
                self.along_ctx(dsts, j, there, side == 0, side == 1, (i,))
                self.on_plane(dsts, plan.f, plan.line, j, there, True, True, (i,))

    def from_plane(self, dist):
        plan = self.plan
        for j, there, _ in self.near(dist):
            first = j < plan.half
            for hop in range(1, plan.across):
                line = lax.rem(plan.a + plan.across - hop, plan.across) * plan.along + plan.b
                row = line * 2 + plan.core
                for i in ORDER:
                    dsts = self.wait(row, j, there, (i,))
                    self.on_plane(dsts, row, line, j, there, False, first, (i,))
            for hop in range(1, plan.along):
                line = plan.a * plan.along + lax.rem(plan.b + plan.along - hop, plan.along)
                row = line * 2 + plan.core
                for i in ORDER:
                    dsts = self.wait(row, j, there, (i,))
                    self.on_plane(
                        dsts, row, line, j, there, jnp.logical_not(first), False, (i,)
                    )

    def from_far(self, dist):
        plan = self.plan
        for j, there, _ in self.near(dist):
            for hop in range(1, plan.across):
                for hop2 in range(1, plan.along):
                    line = lax.rem(plan.a + hop, plan.across) * plan.along + lax.rem(
                        plan.b + hop2, plan.along
                    )
                    row = line * 2 + plan.core
                    for i in ORDER:
                        dsts = self.wait(row, j, there, (i,))
                        self.on_plane(dsts, row, line, j, there, False, False, (i,))

    def finish(self):
        plan = self.plan
        self.wait(plan.f, plan.c)

        def other(line, carry):
            for j in range(plan.ctx):
                self.wait(line * 2 + 1 - plan.core, j)
            return carry

        lax.fori_loop(0, plan.lines, other, 0)


def forward_kernel(
    fsdp, ctx,
    x, vf, m_q, m_k, m_v, m_o, m_g, m_u, m_d, small,
    attended, wos, gus, wds, x_out_ref, q_ref, k_ref, vm_ref, kt_ref, att_ref, wq_ref,
    lse, table, start, gain,
    xs, vs, wq, wqh, own_q, own_o, own_g, own_d, gs, q, k, vm, kt, vt, att, out, acc, mx, tot,
    x_sem, x_out, v_sem, v_out, q_sem, q_out, h_sem, g_sem, g_out,
    w_sem, w_z, w_p, w_s, o_sem, o_out, save_sem,
    w_q, w_k, w_v, w_o, w_g, w_u, w_d, m_sem,
):
    masters = (m_q, m_k, m_v, m_o, m_g, m_u, m_d)
    plan = Plan(fsdp, ctx)
    f, c, core, line, home, half = plan.f, plan.c, plan.core, plan.line, plan.home, plan.half
    tokens, depth = x.shape
    group = tokens * ctx
    cols = depth // ctx
    heads = cols // HEAD
    blocks = group // BLOCK
    per = tokens // BLOCK
    owner = core == home
    away = jnp.logical_not(owner)
    sibling = (line * 2 + 1 - core, c)

    fetched = (w_q, w_k, w_v, w_o, w_g, w_u, w_d)
    for i, (src, dst) in enumerate(zip(masters, fetched)):
        plan.keep(src, dst, m_sem.at[i])
    for i in range(3):
        plan.arrive(fetched[i], m_sem.at[i])
    own_q[...] = jnp.concatenate(
        [w_q[...].astype(BF16), w_k[...].astype(BF16), w_v[...].astype(BF16)], axis=1
    )
    plan.barrier()
    gathering = Gathering(
        plan, (own_o, own_g, own_d), (wos, gus, wds), (w_sem, w_z, w_p, w_s)
    )

    for hop in range(1, fsdp):
        plan.send(small, gs.at[f], g_out.at[hop - 1], g_sem.at[f], (lax.rem(f + hop, fsdp), c))
    plan.keep(small, gs.at[f], g_sem.at[f])
    plan.send(own_q, wqh, h_sem.at[0], h_sem.at[1], (f, lax.rem(c + half, ctx)))

    piece = tokens // PIECES

    def part_of(ref, i):
        return ref.at[pl.ds(i * piece, piece), :]

    def spread_x(src, j, i, below, above, cond):
        dst = part_of(xs.at[j], i)
        if below:
            plan.send(
                src, dst, x_out.at[0, j, i], x_sem.at[j, i], (f, c - 1),
                both(cond, c > home * half),
            )
        if above:
            plan.send(
                src, dst, x_out.at[1, j, i], x_sem.at[j, i], (f, c + 1),
                both(cond, c < home * half + half - 1),
            )
        plan.send(src, dst, x_out.at[2, j, i], x_sem.at[j, i], sibling, cond)

    entry = jnp.where(core == 0, half - 1, half)
    for i in range(PIECES):
        src = part_of(x, i)
        plan.send(
            src, part_of(xs.at[c], i), x_out.at[0, c, i], x_sem.at[c, i], (f, entry), away
        )
        spread_x(src, c, i, True, True, owner)
        plan.keep(src, part_of(xs.at[c], i), x_sem.at[c, i], owner)
    for at in range(plan.lines):
        plan.send(
            own_q, wq.at[f], q_out.at[0, at], q_sem.at[f], (at * 2, c),
            jnp.logical_not(f == at * 2),
        )
    plan.keep(own_q, wq.at[f], q_sem.at[f], core == 0)
    for i in range(half):
        for kk in range(2):
            to = core * half + i
            rank = lax.rem(to + kk * half, ctx)
            src = vf.at[:, pl.ds(pl.multiple_of(rank * cols, cols), cols)]
            mine = both(owner, c == to, core == kk)
            plan.send(
                src, vs.at[c], v_out.at[i, kk], v_sem.at[c], (line * 2 + kk, to),
                jnp.logical_not(mine),
            )
            plan.keep(src, vs.at[c], v_sem.at[c], mine)
    for i in range(3, 7):
        plan.arrive(fetched[i], m_sem.at[i])
    own_o[...] = w_o[...].astype(BF16)
    own_g[...] = jnp.concatenate([w_g[...].astype(BF16), w_u[...].astype(BF16)], axis=1)
    own_d[...] = w_d[...].astype(BF16)

    for row in range(fsdp):
        plan.arrive(gs.at[row], g_sem.at[row])
    total = gs[0]
    for row in range(1, fsdp):
        total = total + gs[row]
    gain[...] = total
    lens = gs[line * 2 + home]
    doc_count = SHORTS_AND_LONG

    def firsts(places):
        end = jnp.zeros((1, 1), F32)
        first = jnp.zeros(places.shape, F32)
        for d in range(doc_count):
            size = lens[2:3, d : d + 1]
            end = end + size
            first = first + jnp.where(places >= end, size, 0.0)
        return first

    places = lax.broadcasted_iota(jnp.int32, (1, group), 1).astype(F32)
    start[...] = firsts(places).astype(jnp.int32)

    def angles(b, carry):
        rows = pl.ds(pl.multiple_of(b * BLOCK, BLOCK), BLOCK)
        at = (b * BLOCK + lax.broadcasted_iota(jnp.int32, (BLOCK, 128), 0)).astype(F32)
        lane = lax.broadcasted_iota(jnp.int32, (BLOCK, 128), 1)
        pair = lax.rem(lane, HEAD // 2).astype(F32)
        angle = (at - firsts(at)) * jnp.exp(pair * (-2.0 * math.log(THETA) / HEAD))
        sine = jnp.sin(angle)
        table[rows, :] = jnp.where(
            lane < HEAD, jnp.cos(angle), jnp.where(lane < HEAD + HEAD // 2, -sine, sine)
        )
        return carry

    lax.fori_loop(0, blocks, angles, 0)

    plan.arrive(wqh, h_sem.at[1])
    for at in range(plan.lines):
        plan.send(
            wqh, wq.at[f], q_out.at[1, at], q_sem.at[f], (at * 2 + 1, c),
            jnp.logical_not(f == at * 2 + 1),
        )
    plan.keep(wqh, wq.at[f], q_sem.at[f], core == 1)
    gathering.start_plane()

    def project(j):
        def body(i, carry):
            rows = pl.ds(pl.multiple_of(j * tokens + i * BLOCK, BLOCK), BLOCK)
            xv = xs[j, pl.ds(pl.multiple_of(i * BLOCK, BLOCK), BLOCK), :].astype(F32)
            rstd = lax.rsqrt(jnp.mean(xv * xv, axis=1, keepdims=True) + EPSILON)
            hv = (xv * rstd * gain[0:1, :]).astype(BF16)
            raw = nn(hv, wq[...].reshape(depth, 3 * cols))
            cos_v, sin_v = turns(table[rows, :], cols)
            rq = raw[:, :cols]
            rk = raw[:, cols : 2 * cols]
            qv = (rq * cos_v + half_swap(rq) * sin_v).astype(BF16)
            q[rows, :] = (qv.astype(F32) * (1.0 / math.sqrt(HEAD))).astype(BF16)
            kv = (rk * cos_v + half_swap(rk) * sin_v).astype(BF16)
            k[rows, :] = kv
            kt[:, rows] = kv.T
            att[rows, :] = 0.5 * raw[:, 2 * cols :]
            return carry

        lax.fori_loop(0, per, body, 0)

    def actions(place):
        out = [gathering.start_ctx] if place == START else []
        for kind in ("from_ctx", "from_plane", "from_far"):
            for dist in range(ctx):
                if (kind, dist) != ("from_ctx", 0) and place == spot_of(kind, dist, ctx, blocks):
                    out.append(functools.partial(getattr(gathering, kind), dist))
        return out

    for dist in range(ctx):
        for i in range(PIECES):
            for j, there, side in gathering.near(dist):
                spot = part_of(xs.at[j], i)
                plan.arrive(spot, x_sem.at[j, i], there)
                if dist:
                    spread_x(spot, j, i, side == 1, side == 0, both(owner, there))
        for act in actions(("x", dist)):
            act()
    for row in range(fsdp):
        plan.arrive(wq.at[row], q_sem.at[row])
    for act in actions("q"):
        act()
    for j in range(ctx):
        project(j)
    for act in actions("p"):
        act()
    saves = [(xs, x_out_ref), (q, q_ref), (k, k_ref), (kt, kt_ref), (wq, wq_ref)]
    for i, (src, dst) in enumerate(saves):
        plan.keep(src, dst, save_sem.at[i])
    for j in range(ctx):
        plan.arrive(vs.at[j], v_sem.at[j])

    def mix(b, carry):
        rows = pl.ds(pl.multiple_of(b * BLOCK, BLOCK), BLOCK)
        first = vs[b // per, pl.ds(pl.multiple_of(lax.rem(b, per) * BLOCK, BLOCK), BLOCK), :]
        mixed = (att[rows, :] + 0.5 * first.astype(F32)).astype(BF16)
        vm[rows, :] = mixed
        vt[:, rows] = mixed.T
        return carry

    lax.fori_loop(0, blocks, mix, 0)
    plan.keep(vm, vm_ref, save_sem.at[5])

    rank = lax.rem(c + core * half, ctx)

    def give(b):
        j = b // per
        where = lax.rem(b, per)
        src = out.at[pl.ds(pl.multiple_of(b * BLOCK, BLOCK), BLOCK), :]
        dst = attended.at[
            pl.ds(pl.multiple_of(where * BLOCK, BLOCK), BLOCK),
            pl.ds(pl.multiple_of(rank * cols, cols), cols),
        ]
        mine = both(owner, c == j)
        plan.send(
            src, dst, o_out.at[b], o_sem.at[rank, where], (line * 2 + home, j),
            jnp.logical_not(mine),
        )
        plan.keep(src, dst, o_sem.at[rank, where], mine)

    schedule = {}

    def at_step(t, act):
        schedule.setdefault(min(t, blocks - 1), []).append(act)

    for place in range(blocks):
        for act in actions(("t", place)):
            at_step(place, act)

    def unit(t, carry):
        b = blocks - 1 - t
        rows = pl.ds(pl.multiple_of(b * BLOCK, BLOCK), BLOCK)
        acc[...] = jnp.zeros_like(acc)
        mx[...] = jnp.full_like(mx, NEGATIVE)
        tot[...] = jnp.zeros_like(tot)
        qv = q[rows, :]
        first = start[0:1, rows]

        def keys(kb, inner):
            krows = pl.ds(pl.multiple_of(kb * KEYS, KEYS), KEYS)
            kv = k[krows, :]
            key_pos = kb * KEYS + lax.broadcasted_iota(jnp.int32, (KEYS, BLOCK), 0)
            query_pos = b * BLOCK + lax.broadcasted_iota(jnp.int32, (KEYS, BLOCK), 1)
            allowed = (key_pos <= query_pos) & (key_pos >= first)
            for head in range(heads):
                band = slice(head * HEAD, (head + 1) * HEAD)
                qm = jnp.where(head_lanes(qv.shape, head), qv, jnp.zeros_like(qv))
                s = jnp.where(allowed, nt(kv, qm), NEGATIVE)
                old = mx[head : head + 1, :]
                new = jnp.maximum(old, jnp.max(s, axis=0, keepdims=True))
                p = jnp.exp(s - new)
                shrink = jnp.exp(old - new)
                mx[head : head + 1, :] = new
                tot[head : head + 1, :] = tot[head : head + 1, :] * shrink + jnp.sum(
                    p, axis=0, keepdims=True
                )
                acc[band, :] = acc[band, :] * shrink + nn(vt[band, krows], p.astype(BF16))
            return inner

        lax.fori_loop(0, b // (KEYS // BLOCK) + 1, keys, 0)
        for head in range(heads):
            band = slice(head * HEAD, (head + 1) * HEAD)
            acc[band, :] = acc[band, :] / tot[head : head + 1, :]
        ov = acc[...].T
        att[rows, :] = ov
        out[rows, :] = ov.astype(BF16)
        lse[:, rows] = mx[...] + jnp.log(tot[...])
        give(b)
        for s in sorted(schedule):

            @pl.when(t == s)
            def _(s=s):
                for act in schedule[s]:
                    act()

        return carry

    kept = plan.started
    plan.started = []
    lax.fori_loop(0, blocks, unit, 0)
    plan.started = kept
    plan.keep(att, att_ref, save_sem.at[6])
    for act in actions("late"):
        act()
    gathering.finish()
    for at in range(ctx):
        for where in range(per):
            plan.arrive(
                attended.at[pl.ds(where * BLOCK, BLOCK), pl.ds(at * cols, cols)],
                o_sem.at[at, where],
            )
    for i, (src, dst) in enumerate(saves + [(vm, vm_ref), (att, att_ref)]):
        plan.arrive(dst, save_sem.at[i])
    plan.drain()
    plan.draining = True
    for b in range(blocks):
        give(b)
    for s in sorted(schedule):
        for act in schedule[s]:
            act()


ORDER = (0, 1, 2)
PIECES = 4
START = ('x', 0)
SHORTS_AND_LONG = 4
KEYS = 512
SPOTS = {
    "from_ctx": (None, ('x', 2), ('x', 3), ('t', 0)),
    "from_plane": (('x', 2), ('x', 3), ('t', 0), ('t', 3)),
    "from_far": (('t', 0), ('t', 2), ('t', 5), 'late'),
}


def spot_of(kind, dist, ctx, blocks):
    if dist >= 4:
        return "p" if kind == "from_ctx" else "late"
    spot = SPOTS[kind][dist]
    return ("t", spot[1] * (blocks // 8)) if spot[0] == "t" else spot


def forward(mesh, x, vf, weights, small):
    fsdp, ctx = mesh.shape["fsdp"], mesh.shape["ctx"]
    tokens, depth = x.shape
    cols = depth // ctx
    group = tokens * ctx
    blocks = group // BLOCK
    per = tokens // BLOCK
    lines = fsdp // 2
    across = math.isqrt(lines)
    peers = max(across - 1 + lines // across - 1, 1)
    shard = depth // fsdp
    out_shape = weights[3].shape
    up_shape = (weights[4].shape[0], 2 * weights[4].shape[1])
    down_shape = weights[6].shape
    anywhere = pl.BlockSpec(memory_space=pl.ANY)
    vmem = pl.BlockSpec(memory_space=pltpu.VMEM)
    dma = pltpu.SemaphoreType.DMA

    def low(*shape):
        return pltpu.VMEM(shape, BF16)

    def full(*shape):
        return pltpu.VMEM(shape, F32)

    def array(dtype, *shape):
        return jax.ShapeDtypeStruct(shape, dtype)

    return pl.pallas_call(
        functools.partial(forward_kernel, fsdp, ctx),
        out_shape=(
            array(BF16, tokens, depth),
            array(BF16, fsdp, out_shape[0], depth),
            array(BF16, ctx, fsdp, *up_shape),
            array(BF16, fsdp, down_shape[0], depth),
            array(BF16, ctx, tokens, depth),
            array(BF16, group, cols),
            array(BF16, group, cols),
            array(BF16, group, cols),
            array(BF16, cols, group),
            array(F32, group, cols),
            array(BF16, fsdp, shard, 3 * cols),
            array(F32, 8, group),
            array(F32, group, 128),
            array(jnp.int32, 1, group),
            array(F32, 8, depth),
        ),
        in_specs=[anywhere] * 9 + [vmem],
        out_specs=[anywhere] * 11 + [vmem] * 4,
        scratch_shapes=[
            low(ctx, tokens, depth), low(ctx, tokens, cols), low(fsdp, shard, 3 * cols),
            low(shard, 3 * cols), low(shard, 3 * cols), low(*out_shape), low(*up_shape),
            low(*down_shape), full(fsdp, 8, depth),
            low(group, cols), low(group, cols), low(group, cols), low(cols, group),
            low(cols, group), full(group, cols), low(group, cols),
            full(cols, BLOCK), full(8, BLOCK), full(8, BLOCK),
            dma((ctx, PIECES)), dma((3, ctx, PIECES)), dma((ctx,)), dma((ctx // 2, 2)),
            dma((fsdp,)), dma((2, lines)), dma((2,)), dma((fsdp,)), dma((fsdp,)),
            dma((3, fsdp, ctx)), dma((3, 2, ctx)), dma((3, peers, lines, ctx)), dma((3, lines, ctx)),
            dma((ctx, per)), dma((blocks,)), dma((7,)),
        ]
        + [full(*weight.shape) for weight in weights]
        + [dma((7,))],
        compiler_params=pltpu.CompilerParams(
            collective_id=0, has_side_effects=True, vmem_limit_bytes=VMEM_LIMIT
        ),
        name="forward",
    )(x, vf, *weights, small)


def chunk_order(i, ctx):
    return i % 2 * (ctx // 2) + i // 2


def reduce_line(plan, low, first, second):
    return second * plan.along + first if low else first * plan.along + second


def reduce_places(plan, j):
    low = j < plan.half
    return (low, plan.b if low else plan.a, plan.a if low else plan.b)


def feed_kernel(
    fsdp, ctx,
    o, x, dy, wo, gain, gu, wd,
    out, dx2, do, dg, s_wo, s_gu, s_wd, early,
    x2, h2, h2t, total, act, dgu,
    my_gu, my_wd, my_wo, got_gu, got_wd, got_wo, near_gu,
    gu_sem, gu_out, wd_sem, wd_out, wo_sem, wo_out, near_sem, near_out,
):
    plan = Plan(fsdp, ctx)
    core = plan.core
    sibling = (plan.line * 2 + 1 - core, plan.c)
    step = pl.program_id(0)
    last = pl.num_programs(0) - 1
    tokens, depth = x.shape
    chunk = wd.shape[0]
    blocks = tokens // BLOCK
    lines = plan.lines
    shard = depth // fsdp
    row_lines = my_wd.shape[1]
    row_count = my_wd.shape[3]
    slot = lax.rem(step, 2)
    side = plan.across

    def give(at):
        place = lax.rem(at, 2)
        for i in range(lines):
            plan.send(
                my_gu.at[place, i, 1 - core], got_gu.at[at, i], gu_out.at[place, i],
                gu_sem.at[at, i], sibling,
            )
        for i in range(row_lines):
            plan.send(
                my_wd.at[place, i, 1 - core], got_wd.at[at, i], wd_out.at[place, i],
                wd_sem.at[at, i], sibling,
            )

    def given(at):
        plan.draining = True
        give(at)
        plan.draining = False

    @pl.when(step == 0)
    def _():
        plan.greet_plane()

        def rows_of(b, carry):
            rows = pl.ds(pl.multiple_of(b * BLOCK, BLOCK), BLOCK)
            mid = x[rows, :].astype(F32) + nn(o[rows, :], wo[...])
            x2[rows, :] = mid
            rstd = lax.rsqrt(jnp.mean(mid * mid, axis=1, keepdims=True) + EPSILON)
            hv = (mid * rstd * gain[...]).astype(BF16)
            h2[rows, :] = hv
            h2t[:, rows] = hv.T
            total[rows, :] = mid
            dx2[rows, :] = jnp.zeros((BLOCK, depth), F32)
            return carry

        lax.fori_loop(0, blocks, rows_of, 0)

    @pl.when(jnp.logical_and(step >= 2, step < last))
    def _():
        given(step - 2)

    @pl.when(step < last)
    def _():
        def rows_of(b, carry):
            rows = pl.ds(pl.multiple_of(b * BLOCK, BLOCK), BLOCK)
            both_ = nn(h2[rows, :], gu[0])
            gate = both_[:, :chunk]
            up = both_[:, chunk:]
            da = nt(dy[rows, :], wd[...]).astype(BF16).astype(F32)
            sig = 1.0 / (1.0 + jnp.exp(-gate))
            silu = gate * sig
            av = (silu * up).astype(BF16)
            act[rows, :] = av
            dgate = (da * up * (sig * (1.0 + gate * (1.0 - sig)))).astype(BF16)
            dup = (da * silu).astype(BF16)
            dv = jnp.concatenate([dgate, dup], axis=1)
            dgu[rows, :] = dv
            total[rows, :] = total[rows, :] + nn(av, wd[...])
            dx2[rows, :] = dx2[rows, :] + nt(dv, gu[0])
            return carry

        lax.fori_loop(0, blocks, rows_of, 0)

        for part in range(depth // 512):
            at = slice(part * 512, (part + 1) * 512)
            val = tn(act[...], dy[:, at])
            for r in range(row_lines * 2):
                my_wd[slot, r // 2, r % 2, :, at] = val[
                    r * row_count : (r + 1) * row_count
                ].astype(BF16)

        rows_each = BLOCK // shard

        def weight(b, carry):
            rows = pl.ds(pl.multiple_of(b * BLOCK, BLOCK), BLOCK)
            val = nn(h2t[rows, :], dgu[...]).astype(BF16)
            for r in range(rows_each):
                my_gu[slot, b * (rows_each // 2) + r // 2, r % 2] = val[
                    r * shard : (r + 1) * shard
                ]
            return carry

        lax.fori_loop(0, depth // BLOCK, weight, 0)
        give(step)

    def over_plane(at):
        j = chunk_order(at, ctx)
        low, first, second = reduce_places(plan, j)
        for hop in range(1, side):
            to = lax.rem(first + hop, side)
            dev = (reduce_line(plan, low, to, second) * 2 + core, plan.c)
            for inner in range(side):
                plan.send(
                    got_gu.at[at, reduce_line(plan, low, to, inner)],
                    near_gu.at[at, hop - 1, inner], near_out.at[at, hop - 1, inner],
                    near_sem.at[at, hop - 1, inner], dev,
                )

    def collect(at):
        place = lax.rem(at, 2)
        for i in range(lines):
            plan.arrive(got_gu.at[at, i], gu_sem.at[at, i])

            @pl.when(at >= plan.early)
            def _(i=i):
                add_rows(s_gu.at[0, i], [my_gu.at[place, i, core], got_gu.at[at, i]])

            @pl.when(at < plan.early)
            def _(i=i):
                add_rows(got_gu.at[at, i], [my_gu.at[place, i, core], got_gu.at[at, i]])

        for early_at in range(plan.early):

            @pl.when(at == early_at)
            def _(early_at=early_at):
                over_plane(early_at)

        for i in range(row_lines):
            plan.arrive(got_wd.at[at, i], wd_sem.at[at, i])
            add_rows(s_wd.at[i], [my_wd.at[place, i, core], got_wd.at[at, i]])

    @pl.when(jnp.logical_and(step >= 1, step < last))
    def _():
        collect(step - 1)

    @pl.when(step == last)
    def _():
        dg[...] = jnp.zeros_like(dg)

        def rows_of(b, carry):
            rows = pl.ds(pl.multiple_of(b * BLOCK, BLOCK), BLOCK)
            out[rows, :] = total[rows, :].astype(BF16)
            mid = x2[rows, :]
            rstd = lax.rsqrt(jnp.mean(mid * mid, axis=1, keepdims=True) + EPSILON)
            xhat = mid * rstd
            dh = dx2[rows, :]
            u = dh * gain[...]
            dm = dy[rows, :].astype(F32) + rstd * (
                u - xhat * jnp.mean(u * xhat, axis=1, keepdims=True)
            )
            dx2[rows, :] = dm
            dg[0:1, :] = dg[0:1, :] + jnp.sum(dh * xhat, axis=0, keepdims=True)
            h2[rows, :] = dm.astype(BF16)
            return carry

        lax.fori_loop(0, blocks, rows_of, 0)
        rows_each = BLOCK // shard

        def weight_out(b, carry):
            at = pl.ds(pl.multiple_of(b * BLOCK, BLOCK), BLOCK)
            val = tn(o[:, at], h2[...]).astype(BF16)
            for r in range(rows_each):
                my_wo[b * (rows_each // 2) + r // 2, r % 2] = val[r * shard : (r + 1) * shard]
            return carry

        lax.fori_loop(0, depth // BLOCK, weight_out, 0)
        for i in range(lines):
            plan.send(my_wo.at[i, 1 - core], got_wo.at[i], wo_out.at[i], wo_sem.at[i], sibling)

        def rows_out(b, carry):
            rows = pl.ds(pl.multiple_of(b * BLOCK, BLOCK), BLOCK)
            do[rows, :] = nt(h2[rows, :], wo[...]).astype(BF16)
            return carry

        lax.fori_loop(0, blocks, rows_out, 0)
        collect(last - 1)
        for i in range(lines):
            plan.arrive(got_wo.at[i], wo_sem.at[i])
            add_rows(s_wo.at[i], [my_wo.at[i, core], got_wo.at[i]])
        for at in (last - 2, last - 1):
            given(at)
        for at in range(plan.early):
            low, first, _ = reduce_places(plan, chunk_order(at, ctx))
            for inner in range(side):
                for hop in range(1, side):
                    plan.arrive(near_gu.at[at, hop - 1, inner], near_sem.at[at, hop - 1, inner])
                add_rows(
                    early.at[at, inner],
                    [got_gu.at[at, reduce_line(plan, low, first, inner)]]
                    + [near_gu.at[at, hop - 1, inner] for hop in range(1, side)],
                )
        plan.draining = True
        for at in range(plan.early):
            over_plane(at)
        for i in range(lines):
            plan.send(my_wo.at[i, 1 - core], got_wo.at[i], wo_out.at[i], wo_sem.at[i], sibling)
        plan.draining = False


def feed_forward(mesh, o, x, dy, wo, gain, gu, wd):
    fsdp, ctx = mesh.shape["fsdp"], mesh.shape["ctx"]
    tokens, depth = x.shape
    steps, _, width = gu.shape
    chunk = width // 2
    lines = fsdp // 2
    shard = depth // fsdp
    row_count = wd.shape[0] // fsdp
    row_lines = fsdp // ctx // 2
    side = math.isqrt(lines)
    early = early_chunks(ctx)
    hops = max(side - 1, 1)
    once = pl.Buffered(1)

    def chunk_of(i):
        return chunk_order(jnp.minimum(i, steps - 1), ctx)

    def chunk_before(i):
        return chunk_order(jnp.maximum(i - 1, 0), ctx)

    def whole(shape):
        return pl.BlockSpec(shape, lambda i: (0,) * len(shape), pipeline_mode=once)

    def whole_out(shape):
        return pl.BlockSpec(shape, lambda i: (0,) * len(shape), pipeline_mode=once)

    shapes = (
        jax.ShapeDtypeStruct((tokens, depth), BF16),
        jax.ShapeDtypeStruct((tokens, depth), F32),
        jax.ShapeDtypeStruct((tokens, depth), BF16),
        jax.ShapeDtypeStruct((8, depth), F32),
        jax.ShapeDtypeStruct((lines, shard, depth), BF16),
        jax.ShapeDtypeStruct((ctx - early, lines, shard, width), BF16),
        jax.ShapeDtypeStruct((lines, row_count, depth), BF16),
        jax.ShapeDtypeStruct((early, side, shard, width), BF16),
    )
    dma = pltpu.SemaphoreType.DMA
    return pl.pallas_call(
        functools.partial(feed_kernel, fsdp, ctx),
        grid=(steps + 1,),
        out_shape=shapes,
        in_specs=[
            whole((tokens, depth)),
            whole((tokens, depth)),
            whole((tokens, depth)),
            whole((depth, depth)),
            whole((1, depth)),
            pl.BlockSpec((1, depth, width), lambda i: (chunk_of(i), 0, 0)),
            pl.BlockSpec((chunk, depth), lambda i: (chunk_of(i), 0)),
        ],
        out_specs=[
            whole_out((tokens, depth)),
            whole_out((tokens, depth)),
            whole_out((tokens, depth)),
            whole_out((8, depth)),
            whole_out((lines, shard, depth)),
            pl.BlockSpec(
                (1, lines, shard, width), lambda i: (jnp.maximum(i - 1 - early, 0), 0, 0, 0)
            ),
            pl.BlockSpec((row_lines, row_count, depth), lambda i: (chunk_before(i), 0, 0)),
            whole_out((early, side, shard, width)),
        ],
        scratch_shapes=[
            pltpu.VMEM((tokens, depth), F32),
            pltpu.VMEM((tokens, depth), BF16),
            pltpu.VMEM((depth, tokens), BF16),
            pltpu.VMEM((tokens, depth), F32),
            pltpu.VMEM((tokens, chunk), BF16),
            pltpu.VMEM((tokens, width), BF16),
            pltpu.VMEM((2, lines, 2, shard, width), BF16),
            pltpu.VMEM((2, row_lines, 2, row_count, depth), BF16),
            pltpu.VMEM((lines, 2, shard, depth), BF16),
            pltpu.VMEM((steps, lines, shard, width), BF16),
            pltpu.VMEM((steps, row_lines, row_count, depth), BF16),
            pltpu.VMEM((lines, shard, depth), BF16),
            pltpu.VMEM((early, hops, side, shard, width), BF16),
            dma((steps, lines)), dma((2, lines)), dma((steps, row_lines)), dma((2, row_lines)),
            dma((lines,)), dma((lines,)), dma((early, hops, side)), dma((early, hops, side)),
        ],
        compiler_params=pltpu.CompilerParams(
            vmem_limit_bytes=VMEM_LIMIT, dimension_semantics=("arbitrary",), collective_id=4,
            has_side_effects=True,
        ),
        name="feed_forward",
    )(o, x, dy, wo, gain, gu, wd)


def chunk_rows(count):
    return 32 if count % 32 == 0 else count


def add_rows(dst, parts):
    count = dst.shape[0]
    rows = chunk_rows(count)

    def body(t, carry):
        at = pl.ds(pl.multiple_of(t * rows, rows), rows)
        total = parts[0][at, :].astype(F32)
        for part in parts[1:]:
            total = total + part[at, :].astype(F32)
        dst[at, :] = total.astype(dst.dtype)
        return carry

    lax.fori_loop(0, count // rows, body, 0)


class Reduction:
    def __init__(self, plan, sources, early, own, near, next_, last, outs, sems):
        self.plan = plan
        self.sources, self.early, self.own, self.near, self.next, self.last, self.outs = (
            sources, early, own, near, next_, last, outs,
        )
        (
            self.own_sem, self.near_sem, self.near_out, self.next_sem, self.next_out,
            self.last_sem, self.last_out,
        ) = sems
        self.side = plan.across
        ctx = plan.ctx
        self.chunks = [chunk_order(i, ctx) for i in range(ctx)]
        self.first_set = [(1, j) for j in self.chunks[: plan.early]]
        self.second_set = [(1, j) for j in self.chunks[plan.early :]]
        self.third_set = [(i, j) for i in (0, 2) for j in self.chunks]

    def piece(self, i, line, j):
        src = self.sources[i]
        if i == 1:
            return src.at[self.chunks.index(j) - self.plan.early, line]
        width = src.shape[2] // self.plan.ctx
        return src.at[line, :, pl.ds(j * width, width)]

    def send_next(self, i, j, source):
        plan = self.plan
        low, first, second = reduce_places(plan, j)
        for hop in range(1, self.side):
            to = lax.rem(second + hop, self.side)
            plan.send(
                source(to),
                self.next[i].at[j, hop - 1],
                self.next_out.at[i, j, hop - 1],
                self.next_sem.at[i, j, hop - 1],
                (reduce_line(plan, low, first, to) * 2 + plan.core, plan.c),
            )

    def start_early(self):
        plan = self.plan
        for at, (i, j) in enumerate(self.first_set):
            self.send_next(i, j, lambda to, at=at: self.early.at[at, to])
            for inner in range(self.side):
                plan.keep(
                    self.early.at[at, inner], self.own[i].at[j, inner], self.own_sem.at[i, j, inner]
                )

    def start(self, pairs):
        plan = self.plan
        for i, j in pairs:
            low, first, second = reduce_places(plan, j)
            for hop in range(1, self.side):
                to = lax.rem(first + hop, self.side)
                dev = (reduce_line(plan, low, to, second) * 2 + plan.core, plan.c)
                for inner in range(self.side):
                    plan.send(
                        self.piece(i, reduce_line(plan, low, to, inner), j),
                        self.near[i].at[j, hop - 1, inner],
                        self.near_out.at[i, j, hop - 1, inner],
                        self.near_sem.at[i, j, hop - 1, inner],
                        dev,
                    )
            for inner in range(self.side):
                plan.keep(
                    self.piece(i, reduce_line(plan, low, first, inner), j),
                    self.own[i].at[j, inner],
                    self.own_sem.at[i, j, inner],
                )

    def step_near(self, pairs):
        plan = self.plan
        for i, j in pairs:
            for inner in range(self.side):
                plan.arrive(self.own[i].at[j, inner], self.own_sem.at[i, j, inner])
                for hop in range(1, self.side):
                    plan.arrive(
                        self.near[i].at[j, hop - 1, inner], self.near_sem.at[i, j, hop - 1, inner]
                    )
                if not plan.draining:
                    add_rows(
                        self.own[i].at[j, inner],
                        [self.own[i].at[j, inner]]
                        + [self.near[i].at[j, hop - 1, inner] for hop in range(1, self.side)],
                    )
            self.send_next(i, j, lambda to, i=i, j=j: self.own[i].at[j, to])

    def step_next(self, pairs):
        plan = self.plan
        for i, j in pairs:
            _, _, second = reduce_places(plan, j)
            if (i, j) in self.first_set:
                for inner in range(self.side):
                    plan.arrive(self.own[i].at[j, inner], self.own_sem.at[i, j, inner])
            for hop in range(1, self.side):
                plan.arrive(self.next[i].at[j, hop - 1], self.next_sem.at[i, j, hop - 1])
            if not plan.draining:
                add_rows(
                    self.own[i].at[j, second],
                    [self.own[i].at[j, second]]
                    + [self.next[i].at[j, hop - 1] for hop in range(1, self.side)],
                )
            self.send_last(i, j, second, both(plan.c == 0, j > 0), both(plan.c == plan.ctx - 1, j < plan.ctx - 1))

    def send_last(self, i, j, second, up, down):
        plan = self.plan
        if up is not None:
            plan.send(
                self.own[i].at[j, second], self.last[i].at[j], self.last_out.at[i, j],
                self.last_sem.at[i, j], (plan.f, plan.c + 1), up,
            )
        if down is not None:
            slot = jnp.where(plan.c - 1 == j, plan.ctx, j)
            plan.send(
                self.own[i].at[j, second], self.last[i].at[slot], self.last_out.at[i, j],
                self.last_sem.at[i, slot], (plan.f, plan.c - 1), down,
            )

    def step_pass(self, pairs, hop):
        plan = self.plan
        for i, j in pairs:
            _, _, second = reduce_places(plan, j)
            up = both(plan.c == hop, plan.c < j) if hop < j else None
            down = both(plan.c == plan.ctx - 1 - hop, plan.c > j) if plan.ctx - 1 - hop > j else None
            for cond in (up, down):
                if cond is not None and not plan.draining:

                    @pl.when(cond)
                    def _(i=i, j=j, second=second):
                        plan.arrive(self.last[i].at[j], self.last_sem.at[i, j])
                        add_rows(
                            self.own[i].at[j, second],
                            [self.own[i].at[j, second], self.last[i].at[j]],
                        )

            self.send_last(i, j, second, up, down)

    def finish(self):
        plan = self.plan
        for i in range(3):
            count = self.outs[i].shape[0]
            rows = chunk_rows(count)
            slots = ((plan.c > 0, plan.c), (plan.c < plan.ctx - 1, plan.ctx))
            for there, slot in slots:
                plan.arrive(self.last[i].at[slot], self.last_sem.at[i, slot], there)

            def body(t, carry, i=i, rows=rows):
                at = pl.ds(pl.multiple_of(t * rows, rows), rows)
                for j in range(plan.ctx):
                    _, _, second = reduce_places(plan, j)

                    @pl.when(plan.c == j)
                    def _(j=j, second=second):
                        total = self.own[i][j, second, at, :].astype(F32)
                        if j > 0:
                            total = total + self.last[i][j, at, :].astype(F32)
                        if j < plan.ctx - 1:
                            total = total + self.last[i][plan.ctx, at, :].astype(F32)
                        self.outs[i][at, :] = total

                return carry

            lax.fori_loop(0, count // rows, body, 0)


def backward_kernel(
    fsdp, ctx,
    d_out, x_in, q_in, k_in, vm_in, kt_in, att_in, lse, wqkv_in, gain, table_in, start,
    dg_two, s_wo, s_gu, s_wd, early,
    folded, vout, g_wo, g_gu, g_wd, g_qkv, dg_all,
    part, q, k, vm, kt, att, do, wqkv, table,
    dqt, dkk, dvv, rows_t, d3, gw_full, gw,
    other, chain, gw_near, gw_sum, gw_last, dg, dg_near, dg_sum, dg_last,
    o_wo, o_gu, o_wd, n_wo, n_gu, n_wd, x_wo, x_gu, x_wd, l_wo, l_gu, l_wd,
    load_sem, do_sem, do_out, v_sem, v_out,
    sib_sem, sib_out, chain_sem, chain_out, end_sem, end_out,
    gw_sem, gw_out, gl_sem, gl_out, dn_sem, dn_out, dl_sem, dl_out,
    own_sem, near_sem, near_out, next_sem, next_out, last_sem, last_out,
):
    plan = Plan(fsdp, ctx)
    f, c, core, line, home, half = plan.f, plan.c, plan.core, plan.line, plan.home, plan.half
    lines = plan.lines
    sibling = (line * 2 + 1 - core, c)
    low, high = home * half, home * half + half - 1
    blocks, _, depth = part.shape
    group = blocks * BLOCK
    cols = vm.shape[1]
    heads = cols // HEAD
    tokens = group // ctx
    per = tokens // BLOCK
    pairs = blocks // 2
    plan.barrier()

    for i in range(half):
        for kk in range(2):
            to = core * half + i
            rank = lax.rem(to + kk * half, ctx)
            src = d_out.at[:, pl.ds(pl.multiple_of(rank * cols, cols), cols)]
            mine = both(core == home, c == to, core == kk)
            plan.send(
                src, do.at[c], do_out.at[i * 2 + kk], do_sem.at[c], (line * 2 + kk, to),
                jnp.logical_not(mine),
            )
            plan.keep(src, do.at[c], do_sem.at[c], mine)
    loads = (
        (q_in, q), (k_in, k), (vm_in, vm), (kt_in, kt), (att_in, att), (table_in, table),
        (wqkv_in, wqkv), (x_in, part),
    )
    for i, (src, dst) in enumerate(loads):
        plan.keep(src, dst, load_sem.at[i])
    reduction = Reduction(
        plan, (s_wo, s_gu, s_wd), early, (o_wo, o_gu, o_wd), (n_wo, n_gu, n_wd), (x_wo, x_gu, x_wd),
        (l_wo, l_gu, l_wd), (g_wo, g_gu, g_wd),
        (own_sem, near_sem, near_out, next_sem, next_out, last_sem, last_out),
    )
    reduction.start_early()
    reduction.start(reduction.second_set)
    reduction.start(reduction.third_set)

    dqt[...] = jnp.zeros_like(dqt)
    dkk[...] = jnp.zeros_like(dkk)
    dvv[...] = jnp.zeros_like(dvv)
    gw_full[...] = jnp.zeros_like(gw_full)
    dg[...] = jnp.zeros_like(dg)
    dg[1:2, :] = dg_two[0:1, :]
    for i, (src, dst) in enumerate(loads):
        plan.arrive(dst, load_sem.at[i])
    for j in range(ctx):
        plan.arrive(do.at[j], do_sem.at[j])

    def grads_of(b):
        return do[b // per, pl.ds(pl.multiple_of(lax.rem(b, per) * BLOCK, BLOCK), BLOCK), :]

    def dots(b, carry):
        rows = pl.ds(pl.multiple_of(b * BLOCK, BLOCK), BLOCK)
        prod = grads_of(b).astype(F32) * att[rows, :]
        upper = prod.astype(BF16)
        lower = (prod - upper.astype(F32)).astype(BF16)
        head_row = lax.broadcasted_iota(jnp.int32, (8, cols), 0)
        lane = lax.broadcasted_iota(jnp.int32, (8, cols), 1)
        choose = (lane // HEAD == head_row).astype(F32).astype(BF16)
        rows_t[:, rows] = nt(choose, upper) + nt(choose, lower)
        return carry

    lax.fori_loop(0, blocks, dots, 0)

    def tile(kb, qb):
        krows = pl.ds(pl.multiple_of(kb * BLOCK, BLOCK), BLOCK)
        rows = pl.ds(pl.multiple_of(qb * BLOCK, BLOCK), BLOCK)
        kv = k[krows, :]
        vv = vm[krows, :]
        qv = q[rows, :]
        dov = grads_of(qb)
        key_pos = kb * BLOCK + lax.broadcasted_iota(jnp.int32, (BLOCK, BLOCK), 0)
        query_pos = qb * BLOCK + lax.broadcasted_iota(jnp.int32, (BLOCK, BLOCK), 1)
        allowed = (key_pos <= query_pos) & (key_pos >= start[0:1, rows])
        dk_sum = dkk[krows, :]
        dv_sum = dvv[krows, :]
        for head in range(heads):
            band = slice(head * HEAD, (head + 1) * HEAD)
            lanes = head_lanes(qv.shape, head)
            qm = jnp.where(lanes, qv, jnp.zeros_like(qv))
            dom = jnp.where(lanes, dov, jnp.zeros_like(dov))
            s = jnp.where(allowed, nt(kv, qm), NEGATIVE)
            p = jnp.exp(s - lse[head : head + 1, rows])
            ds = (p * (nt(vv, dom) - rows_t[head : head + 1, rows])).astype(BF16)
            dv_sum = dv_sum + nn(p.astype(BF16), dom)
            dk_sum = dk_sum + nn(ds, qm)
            dqt[band, rows] = dqt[band, rows] + nn(kt[band, krows], ds)
        dkk[krows, :] = dk_sum
        dvv[krows, :] = dv_sum

    def unit_of(t):
        return jnp.where(home == 0, blocks - 1 - t, t)

    def finish(o):
        rows = pl.ds(pl.multiple_of(o * BLOCK, BLOCK), BLOCK)
        cos_v, sin_v = turns(table[rows, :], cols)
        dq = dqt[:, rows].T * (1.0 / math.sqrt(HEAD))
        d3[rows, :cols] = (dq * cos_v - half_swap(dq) * sin_v).astype(BF16)
        dk = dkk[rows, :]
        d3[rows, cols : 2 * cols] = (dk * cos_v - half_swap(dk) * sin_v).astype(BF16)
        d3[rows, 2 * cols :] = (0.5 * dvv[rows, :]).astype(BF16)
        dh = nt(d3[rows, :], wqkv[...])
        xv = part[o].astype(F32)
        rstd = lax.rsqrt(jnp.mean(xv * xv, axis=1, keepdims=True) + EPSILON)
        xhat = xv * rstd
        h1 = (xhat * gain[...]).astype(BF16)
        u = dh * gain[...]
        part[o] = (rstd * (u - xhat * jnp.mean(u * xhat, axis=1, keepdims=True))).astype(BF16)
        dg[0:1, :] = dg[0:1, :] + jnp.sum(dh * xhat, axis=0, keepdims=True)
        gw_full[...] = gw_full[...] + tn(h1, d3[rows, :])

    def give(t):
        o = unit_of(t)
        slot = t // 2
        plan.send(
            part.at[o], other.at[slot], sib_out.at[slot], sib_sem.at[slot], sibling,
            lax.rem(o, 2) != core,
        )

    def pair_unit(i):
        return jnp.where(home == 0, blocks - 2 - 2 * i, 2 * i) + core

    def add_unit(o, src):
        def body(t, carry):
            at = pl.ds(pl.multiple_of(t * 32, 32), 32)
            part[o, at, :] = (part[o, at, :].astype(F32) + src[at, :].astype(F32)).astype(BF16)
            return carry

        lax.fori_loop(0, BLOCK // 32, body, 0)

    def sum_pair(i):
        plan.arrive(other.at[i], sib_sem.at[i])
        if not plan.draining:
            add_unit(pair_unit(i), other.at[i])

    def pass_pair(i, hears):
        o = pair_unit(i)
        j = o // per
        top = jnp.minimum(j, high)
        bottom = jnp.maximum(j, low)
        from_below = both(c > low, c <= top)
        from_above = both(c < high, c >= bottom)
        now = jnp.logical_or(from_below, from_above) == hears
        spot = jnp.where(j == c, pairs, i)
        if hears and not plan.draining:

            @pl.when(from_below)
            def _():
                plan.arrive(chain.at[i], chain_sem.at[i])
                add_unit(o, chain.at[i])

            @pl.when(from_above)
            def _():
                plan.arrive(chain.at[spot], chain_sem.at[spot])
                add_unit(o, chain.at[spot])

        plan.send(
            part.at[o], chain.at[i], chain_out.at[0, i], chain_sem.at[i], (f, c + 1),
            both(now, c < top),
        )
        below = jnp.where(j == c - 1, pairs, i)
        plan.send(
            part.at[o], chain.at[below], chain_out.at[1, i], chain_sem.at[below], (f, c - 1),
            both(now, c > bottom),
        )
        end = jnp.clip(j, low, high)
        mine = both(c == end, j == c, core == home)
        where = lax.rem(o, per)
        dst = folded.at[pl.ds(pl.multiple_of(where * BLOCK, BLOCK), BLOCK), :]
        plan.send(
            part.at[o], dst, end_out.at[i], end_sem.at[where], (line * 2 + home, j),
            both(now, c == end, jnp.logical_not(mine)),
        )
        plan.keep(part.at[o], dst, end_sem.at[where], both(now, mine))

    rank = lax.rem(c + core * half, ctx)

    def give_values(i):
        j = jnp.where(home == 0, ctx - 1 - i, i)
        src = d3.at[pl.ds(pl.multiple_of(j * tokens, tokens), tokens), 2 * cols : 3 * cols]
        dst = vout.at[:, pl.ds(pl.multiple_of(rank * cols, cols), cols)]
        mine = both(core == home, c == j)
        plan.send(
            src, dst, v_out.at[i], v_sem.at[rank], (line * 2 + home, j), jnp.logical_not(mine)
        )
        plan.keep(src, dst, v_sem.at[rank], mine)

    schedule = {}
    schedule_first = []
    schedule_last = []

    def at_step(t, act):
        schedule.setdefault(t, []).append(act)

    scale = blocks // 8
    for kind, which, place in REDUCE_STEPS:
        pairs_of = getattr(reduction, which)
        if place < 0:
            schedule_first.append(functools.partial(getattr(reduction, kind), pairs_of))
            continue
        if kind != "step_pass":
            at_step(place * scale, functools.partial(getattr(reduction, kind), pairs_of))
            continue
        for hop in range(1, ctx - 1):
            act = functools.partial(reduction.step_pass, pairs_of, hop)
            when = place + PASS_GAP * (hop - 1)
            if when < 8 and hop < 3:
                at_step(when * scale, act)
            else:
                schedule_last.append(act)
    for i in range(pairs - 1):
        at_step(2 * i + 1, lambda i=i: give_values(i))
        at_step(2 * i + 2, lambda i=i: sum_pair(i))
        at_step(2 * i + 2, lambda i=i: pass_pair(i, False))
        if i < pairs - 2:
            at_step(2 * i + 4, lambda i=i: pass_pair(i, True))
    at_step(blocks - 1, lambda: give_values(pairs - 1))

    def step(t, carry):
        o = unit_of(t)

        def inner(i, carry2):
            tile(jnp.where(home == 0, i, o), jnp.where(home == 0, o, o + i))
            return carry2

        lax.fori_loop(0, blocks - t, inner, 0)
        finish(o)
        give(t)
        for s in sorted(schedule):

            @pl.when(t == s)
            def _(s=s):
                for act in schedule[s]:
                    act()

        return carry

    for act in schedule_first:
        act()
    kept = plan.started
    plan.started = []
    lax.fori_loop(0, blocks, step, 0)
    plan.started = kept

    for hop in range(1, fsdp):
        dev = (lax.rem(f + hop, fsdp), c)
        plan.send(dg, dg_near.at[f], dn_out.at[hop - 1], dn_sem.at[f], dev)
    plan.keep(dg, dg_near.at[f], dn_sem.at[f])

    pass_pair(pairs - 2, True)
    sum_pair(pairs - 1)
    pass_pair(pairs - 1, False)
    shard = depth // fsdp
    rows_each = BLOCK // shard

    def weight(b, carry):
        at = pl.ds(pl.multiple_of(b * BLOCK, BLOCK), BLOCK)
        val = gw_full[at, :].astype(BF16)
        for r in range(rows_each):
            gw[b * (rows_each // 2) + r // 2, r % 2] = val[r * shard : (r + 1) * shard]
        return carry

    lax.fori_loop(0, depth // BLOCK, weight, 0)
    for i in range(3):
        for hop in range(1, lines):
            to = lax.rem(line + hop, lines)
            plan.send(
                gw.at[to, :, :, pl.ds(i * cols, cols)],
                gw_near.at[hop - 1, :, :, pl.ds(i * cols, cols)],
                gw_out.at[i, hop - 1], gw_sem.at[i, hop - 1], (to * 2 + core, c),
            )
    pass_pair(pairs - 1, True)

    for at in range(fsdp):
        plan.arrive(dg_near.at[at], dn_sem.at[at])
    total = dg_near[0]
    for at in range(1, fsdp):
        total = total + dg_near[at]
    dg_sum[...] = total
    for hop in range(1, ctx):
        plan.send(
            dg_sum, dg_last.at[c], dl_out.at[hop - 1], dl_sem.at[c], (f, lax.rem(c + hop, ctx))
        )
    plan.keep(dg_sum, dg_last.at[c], dl_sem.at[c])

    plane = jnp.where(core == 0, c, lax.rem(c + half, ctx))
    for i in range(3):
        band = pl.ds(i * cols, cols)
        for hop in range(1, lines):
            plan.arrive(gw_near.at[hop - 1, :, :, band], gw_sem.at[i, hop - 1])
        for kk in range(2):
            add_rows(
                gw_sum.at[kk, :, band],
                [gw.at[line, kk, :, band]]
                + [gw_near.at[hop - 1, kk, :, band] for hop in range(1, lines)],
            )
            mine = both(core == 0, kk == 0)
            src, dst = gw_sum.at[kk, :, band], gw_last.at[core, :, band]
            plan.send(
                src, dst, gl_out.at[kk, i], gl_sem.at[core, i], (line * 2 + kk, plane),
                jnp.logical_not(mine),
            )
            plan.keep(src, dst, gl_sem.at[core, i], mine)

    for act in schedule_last:
        act()
    reduction.finish()
    for at in range(ctx):
        plan.arrive(dg_last.at[at], dl_sem.at[at])
    total = dg_last[0]
    for at in range(1, ctx):
        total = total + dg_last[at]
    dg_all[...] = total
    for kk in range(2):
        for i in range(3):
            plan.arrive(gw_last.at[kk, :, pl.ds(i * cols, cols)], gl_sem.at[kk, i])
    add_rows(g_qkv, [gw_last.at[0], gw_last.at[1]])
    for at in range(per):
        plan.arrive(folded.at[pl.ds(at * BLOCK, BLOCK), :], end_sem.at[at])
    for at in range(ctx):
        plan.arrive(vout.at[:, pl.ds(at * cols, cols)], v_sem.at[at])
    plan.drain()
    plan.draining = True
    for t in range(blocks):
        give(t)
    for s in sorted(schedule):
        for act in schedule[s]:
            act()


PASS_GAP = 1
REDUCE_STEPS = (
    ("step_near", "second_set", 0),
    ("step_next", "first_set", 0),
    ("step_near", "third_set", 1),
    ("step_next", "second_set", 2),
    ("step_pass", "first_set", 2),
    ("step_next", "third_set", 3),
    ("step_pass", "second_set", 4),
    ("step_pass", "third_set", 6),
)


def backward(mesh, d_out, x, q, k, vm, kt, att, lse, wqkv, gain, table, start, dg_two, sums):
    fsdp, ctx = mesh.shape["fsdp"], mesh.shape["ctx"]
    group, depth = x.shape
    cols = vm.shape[1]
    tokens = group // ctx
    blocks = group // BLOCK
    x = x.reshape(blocks, BLOCK, depth)
    pairs = blocks // 2
    half = ctx // 2
    lines = fsdp // 2
    side = math.isqrt(lines)
    shard = depth // fsdp
    s_wo, s_gu, s_wd, _ = sums
    shapes = (
        (s_wo.shape[1], s_wo.shape[2] // ctx),
        (s_gu.shape[2], s_gu.shape[3]),
        (s_wd.shape[1], s_wd.shape[2] // ctx),
    )
    anywhere = pl.BlockSpec(memory_space=pl.ANY)
    vmem = pl.BlockSpec(memory_space=pltpu.VMEM)
    dma = pltpu.SemaphoreType.DMA
    hops = max(side - 1, 1)

    def low(*shape):
        return pltpu.VMEM(shape, BF16)

    def full(*shape):
        return pltpu.VMEM(shape, F32)

    return pl.pallas_call(
        functools.partial(backward_kernel, fsdp, ctx),
        out_shape=(
            jax.ShapeDtypeStruct((tokens, depth), BF16),
            jax.ShapeDtypeStruct((tokens, depth), BF16),
            jax.ShapeDtypeStruct(shapes[0], F32),
            jax.ShapeDtypeStruct(shapes[1], F32),
            jax.ShapeDtypeStruct(shapes[2], F32),
            jax.ShapeDtypeStruct((shard, 3 * cols), F32),
            jax.ShapeDtypeStruct((8, depth), F32),
        ),
        in_specs=[anywhere] * 7 + [vmem, anywhere, vmem] + [anywhere] + [vmem] * 2 + [anywhere] * 4,
        out_specs=[anywhere] * 2 + [vmem] * 5,
        scratch_shapes=[
            low(blocks, BLOCK, depth), low(group, cols), low(group, cols), low(group, cols),
            low(cols, group), full(group, cols), low(ctx, tokens, cols), low(depth, 3 * cols),
            full(group, table.shape[1]),
            full(cols, group), full(group, cols), full(group, cols),
            full(8, group), low(group, 3 * cols), full(depth, 3 * cols), low(lines, 2, shard, 3 * cols),
            low(pairs, BLOCK, depth), low(pairs + 1, BLOCK, depth),
            low(max(lines - 1, 1), 2, shard, 3 * cols), low(2, shard, 3 * cols),
            low(2, shard, 3 * cols),
            full(8, depth), full(fsdp, 8, depth), full(8, depth), full(ctx, 8, depth),
        ]
        + [low(ctx, side, *shape) for shape in shapes]
        + [low(ctx, hops, side, *shape) for shape in shapes]
        + [low(ctx, hops, *shape) for shape in shapes]
        + [low(ctx + 1, *shape) for shape in shapes]
        + [
            dma((8,)), dma((ctx,)), dma((ctx,)), dma((ctx,)), dma((ctx,)),
            dma((pairs,)), dma((pairs,)), dma((pairs + 1,)), dma((2, pairs)),
            dma((tokens // BLOCK,)), dma((pairs,)),
            dma((3, lines)), dma((3, lines)), dma((2, 3)), dma((2, 3)),
            dma((fsdp,)), dma((fsdp,)), dma((ctx,)), dma((ctx,)),
            dma((3, ctx, side)), dma((3, ctx, hops, side)), dma((3, ctx, hops, side)),
            dma((3, ctx, hops)), dma((3, ctx, hops)), dma((3, ctx + 1)), dma((3, ctx)),
        ],
        compiler_params=pltpu.CompilerParams(
            collective_id=3, has_side_effects=True, vmem_limit_bytes=BACKWARD_LIMIT
        ),
        name="backward",
    )(d_out, x, q, k, vm, kt, att, lse, wqkv, gain, table, start, dg_two, *sums)


def layer(
    mesh, tokens, value_first, lengths, w_query, w_key, w_value, w_out, w_gate, w_up, w_down,
    gain_attn, gain_ffn, out_grad, value_grad,
):
    fsdp, ctx = mesh.shape["fsdp"], mesh.shape["ctx"]
    count, depth = tokens.shape
    group = count * ctx
    cols = depth // ctx
    rows = depth // fsdp
    f, c = lax.axis_index("fsdp"), lax.axis_index("ctx")
    small = jnp.stack([gain_attn, gain_ffn]).astype(BF16).astype(F32)
    small = lax.dynamic_update_slice(
        jnp.zeros((8, depth), F32), small, (jnp.int32(0), (f * rows).astype(jnp.int32))
    )
    small = lax.dynamic_update_slice(small, lengths.astype(F32), (2, 0))
    (
        attended, wos, gus, wds, xs, q, k, vm, kt, att, wq, lse, table, first, gains
    ) = forward(
        mesh, tokens, value_first, (w_query, w_key, w_value, w_out, w_gate, w_up, w_down), small
    )
    gain_one, gain_two = gains[0:1], gains[1:2]
    wq = wq.reshape(depth, 3 * cols)
    result, dx2, d_out, dg_two, *sums = feed_forward(
        mesh, attended, tokens, out_grad, wos.reshape(depth, depth), gain_two,
        gus.reshape(ctx, depth, -1), wds.reshape(-1, depth),
    )
    folded, dvr, g_wo, g_gu, g_wd, g_qkv, gain_grads = backward(
        mesh, d_out, xs.reshape(group, depth), q, k, vm, kt, att, lse, wq, gain_one, table, first, dg_two,
        sums,
    )
    gain_grads = lax.dynamic_slice(
        gain_grads, (jnp.int32(0), (f * rows).astype(jnp.int32)), (2, rows)
    )
    ff = w_gate.shape[1]
    return (
        result,
        dx2 + folded.astype(F32),
        value_grad + dvr.astype(F32),
        g_qkv[:, :cols],
        g_qkv[:, cols : 2 * cols],
        g_qkv[:, 2 * cols :],
        g_wo,
        g_gu[:, :ff],
        g_gu[:, ff:],
        g_wd,
        gain_grads[0],
        gain_grads[1],
    )


def solution(mesh):
    rows = P(("fsdp", "ctx"), None)
    shard = P("fsdp", "ctx")
    return jax.shard_map(
        functools.partial(layer, mesh),
        mesh=mesh,
        in_specs=(rows, rows, P("fsdp", None)) + (shard,) * 7 + (P("fsdp"),) * 2 + (rows, rows),
        out_specs=(rows, rows, rows) + (shard,) * 7 + (P("fsdp"),) * 2,
        check_vma=False,
    )
```

```python
import functools
import math

import jax
import jax.numpy as jnp
from jax import lax
from jax.experimental import pallas as pl
from jax.experimental.pallas import tpu as pltpu
from jax.sharding import PartitionSpec as P

HEAD = 64
EPSILON = 1e-05
THETA = 10000.0
NEGATIVE = -1e30
BLOCK = 256
VMEM_LIMIT = 58 * 1024 * 1024
BACKWARD_LIMIT = 58 * 1024 * 1024
MESH = pl.DeviceIdType.MESH
BF16 = jnp.bfloat16
F32 = jnp.float32


def nn(left, right):
    return lax.dot_general(left, right, (((1,), (0,)), ((), ())), preferred_element_type=F32)


def nt(left, right):
    return lax.dot_general(left, right, (((1,), (1,)), ((), ())), preferred_element_type=F32)


def tn(left, right):
    return lax.dot_general(left, right, (((0,), (0,)), ((), ())), preferred_element_type=F32)


def turns(table, width):
    lane = lax.broadcasted_iota(jnp.int32, table.shape, 1)
    swapped = pltpu.roll(table, HEAD, 1)
    cos = jnp.where(lane < HEAD, table, swapped)
    sin = jnp.where(lane < HEAD, swapped, table)
    times = width // table.shape[1]
    return jnp.concatenate([cos] * times, axis=1), jnp.concatenate([sin] * times, axis=1)


def half_swap(rows):
    width = rows.shape[1]
    lane = lax.broadcasted_iota(jnp.int32, rows.shape, 1)
    low = lax.rem(lane, HEAD) < HEAD // 2
    return jnp.where(
        low,
        pltpu.roll(rows, width - HEAD // 2, 1),
        pltpu.roll(rows, HEAD // 2, 1),
    )


def head_lanes(shape, head):
    lane = lax.broadcasted_iota(jnp.int32, shape, 1)
    return (lane >= head * HEAD) & (lane < (head + 1) * HEAD)


def early_chunks(ctx):
    return max(ctx // 2, 1)


class Plan:
    def __init__(self, fsdp, ctx):
        self.fsdp, self.ctx = fsdp, ctx
        self.lines = fsdp // 2
        self.across = math.isqrt(self.lines)
        self.along = self.lines // self.across
        self.half = ctx // 2
        self.early = early_chunks(ctx)
        self.f = lax.axis_index("fsdp")
        self.c = lax.axis_index("ctx")
        self.core = lax.rem(self.f, 2)
        self.line = self.f // 2
        self.a = self.line // self.along
        self.b = lax.rem(self.line, self.along)
        self.home = self.c // self.half
        self.started = []
        self.draining = False

    def barrier(self):
        sem = pltpu.get_barrier_semaphore()
        count = 0
        for step in range(1, self.fsdp):
            dev = (lax.rem(self.f + step, self.fsdp), self.c)
            pl.semaphore_signal(sem, inc=1, device_id=dev, device_id_type=MESH)
            count += 1
        for step in range(1, self.ctx):
            for core in range(2):
                dev = (self.line * 2 + core, lax.rem(self.c + step, self.ctx))
                pl.semaphore_signal(sem, inc=1, device_id=dev, device_id_type=MESH)
                count += 1
        pl.semaphore_wait(sem, count)

    def greet_plane(self):
        sem = pltpu.get_barrier_semaphore()
        for step in range(1, self.fsdp):
            dev = (lax.rem(self.f + step, self.fsdp), self.c)
            pl.semaphore_signal(sem, inc=1, device_id=dev, device_id_type=MESH)
        pl.semaphore_wait(sem, self.fsdp - 1)

    def when(self, cond, act):
        if cond is True:
            act()
        else:
            pl.when(cond)(act)

    def send(self, src, dst, send_sem, recv_sem, dev, cond=True):
        def copy():
            return pltpu.make_async_remote_copy(
                src_ref=src, dst_ref=dst, send_sem=send_sem, recv_sem=recv_sem,
                device_id=dev, device_id_type=MESH,
            )

        if self.draining:
            self.when(cond, lambda: copy().wait_send())
            return
        self.when(cond, lambda: copy().start())
        self.started.append((cond, lambda: copy().wait_send()))

    def keep(self, src, dst, sem, cond=True):
        if self.draining:
            return
        self.when(cond, lambda: pltpu.make_async_copy(src, dst, sem).start())

    def arrive(self, dst, sem, cond=True):
        if self.draining:
            return
        self.when(cond, lambda: pltpu.make_async_copy(dst, dst, sem).wait())

    def drain(self):
        for cond, act in self.started:
            self.when(cond, act)
        self.started = []


def both(*conds):
    out = True
    for cond in conds:
        if cond is not True:
            out = cond if out is True else jnp.logical_and(out, cond)
    return out


class Gathering:
    def __init__(self, plan, own, whole, sems):
        self.plan, self.own, self.whole = plan, own, whole
        self.sem, self.z_out, self.p_out, self.s_out = sems
        self.widths = (own[0].shape[1], None, own[2].shape[1])

    def spots(self, row, j):
        wos, gus, wds = self.whole

        def band(width):
            return pl.ds(pl.multiple_of(j * width, width), width)

        return (
            wos.at[row, :, band(self.widths[0])], gus.at[j, row], wds.at[row, :, band(self.widths[2])],
        )

    def along_ctx(self, srcs, j, cond, up, down, items=(0, 1, 2)):
        plan = self.plan
        dsts = self.spots(plan.f, j)
        for i in items:
            if up:
                plan.send(
                    srcs[i], dsts[i], self.z_out.at[i, 0, j], self.sem.at[i, plan.f, j],
                    (plan.f, plan.c + 1), both(cond, plan.c < plan.ctx - 1),
                )
            if down:
                plan.send(
                    srcs[i], dsts[i], self.z_out.at[i, 1, j], self.sem.at[i, plan.f, j],
                    (plan.f, plan.c - 1), both(cond, plan.c > 0),
                )

    def on_plane(self, srcs, row, line, j, cond, over_a, over_b, items=(0, 1, 2)):
        plan = self.plan
        dsts = self.spots(row, j)
        for i in items:
            if over_a is not False:
                for hop in range(1, plan.across):
                    to = (lax.rem(plan.a + hop, plan.across) * plan.along + plan.b) * 2 + plan.core
                    plan.send(
                        srcs[i], dsts[i], self.p_out.at[i, hop - 1, line, j],
                        self.sem.at[i, row, j], (to, plan.c), both(cond, over_a),
                    )
            if over_b is not False:
                for hop in range(1, plan.along):
                    to = (plan.a * plan.along + lax.rem(plan.b + hop, plan.along)) * 2 + plan.core
                    plan.send(
                        srcs[i], dsts[i], self.p_out.at[i, plan.across + hop - 2, line, j],
                        self.sem.at[i, row, j], (to, plan.c), both(cond, over_b),
                    )
            plan.send(
                srcs[i], dsts[i], self.s_out.at[i, line, j], self.sem.at[i, row, j],
                (plan.line * 2 + 1 - plan.core, plan.c), cond,
            )

    def near(self, dist):
        plan = self.plan
        for side in range(2 if dist else 1):
            j = plan.c - dist if side == 0 else plan.c + dist
            there = True if dist == 0 else (j >= 0 if side == 0 else j < plan.ctx)
            yield jnp.clip(j, 0, plan.ctx - 1), there, side

    def start_ctx(self):
        self.along_ctx(self.own, self.plan.c, True, True, True)

    def start_plane(self):
        plan = self.plan
        self.on_plane(self.own, plan.f, plan.line, plan.c, True, True, True)
        for src, dst, i in zip(self.own, self.spots(plan.f, plan.c), range(3)):
            plan.keep(src, dst, self.sem.at[i, plan.f, plan.c])

    def wait(self, row, j, cond=True, items=(0, 1, 2)):
        dsts = self.spots(row, j)
        for i in items:
            self.plan.arrive(dsts[i], self.sem.at[i, row, j], cond)
        return dsts

    def from_ctx(self, dist):
        plan = self.plan
        for j, there, side in self.near(dist):
            for i in ORDER:
                dsts = self.wait(plan.f, j, there, (i,))
                self.along_ctx(dsts, j, there, side == 0, side == 1, (i,))
                self.on_plane(dsts, plan.f, plan.line, j, there, True, True, (i,))

    def from_plane(self, dist):
        plan = self.plan
        for j, there, _ in self.near(dist):
            first = j < plan.half
            for hop in range(1, plan.across):
                line = lax.rem(plan.a + plan.across - hop, plan.across) * plan.along + plan.b
                row = line * 2 + plan.core
                for i in ORDER:
                    dsts = self.wait(row, j, there, (i,))
                    self.on_plane(dsts, row, line, j, there, False, first, (i,))
            for hop in range(1, plan.along):
                line = plan.a * plan.along + lax.rem(plan.b + plan.along - hop, plan.along)
                row = line * 2 + plan.core
                for i in ORDER:
                    dsts = self.wait(row, j, there, (i,))
                    self.on_plane(
                        dsts, row, line, j, there, jnp.logical_not(first), False, (i,)
                    )

    def from_far(self, dist):
        plan = self.plan
        for j, there, _ in self.near(dist):
            for hop in range(1, plan.across):
                for hop2 in range(1, plan.along):
                    line = lax.rem(plan.a + hop, plan.across) * plan.along + lax.rem(
                        plan.b + hop2, plan.along
                    )
                    row = line * 2 + plan.core
                    for i in ORDER:
                        dsts = self.wait(row, j, there, (i,))
                        self.on_plane(dsts, row, line, j, there, False, False, (i,))

    def finish(self):
        plan = self.plan
        self.wait(plan.f, plan.c)

        def other(line, carry):
            for j in range(plan.ctx):
                self.wait(line * 2 + 1 - plan.core, j)
            return carry

        lax.fori_loop(0, plan.lines, other, 0)


def forward_kernel(
    fsdp, ctx,
    x, vf, m_q, m_k, m_v, m_o, m_g, m_u, m_d, small,
    attended, wos, gus, wds, x_out_ref, q_ref, k_ref, vm_ref, kt_ref, att_ref, wq_ref,
    lse, table, start, gain,
    xs, vs, wq, wqh, own_q, own_o, own_g, own_d, gs, q, k, vm, kt, vt, att, out, acc, mx, tot,
    x_sem, x_out, v_sem, v_out, q_sem, q_out, h_sem, g_sem, g_out,
    w_sem, w_z, w_p, w_s, o_sem, o_out, save_sem,
    w_q, w_k, w_v, w_o, w_g, w_u, w_d, m_sem,
):
    masters = (m_q, m_k, m_v, m_o, m_g, m_u, m_d)
    plan = Plan(fsdp, ctx)
    f, c, core, line, home, half = plan.f, plan.c, plan.core, plan.line, plan.home, plan.half
    tokens, depth = x.shape
    group = tokens * ctx
    cols = depth // ctx
    heads = cols // HEAD
    blocks = group // BLOCK
    per = tokens // BLOCK
    owner = core == home
    away = jnp.logical_not(owner)
    sibling = (line * 2 + 1 - core, c)

    fetched = (w_q, w_k, w_v, w_o, w_g, w_u, w_d)
    for i, (src, dst) in enumerate(zip(masters, fetched)):
        plan.keep(src, dst, m_sem.at[i])
    for i in range(3):
        plan.arrive(fetched[i], m_sem.at[i])
    own_q[...] = jnp.concatenate(
        [w_q[...].astype(BF16), w_k[...].astype(BF16), w_v[...].astype(BF16)], axis=1
    )
    plan.barrier()
    gathering = Gathering(
        plan, (own_o, own_g, own_d), (wos, gus, wds), (w_sem, w_z, w_p, w_s)
    )

    for hop in range(1, fsdp):
        plan.send(small, gs.at[f], g_out.at[hop - 1], g_sem.at[f], (lax.rem(f + hop, fsdp), c))
    plan.keep(small, gs.at[f], g_sem.at[f])
    plan.send(own_q, wqh, h_sem.at[0], h_sem.at[1], (f, lax.rem(c + half, ctx)))

    piece = tokens // PIECES

    def part_of(ref, i):
        return ref.at[pl.ds(i * piece, piece), :]

    def spread_x(src, j, i, below, above, cond):
        dst = part_of(xs.at[j], i)
        if below:
            plan.send(
                src, dst, x_out.at[0, j, i], x_sem.at[j, i], (f, c - 1),
                both(cond, c > home * half),
            )
        if above:
            plan.send(
                src, dst, x_out.at[1, j, i], x_sem.at[j, i], (f, c + 1),
                both(cond, c < home * half + half - 1),
            )
        plan.send(src, dst, x_out.at[2, j, i], x_sem.at[j, i], sibling, cond)

    entry = jnp.where(core == 0, half - 1, half)
    for i in range(PIECES):
        src = part_of(x, i)
        plan.send(
            src, part_of(xs.at[c], i), x_out.at[0, c, i], x_sem.at[c, i], (f, entry), away
        )
        spread_x(src, c, i, True, True, owner)
        plan.keep(src, part_of(xs.at[c], i), x_sem.at[c, i], owner)
    for at in range(plan.lines):
        plan.send(
            own_q, wq.at[f], q_out.at[0, at], q_sem.at[f], (at * 2, c),
            jnp.logical_not(f == at * 2),
        )
    plan.keep(own_q, wq.at[f], q_sem.at[f], core == 0)
    for i in range(half):
        for kk in range(2):
            to = core * half + i
            rank = lax.rem(to + kk * half, ctx)
            src = vf.at[:, pl.ds(pl.multiple_of(rank * cols, cols), cols)]
            mine = both(owner, c == to, core == kk)
            plan.send(
                src, vs.at[c], v_out.at[i, kk], v_sem.at[c], (line * 2 + kk, to),
                jnp.logical_not(mine),
            )
            plan.keep(src, vs.at[c], v_sem.at[c], mine)
    for i in range(3, 7):
        plan.arrive(fetched[i], m_sem.at[i])
    own_o[...] = w_o[...].astype(BF16)
    own_g[...] = jnp.concatenate([w_g[...].astype(BF16), w_u[...].astype(BF16)], axis=1)
    own_d[...] = w_d[...].astype(BF16)

    for row in range(fsdp):
        plan.arrive(gs.at[row], g_sem.at[row])
    total = gs[0]
    for row in range(1, fsdp):
        total = total + gs[row]
    gain[...] = total
    lens = gs[line * 2 + home]
    doc_count = SHORTS_AND_LONG

    def firsts(places):
        end = jnp.zeros((1, 1), F32)
        first = jnp.zeros(places.shape, F32)
        for d in range(doc_count):
            size = lens[2:3, d : d + 1]
            end = end + size
            first = first + jnp.where(places >= end, size, 0.0)
        return first

    places = lax.broadcasted_iota(jnp.int32, (1, group), 1).astype(F32)
    start[...] = firsts(places).astype(jnp.int32)

    def angles(b, carry):
        rows = pl.ds(pl.multiple_of(b * BLOCK, BLOCK), BLOCK)
        at = (b * BLOCK + lax.broadcasted_iota(jnp.int32, (BLOCK, 128), 0)).astype(F32)
        lane = lax.broadcasted_iota(jnp.int32, (BLOCK, 128), 1)
        pair = lax.rem(lane, HEAD // 2).astype(F32)
        angle = (at - firsts(at)) * jnp.exp(pair * (-2.0 * math.log(THETA) / HEAD))
        sine = jnp.sin(angle)
        table[rows, :] = jnp.where(
            lane < HEAD, jnp.cos(angle), jnp.where(lane < HEAD + HEAD // 2, -sine, sine)
        )
        return carry

    lax.fori_loop(0, blocks, angles, 0)

    plan.arrive(wqh, h_sem.at[1])
    for at in range(plan.lines):
        plan.send(
            wqh, wq.at[f], q_out.at[1, at], q_sem.at[f], (at * 2 + 1, c),
            jnp.logical_not(f == at * 2 + 1),
        )
    plan.keep(wqh, wq.at[f], q_sem.at[f], core == 1)
    gathering.start_plane()

    def project(j):
        def body(i, carry):
            rows = pl.ds(pl.multiple_of(j * tokens + i * BLOCK, BLOCK), BLOCK)
            xv = xs[j, pl.ds(pl.multiple_of(i * BLOCK, BLOCK), BLOCK), :].astype(F32)
            rstd = lax.rsqrt(jnp.mean(xv * xv, axis=1, keepdims=True) + EPSILON)
            hv = (xv * rstd * gain[0:1, :]).astype(BF16)
            raw = nn(hv, wq[...].reshape(depth, 3 * cols))
            cos_v, sin_v = turns(table[rows, :], cols)
            rq = raw[:, :cols]
            rk = raw[:, cols : 2 * cols]
            qv = (rq * cos_v + half_swap(rq) * sin_v).astype(BF16)
            q[rows, :] = (qv.astype(F32) * (1.0 / math.sqrt(HEAD))).astype(BF16)
            kv = (rk * cos_v + half_swap(rk) * sin_v).astype(BF16)
            k[rows, :] = kv
            kt[:, rows] = kv.T
            att[rows, :] = 0.5 * raw[:, 2 * cols :]
            return carry

        lax.fori_loop(0, per, body, 0)

    def actions(place):
        out = [gathering.start_ctx] if place == START else []
        for kind in ("from_ctx", "from_plane", "from_far"):
            for dist in range(ctx):
                if (kind, dist) != ("from_ctx", 0) and place == spot_of(kind, dist, ctx, blocks):
                    out.append(functools.partial(getattr(gathering, kind), dist))
        return out

    for dist in range(ctx):
        for i in range(PIECES):
            for j, there, side in gathering.near(dist):
                spot = part_of(xs.at[j], i)
                plan.arrive(spot, x_sem.at[j, i], there)
                if dist:
                    spread_x(spot, j, i, side == 1, side == 0, both(owner, there))
        for act in actions(("x", dist)):
            act()
    for row in range(fsdp):
        plan.arrive(wq.at[row], q_sem.at[row])
    for act in actions("q"):
        act()
    for j in range(ctx):
        project(j)
    for act in actions("p"):
        act()
    saves = [(xs, x_out_ref), (q, q_ref), (k, k_ref), (kt, kt_ref), (wq, wq_ref)]
    for i, (src, dst) in enumerate(saves):
        plan.keep(src, dst, save_sem.at[i])
    for j in range(ctx):
        plan.arrive(vs.at[j], v_sem.at[j])

    def mix(b, carry):
        rows = pl.ds(pl.multiple_of(b * BLOCK, BLOCK), BLOCK)
        first = vs[b // per, pl.ds(pl.multiple_of(lax.rem(b, per) * BLOCK, BLOCK), BLOCK), :]
        mixed = (att[rows, :] + 0.5 * first.astype(F32)).astype(BF16)
        vm[rows, :] = mixed
        vt[:, rows] = mixed.T
        return carry

    lax.fori_loop(0, blocks, mix, 0)
    plan.keep(vm, vm_ref, save_sem.at[5])

    rank = lax.rem(c + core * half, ctx)

    def give(b):
        j = b // per
        where = lax.rem(b, per)
        src = out.at[pl.ds(pl.multiple_of(b * BLOCK, BLOCK), BLOCK), :]
        dst = attended.at[
            pl.ds(pl.multiple_of(where * BLOCK, BLOCK), BLOCK),
            pl.ds(pl.multiple_of(rank * cols, cols), cols),
        ]
        mine = both(owner, c == j)
        plan.send(
            src, dst, o_out.at[b], o_sem.at[rank, where], (line * 2 + home, j),
            jnp.logical_not(mine),
        )
        plan.keep(src, dst, o_sem.at[rank, where], mine)

    schedule = {}

    def at_step(t, act):
        schedule.setdefault(min(t, blocks - 1), []).append(act)

    for place in range(blocks):
        for act in actions(("t", place)):
            at_step(place, act)

    def unit(t, carry):
        b = blocks - 1 - t
        rows = pl.ds(pl.multiple_of(b * BLOCK, BLOCK), BLOCK)
        acc[...] = jnp.zeros_like(acc)
        mx[...] = jnp.full_like(mx, NEGATIVE)
        tot[...] = jnp.zeros_like(tot)
        qv = q[rows, :]
        first = start[0:1, rows]

        def keys(kb, inner):
            krows = pl.ds(pl.multiple_of(kb * KEYS, KEYS), KEYS)
            kv = k[krows, :]
            key_pos = kb * KEYS + lax.broadcasted_iota(jnp.int32, (KEYS, BLOCK), 0)
            query_pos = b * BLOCK + lax.broadcasted_iota(jnp.int32, (KEYS, BLOCK), 1)
            allowed = (key_pos <= query_pos) & (key_pos >= first)
            for head in range(heads):
                band = slice(head * HEAD, (head + 1) * HEAD)
                qm = jnp.where(head_lanes(qv.shape, head), qv, jnp.zeros_like(qv))
                s = jnp.where(allowed, nt(kv, qm), NEGATIVE)
                old = mx[head : head + 1, :]
                new = jnp.maximum(old, jnp.max(s, axis=0, keepdims=True))
                p = jnp.exp(s - new)
                shrink = jnp.exp(old - new)
                mx[head : head + 1, :] = new
                tot[head : head + 1, :] = tot[head : head + 1, :] * shrink + jnp.sum(
                    p, axis=0, keepdims=True
                )
                acc[band, :] = acc[band, :] * shrink + nn(vt[band, krows], p.astype(BF16))
            return inner

        lax.fori_loop(0, b // (KEYS // BLOCK) + 1, keys, 0)
        for head in range(heads):
            band = slice(head * HEAD, (head + 1) * HEAD)
            acc[band, :] = acc[band, :] / tot[head : head + 1, :]
        ov = acc[...].T
        att[rows, :] = ov
        out[rows, :] = ov.astype(BF16)
        lse[:, rows] = mx[...] + jnp.log(tot[...])
        give(b)
        for s in sorted(schedule):

            @pl.when(t == s)
            def _(s=s):
                for act in schedule[s]:
                    act()

        return carry

    kept = plan.started
    plan.started = []
    lax.fori_loop(0, blocks, unit, 0)
    plan.started = kept
    plan.keep(att, att_ref, save_sem.at[6])
    for act in actions("late"):
        act()
    gathering.finish()
    for at in range(ctx):
        for where in range(per):
            plan.arrive(
                attended.at[pl.ds(where * BLOCK, BLOCK), pl.ds(at * cols, cols)],
                o_sem.at[at, where],
            )
    for i, (src, dst) in enumerate(saves + [(vm, vm_ref), (att, att_ref)]):
        plan.arrive(dst, save_sem.at[i])
    plan.drain()
    plan.draining = True
    for b in range(blocks):
        give(b)
    for s in sorted(schedule):
        for act in schedule[s]:
            act()


ORDER = (0, 1, 2)
PIECES = 4
START = ('x', 0)
SHORTS_AND_LONG = 4
KEYS = 512
SPOTS = {
    "from_ctx": (None, ('x', 2), ('x', 3), ('t', 0)),
    "from_plane": (('x', 2), ('x', 3), ('t', 0), ('t', 3)),
    "from_far": (('t', 0), ('t', 2), ('t', 5), 'late'),
}


def spot_of(kind, dist, ctx, blocks):
    if dist >= 4:
        return "p" if kind == "from_ctx" else "late"
    spot = SPOTS[kind][dist]
    return ("t", spot[1] * (blocks // 8)) if spot[0] == "t" else spot


def forward(mesh, x, vf, weights, small):
    fsdp, ctx = mesh.shape["fsdp"], mesh.shape["ctx"]
    tokens, depth = x.shape
    cols = depth // ctx
    group = tokens * ctx
    blocks = group // BLOCK
    per = tokens // BLOCK
    lines = fsdp // 2
    across = math.isqrt(lines)
    peers = max(across - 1 + lines // across - 1, 1)
    shard = depth // fsdp
    out_shape = weights[3].shape
    up_shape = (weights[4].shape[0], 2 * weights[4].shape[1])
    down_shape = weights[6].shape
    anywhere = pl.BlockSpec(memory_space=pl.ANY)
    vmem = pl.BlockSpec(memory_space=pltpu.VMEM)
    dma = pltpu.SemaphoreType.DMA

    def low(*shape):
        return pltpu.VMEM(shape, BF16)

    def full(*shape):
        return pltpu.VMEM(shape, F32)

    def array(dtype, *shape):
        return jax.ShapeDtypeStruct(shape, dtype)

    return pl.pallas_call(
        functools.partial(forward_kernel, fsdp, ctx),
        out_shape=(
            array(BF16, tokens, depth),
            array(BF16, fsdp, out_shape[0], depth),
            array(BF16, ctx, fsdp, *up_shape),
            array(BF16, fsdp, down_shape[0], depth),
            array(BF16, ctx, tokens, depth),
            array(BF16, group, cols),
            array(BF16, group, cols),
            array(BF16, group, cols),
            array(BF16, cols, group),
            array(F32, group, cols),
            array(BF16, fsdp, shard, 3 * cols),
            array(F32, 8, group),
            array(F32, group, 128),
            array(jnp.int32, 1, group),
            array(F32, 8, depth),
        ),
        in_specs=[anywhere] * 9 + [vmem],
        out_specs=[anywhere] * 11 + [vmem] * 4,
        scratch_shapes=[
            low(ctx, tokens, depth), low(ctx, tokens, cols), low(fsdp, shard, 3 * cols),
            low(shard, 3 * cols), low(shard, 3 * cols), low(*out_shape), low(*up_shape),
            low(*down_shape), full(fsdp, 8, depth),
            low(group, cols), low(group, cols), low(group, cols), low(cols, group),
            low(cols, group), full(group, cols), low(group, cols),
            full(cols, BLOCK), full(8, BLOCK), full(8, BLOCK),
            dma((ctx, PIECES)), dma((3, ctx, PIECES)), dma((ctx,)), dma((ctx // 2, 2)),
            dma((fsdp,)), dma((2, lines)), dma((2,)), dma((fsdp,)), dma((fsdp,)),
            dma((3, fsdp, ctx)), dma((3, 2, ctx)), dma((3, peers, lines, ctx)), dma((3, lines, ctx)),
            dma((ctx, per)), dma((blocks,)), dma((7,)),
        ]
        + [full(*weight.shape) for weight in weights]
        + [dma((7,))],
        compiler_params=pltpu.CompilerParams(
            collective_id=0, has_side_effects=True, vmem_limit_bytes=VMEM_LIMIT
        ),
        name="forward",
    )(x, vf, *weights, small)


def chunk_order(i, ctx):
    return i % 2 * (ctx // 2) + i // 2


def reduce_line(plan, low, first, second):
    return second * plan.along + first if low else first * plan.along + second


def reduce_places(plan, j):
    low = j < plan.half
    return (low, plan.b if low else plan.a, plan.a if low else plan.b)


def feed_kernel(
    fsdp, ctx,
    o, x, dy, wo, gain, gu, wd,
    out, dx2, do, dg, s_wo, s_gu, s_wd, early,
    x2, h2, h2t, total, act, dgu,
    my_gu, my_wd, my_wo, got_gu, got_wd, got_wo, near_gu,
    gu_sem, gu_out, wd_sem, wd_out, wo_sem, wo_out, near_sem, near_out,
):
    plan = Plan(fsdp, ctx)
    core = plan.core
    sibling = (plan.line * 2 + 1 - core, plan.c)
    step = pl.program_id(0)
    last = pl.num_programs(0) - 1
    tokens, depth = x.shape
    chunk = wd.shape[0]
    blocks = tokens // BLOCK
    lines = plan.lines
    shard = depth // fsdp
    row_lines = my_wd.shape[1]
    row_count = my_wd.shape[3]
    slot = lax.rem(step, 2)
    side = plan.across

    def give(at):
        place = lax.rem(at, 2)
        for i in range(lines):
            plan.send(
                my_gu.at[place, i, 1 - core], got_gu.at[at, i], gu_out.at[place, i],
                gu_sem.at[at, i], sibling,
            )
        for i in range(row_lines):
            plan.send(
                my_wd.at[place, i, 1 - core], got_wd.at[at, i], wd_out.at[place, i],
                wd_sem.at[at, i], sibling,
            )

    def given(at):
        plan.draining = True
        give(at)
        plan.draining = False

    @pl.when(step == 0)
    def _():
        plan.greet_plane()

        def rows_of(b, carry):
            rows = pl.ds(pl.multiple_of(b * BLOCK, BLOCK), BLOCK)
            mid = x[rows, :].astype(F32) + nn(o[rows, :], wo[...])
            x2[rows, :] = mid
            rstd = lax.rsqrt(jnp.mean(mid * mid, axis=1, keepdims=True) + EPSILON)
            hv = (mid * rstd * gain[...]).astype(BF16)
            h2[rows, :] = hv
            h2t[:, rows] = hv.T
            total[rows, :] = mid
            dx2[rows, :] = jnp.zeros((BLOCK, depth), F32)
            return carry

        lax.fori_loop(0, blocks, rows_of, 0)

    @pl.when(jnp.logical_and(step >= 2, step < last))
    def _():
        given(step - 2)

    @pl.when(step < last)
    def _():
        def rows_of(b, carry):
            rows = pl.ds(pl.multiple_of(b * BLOCK, BLOCK), BLOCK)
            both_ = nn(h2[rows, :], gu[0])
            gate = both_[:, :chunk]
            up = both_[:, chunk:]
            da = nt(dy[rows, :], wd[...]).astype(BF16).astype(F32)
            sig = 1.0 / (1.0 + jnp.exp(-gate))
            silu = gate * sig
            av = (silu * up).astype(BF16)
            act[rows, :] = av
            dgate = (da * up * (sig * (1.0 + gate * (1.0 - sig)))).astype(BF16)
            dup = (da * silu).astype(BF16)
            dv = jnp.concatenate([dgate, dup], axis=1)
            dgu[rows, :] = dv
            total[rows, :] = total[rows, :] + nn(av, wd[...])
            dx2[rows, :] = dx2[rows, :] + nt(dv, gu[0])
            return carry

        lax.fori_loop(0, blocks, rows_of, 0)

        for part in range(depth // 512):
            at = slice(part * 512, (part + 1) * 512)
            val = tn(act[...], dy[:, at])
            for r in range(row_lines * 2):
                my_wd[slot, r // 2, r % 2, :, at] = val[
                    r * row_count : (r + 1) * row_count
                ].astype(BF16)

        rows_each = BLOCK // shard

        def weight(b, carry):
            rows = pl.ds(pl.multiple_of(b * BLOCK, BLOCK), BLOCK)
            val = nn(h2t[rows, :], dgu[...]).astype(BF16)
            for r in range(rows_each):
                my_gu[slot, b * (rows_each // 2) + r // 2, r % 2] = val[
                    r * shard : (r + 1) * shard
                ]
            return carry

        lax.fori_loop(0, depth // BLOCK, weight, 0)
        give(step)

    def over_plane(at):
        j = chunk_order(at, ctx)
        low, first, second = reduce_places(plan, j)
        for hop in range(1, side):
            to = lax.rem(first + hop, side)
            dev = (reduce_line(plan, low, to, second) * 2 + core, plan.c)
            for inner in range(side):
                plan.send(
                    got_gu.at[at, reduce_line(plan, low, to, inner)],
                    near_gu.at[at, hop - 1, inner], near_out.at[at, hop - 1, inner],
                    near_sem.at[at, hop - 1, inner], dev,
                )

    def collect(at):
        place = lax.rem(at, 2)
        for i in range(lines):
            plan.arrive(got_gu.at[at, i], gu_sem.at[at, i])

            @pl.when(at >= plan.early)
            def _(i=i):
                add_rows(s_gu.at[0, i], [my_gu.at[place, i, core], got_gu.at[at, i]])

            @pl.when(at < plan.early)
            def _(i=i):
                add_rows(got_gu.at[at, i], [my_gu.at[place, i, core], got_gu.at[at, i]])

        for early_at in range(plan.early):

            @pl.when(at == early_at)
            def _(early_at=early_at):
                over_plane(early_at)

        for i in range(row_lines):
            plan.arrive(got_wd.at[at, i], wd_sem.at[at, i])
            add_rows(s_wd.at[i], [my_wd.at[place, i, core], got_wd.at[at, i]])

    @pl.when(jnp.logical_and(step >= 1, step < last))
    def _():
        collect(step - 1)

    @pl.when(step == last)
    def _():
        dg[...] = jnp.zeros_like(dg)

        def rows_of(b, carry):
            rows = pl.ds(pl.multiple_of(b * BLOCK, BLOCK), BLOCK)
            out[rows, :] = total[rows, :].astype(BF16)
            mid = x2[rows, :]
            rstd = lax.rsqrt(jnp.mean(mid * mid, axis=1, keepdims=True) + EPSILON)
            xhat = mid * rstd
            dh = dx2[rows, :]
            u = dh * gain[...]
            dm = dy[rows, :].astype(F32) + rstd * (
                u - xhat * jnp.mean(u * xhat, axis=1, keepdims=True)
            )
            dx2[rows, :] = dm
            dg[0:1, :] = dg[0:1, :] + jnp.sum(dh * xhat, axis=0, keepdims=True)
            h2[rows, :] = dm.astype(BF16)
            return carry

        lax.fori_loop(0, blocks, rows_of, 0)
        rows_each = BLOCK // shard

        def weight_out(b, carry):
            at = pl.ds(pl.multiple_of(b * BLOCK, BLOCK), BLOCK)
            val = tn(o[:, at], h2[...]).astype(BF16)
            for r in range(rows_each):
                my_wo[b * (rows_each // 2) + r // 2, r % 2] = val[r * shard : (r + 1) * shard]
            return carry

        lax.fori_loop(0, depth // BLOCK, weight_out, 0)
        for i in range(lines):
            plan.send(my_wo.at[i, 1 - core], got_wo.at[i], wo_out.at[i], wo_sem.at[i], sibling)

        def rows_out(b, carry):
            rows = pl.ds(pl.multiple_of(b * BLOCK, BLOCK), BLOCK)
            do[rows, :] = nt(h2[rows, :], wo[...]).astype(BF16)
            return carry

        lax.fori_loop(0, blocks, rows_out, 0)
        collect(last - 1)
        for i in range(lines):
            plan.arrive(got_wo.at[i], wo_sem.at[i])
            add_rows(s_wo.at[i], [my_wo.at[i, core], got_wo.at[i]])
        for at in (last - 2, last - 1):
            given(at)
        for at in range(plan.early):
            low, first, _ = reduce_places(plan, chunk_order(at, ctx))
            for inner in range(side):
                for hop in range(1, side):
                    plan.arrive(near_gu.at[at, hop - 1, inner], near_sem.at[at, hop - 1, inner])
                add_rows(
                    early.at[at, inner],
                    [got_gu.at[at, reduce_line(plan, low, first, inner)]]
                    + [near_gu.at[at, hop - 1, inner] for hop in range(1, side)],
                )
        plan.draining = True
        for at in range(plan.early):
            over_plane(at)
        for i in range(lines):
            plan.send(my_wo.at[i, 1 - core], got_wo.at[i], wo_out.at[i], wo_sem.at[i], sibling)
        plan.draining = False


def feed_forward(mesh, o, x, dy, wo, gain, gu, wd):
    fsdp, ctx = mesh.shape["fsdp"], mesh.shape["ctx"]
    tokens, depth = x.shape
    steps, _, width = gu.shape
    chunk = width // 2
    lines = fsdp // 2
    shard = depth // fsdp
    row_count = wd.shape[0] // fsdp
    row_lines = fsdp // ctx // 2
    side = math.isqrt(lines)
    early = early_chunks(ctx)
    hops = max(side - 1, 1)
    once = pl.Buffered(1)

    def chunk_of(i):
        return chunk_order(jnp.minimum(i, steps - 1), ctx)

    def chunk_before(i):
        return chunk_order(jnp.maximum(i - 1, 0), ctx)

    def whole(shape):
        return pl.BlockSpec(shape, lambda i: (0,) * len(shape), pipeline_mode=once)

    def whole_out(shape):
        return pl.BlockSpec(shape, lambda i: (0,) * len(shape), pipeline_mode=once)

    shapes = (
        jax.ShapeDtypeStruct((tokens, depth), BF16),
        jax.ShapeDtypeStruct((tokens, depth), F32),
        jax.ShapeDtypeStruct((tokens, depth), BF16),
        jax.ShapeDtypeStruct((8, depth), F32),
        jax.ShapeDtypeStruct((lines, shard, depth), BF16),
        jax.ShapeDtypeStruct((ctx - early, lines, shard, width), BF16),
        jax.ShapeDtypeStruct((lines, row_count, depth), BF16),
        jax.ShapeDtypeStruct((early, side, shard, width), BF16),
    )
    dma = pltpu.SemaphoreType.DMA
    return pl.pallas_call(
        functools.partial(feed_kernel, fsdp, ctx),
        grid=(steps + 1,),
        out_shape=shapes,
        in_specs=[
            whole((tokens, depth)),
            whole((tokens, depth)),
            whole((tokens, depth)),
            whole((depth, depth)),
            whole((1, depth)),
            pl.BlockSpec((1, depth, width), lambda i: (chunk_of(i), 0, 0)),
            pl.BlockSpec((chunk, depth), lambda i: (chunk_of(i), 0)),
        ],
        out_specs=[
            whole_out((tokens, depth)),
            whole_out((tokens, depth)),
            whole_out((tokens, depth)),
            whole_out((8, depth)),
            whole_out((lines, shard, depth)),
            pl.BlockSpec(
                (1, lines, shard, width), lambda i: (jnp.maximum(i - 1 - early, 0), 0, 0, 0)
            ),
            pl.BlockSpec((row_lines, row_count, depth), lambda i: (chunk_before(i), 0, 0)),
            whole_out((early, side, shard, width)),
        ],
        scratch_shapes=[
            pltpu.VMEM((tokens, depth), F32),
            pltpu.VMEM((tokens, depth), BF16),
            pltpu.VMEM((depth, tokens), BF16),
            pltpu.VMEM((tokens, depth), F32),
            pltpu.VMEM((tokens, chunk), BF16),
            pltpu.VMEM((tokens, width), BF16),
            pltpu.VMEM((2, lines, 2, shard, width), BF16),
            pltpu.VMEM((2, row_lines, 2, row_count, depth), BF16),
            pltpu.VMEM((lines, 2, shard, depth), BF16),
            pltpu.VMEM((steps, lines, shard, width), BF16),
            pltpu.VMEM((steps, row_lines, row_count, depth), BF16),
            pltpu.VMEM((lines, shard, depth), BF16),
            pltpu.VMEM((early, hops, side, shard, width), BF16),
            dma((steps, lines)), dma((2, lines)), dma((steps, row_lines)), dma((2, row_lines)),
            dma((lines,)), dma((lines,)), dma((early, hops, side)), dma((early, hops, side)),
        ],
        compiler_params=pltpu.CompilerParams(
            vmem_limit_bytes=VMEM_LIMIT, dimension_semantics=("arbitrary",), collective_id=4,
            has_side_effects=True,
        ),
        name="feed_forward",
    )(o, x, dy, wo, gain, gu, wd)


def chunk_rows(count):
    return 32 if count % 32 == 0 else count


def add_rows(dst, parts):
    count = dst.shape[0]
    rows = chunk_rows(count)

    def body(t, carry):
        at = pl.ds(pl.multiple_of(t * rows, rows), rows)
        total = parts[0][at, :].astype(F32)
        for part in parts[1:]:
            total = total + part[at, :].astype(F32)
        dst[at, :] = total.astype(dst.dtype)
        return carry

    lax.fori_loop(0, count // rows, body, 0)


class Reduction:
    def __init__(self, plan, sources, early, own, near, next_, last, outs, sems):
        self.plan = plan
        self.sources, self.early, self.own, self.near, self.next, self.last, self.outs = (
            sources, early, own, near, next_, last, outs,
        )
        (
            self.own_sem, self.near_sem, self.near_out, self.next_sem, self.next_out,
            self.last_sem, self.last_out,
        ) = sems
        self.side = plan.across
        ctx = plan.ctx
        self.chunks = [chunk_order(i, ctx) for i in range(ctx)]
        self.first_set = [(1, j) for j in self.chunks[: plan.early]]
        self.second_set = [(1, j) for j in self.chunks[plan.early :]]
        self.third_set = [(i, j) for i in (0, 2) for j in self.chunks]

    def piece(self, i, line, j):
        src = self.sources[i]
        if i == 1:
            return src.at[self.chunks.index(j) - self.plan.early, line]
        width = src.shape[2] // self.plan.ctx
        return src.at[line, :, pl.ds(j * width, width)]

    def send_next(self, i, j, source):
        plan = self.plan
        low, first, second = reduce_places(plan, j)
        for hop in range(1, self.side):
            to = lax.rem(second + hop, self.side)
            plan.send(
                source(to),
                self.next[i].at[j, hop - 1],
                self.next_out.at[i, j, hop - 1],
                self.next_sem.at[i, j, hop - 1],
                (reduce_line(plan, low, first, to) * 2 + plan.core, plan.c),
            )

    def start_early(self):
        plan = self.plan
        for at, (i, j) in enumerate(self.first_set):
            self.send_next(i, j, lambda to, at=at: self.early.at[at, to])
            for inner in range(self.side):
                plan.keep(
                    self.early.at[at, inner], self.own[i].at[j, inner], self.own_sem.at[i, j, inner]
                )

    def start(self, pairs):
        plan = self.plan
        for i, j in pairs:
            low, first, second = reduce_places(plan, j)
            for hop in range(1, self.side):
                to = lax.rem(first + hop, self.side)
                dev = (reduce_line(plan, low, to, second) * 2 + plan.core, plan.c)
                for inner in range(self.side):
                    plan.send(
                        self.piece(i, reduce_line(plan, low, to, inner), j),
                        self.near[i].at[j, hop - 1, inner],
                        self.near_out.at[i, j, hop - 1, inner],
                        self.near_sem.at[i, j, hop - 1, inner],
                        dev,
                    )
            for inner in range(self.side):
                plan.keep(
                    self.piece(i, reduce_line(plan, low, first, inner), j),
                    self.own[i].at[j, inner],
                    self.own_sem.at[i, j, inner],
                )

    def step_near(self, pairs):
        plan = self.plan
        for i, j in pairs:
            for inner in range(self.side):
                plan.arrive(self.own[i].at[j, inner], self.own_sem.at[i, j, inner])
                for hop in range(1, self.side):
                    plan.arrive(
                        self.near[i].at[j, hop - 1, inner], self.near_sem.at[i, j, hop - 1, inner]
                    )
                if not plan.draining:
                    add_rows(
                        self.own[i].at[j, inner],
                        [self.own[i].at[j, inner]]
                        + [self.near[i].at[j, hop - 1, inner] for hop in range(1, self.side)],
                    )
            self.send_next(i, j, lambda to, i=i, j=j: self.own[i].at[j, to])

    def step_next(self, pairs):
        plan = self.plan
        for i, j in pairs:
            _, _, second = reduce_places(plan, j)
            if (i, j) in self.first_set:
                for inner in range(self.side):
                    plan.arrive(self.own[i].at[j, inner], self.own_sem.at[i, j, inner])
            for hop in range(1, self.side):
                plan.arrive(self.next[i].at[j, hop - 1], self.next_sem.at[i, j, hop - 1])
            if not plan.draining:
                add_rows(
                    self.own[i].at[j, second],
                    [self.own[i].at[j, second]]
                    + [self.next[i].at[j, hop - 1] for hop in range(1, self.side)],
                )
            self.send_last(i, j, second, both(plan.c == 0, j > 0), both(plan.c == plan.ctx - 1, j < plan.ctx - 1))

    def send_last(self, i, j, second, up, down):
        plan = self.plan
        if up is not None:
            plan.send(
                self.own[i].at[j, second], self.last[i].at[j], self.last_out.at[i, j],
                self.last_sem.at[i, j], (plan.f, plan.c + 1), up,
            )
        if down is not None:
            slot = jnp.where(plan.c - 1 == j, plan.ctx, j)
            plan.send(
                self.own[i].at[j, second], self.last[i].at[slot], self.last_out.at[i, j],
                self.last_sem.at[i, slot], (plan.f, plan.c - 1), down,
            )

    def step_pass(self, pairs, hop):
        plan = self.plan
        for i, j in pairs:
            _, _, second = reduce_places(plan, j)
            up = both(plan.c == hop, plan.c < j) if hop < j else None
            down = both(plan.c == plan.ctx - 1 - hop, plan.c > j) if plan.ctx - 1 - hop > j else None
            for cond in (up, down):
                if cond is not None and not plan.draining:

                    @pl.when(cond)
                    def _(i=i, j=j, second=second):
                        plan.arrive(self.last[i].at[j], self.last_sem.at[i, j])
                        add_rows(
                            self.own[i].at[j, second],
                            [self.own[i].at[j, second], self.last[i].at[j]],
                        )

            self.send_last(i, j, second, up, down)

    def finish(self):
        plan = self.plan
        for i in range(3):
            count = self.outs[i].shape[0]
            rows = chunk_rows(count)
            slots = ((plan.c > 0, plan.c), (plan.c < plan.ctx - 1, plan.ctx))
            for there, slot in slots:
                plan.arrive(self.last[i].at[slot], self.last_sem.at[i, slot], there)

            def body(t, carry, i=i, rows=rows):
                at = pl.ds(pl.multiple_of(t * rows, rows), rows)
                for j in range(plan.ctx):
                    _, _, second = reduce_places(plan, j)

                    @pl.when(plan.c == j)
                    def _(j=j, second=second):
                        total = self.own[i][j, second, at, :].astype(F32)
                        if j > 0:
                            total = total + self.last[i][j, at, :].astype(F32)
                        if j < plan.ctx - 1:
                            total = total + self.last[i][plan.ctx, at, :].astype(F32)
                        self.outs[i][at, :] = total

                return carry

            lax.fori_loop(0, count // rows, body, 0)


def backward_kernel(
    fsdp, ctx,
    d_out, x_in, q_in, k_in, vm_in, kt_in, att_in, lse, wqkv_in, gain, table_in, start,
    dg_two, s_wo, s_gu, s_wd, early,
    folded, vout, g_wo, g_gu, g_wd, g_qkv, dg_all,
    part, q, k, vm, kt, att, do, wqkv, table,
    dqt, dkk, dvv, rows_t, d3, gw_full, gw,
    other, chain, gw_near, gw_sum, gw_last, dg, dg_near, dg_sum, dg_last,
    o_wo, o_gu, o_wd, n_wo, n_gu, n_wd, x_wo, x_gu, x_wd, l_wo, l_gu, l_wd,
    load_sem, do_sem, do_out, v_sem, v_out,
    sib_sem, sib_out, chain_sem, chain_out, end_sem, end_out,
    gw_sem, gw_out, gl_sem, gl_out, dn_sem, dn_out, dl_sem, dl_out,
    own_sem, near_sem, near_out, next_sem, next_out, last_sem, last_out,
):
    plan = Plan(fsdp, ctx)
    f, c, core, line, home, half = plan.f, plan.c, plan.core, plan.line, plan.home, plan.half
    lines = plan.lines
    sibling = (line * 2 + 1 - core, c)
    low, high = home * half, home * half + half - 1
    blocks, _, depth = part.shape
    group = blocks * BLOCK
    cols = vm.shape[1]
    heads = cols // HEAD
    tokens = group // ctx
    per = tokens // BLOCK
    pairs = blocks // 2
    plan.barrier()

    for i in range(half):
        for kk in range(2):
            to = core * half + i
            rank = lax.rem(to + kk * half, ctx)
            src = d_out.at[:, pl.ds(pl.multiple_of(rank * cols, cols), cols)]
            mine = both(core == home, c == to, core == kk)
            plan.send(
                src, do.at[c], do_out.at[i * 2 + kk], do_sem.at[c], (line * 2 + kk, to),
                jnp.logical_not(mine),
            )
            plan.keep(src, do.at[c], do_sem.at[c], mine)
    loads = (
        (q_in, q), (k_in, k), (vm_in, vm), (kt_in, kt), (att_in, att), (table_in, table),
        (wqkv_in, wqkv), (x_in, part),
    )
    for i, (src, dst) in enumerate(loads):
        plan.keep(src, dst, load_sem.at[i])
    reduction = Reduction(
        plan, (s_wo, s_gu, s_wd), early, (o_wo, o_gu, o_wd), (n_wo, n_gu, n_wd), (x_wo, x_gu, x_wd),
        (l_wo, l_gu, l_wd), (g_wo, g_gu, g_wd),
        (own_sem, near_sem, near_out, next_sem, next_out, last_sem, last_out),
    )
    reduction.start_early()
    reduction.start(reduction.second_set)
    reduction.start(reduction.third_set)

    dqt[...] = jnp.zeros_like(dqt)
    dkk[...] = jnp.zeros_like(dkk)
    dvv[...] = jnp.zeros_like(dvv)
    gw_full[...] = jnp.zeros_like(gw_full)
    dg[...] = jnp.zeros_like(dg)
    dg[1:2, :] = dg_two[0:1, :]
    for i, (src, dst) in enumerate(loads):
        plan.arrive(dst, load_sem.at[i])
    for j in range(ctx):
        plan.arrive(do.at[j], do_sem.at[j])

    def grads_of(b):
        return do[b // per, pl.ds(pl.multiple_of(lax.rem(b, per) * BLOCK, BLOCK), BLOCK), :]

    def dots(b, carry):
        rows = pl.ds(pl.multiple_of(b * BLOCK, BLOCK), BLOCK)
        prod = grads_of(b).astype(F32) * att[rows, :]
        upper = prod.astype(BF16)
        lower = (prod - upper.astype(F32)).astype(BF16)
        head_row = lax.broadcasted_iota(jnp.int32, (8, cols), 0)
        lane = lax.broadcasted_iota(jnp.int32, (8, cols), 1)
        choose = (lane // HEAD == head_row).astype(F32).astype(BF16)
        rows_t[:, rows] = nt(choose, upper) + nt(choose, lower)
        return carry

    lax.fori_loop(0, blocks, dots, 0)

    def tile(kb, qb):
        krows = pl.ds(pl.multiple_of(kb * BLOCK, BLOCK), BLOCK)
        rows = pl.ds(pl.multiple_of(qb * BLOCK, BLOCK), BLOCK)
        kv = k[krows, :]
        vv = vm[krows, :]
        qv = q[rows, :]
        dov = grads_of(qb)
        key_pos = kb * BLOCK + lax.broadcasted_iota(jnp.int32, (BLOCK, BLOCK), 0)
        query_pos = qb * BLOCK + lax.broadcasted_iota(jnp.int32, (BLOCK, BLOCK), 1)
        allowed = (key_pos <= query_pos) & (key_pos >= start[0:1, rows])
        dk_sum = dkk[krows, :]
        dv_sum = dvv[krows, :]
        for head in range(heads):
            band = slice(head * HEAD, (head + 1) * HEAD)
            lanes = head_lanes(qv.shape, head)
            qm = jnp.where(lanes, qv, jnp.zeros_like(qv))
            dom = jnp.where(lanes, dov, jnp.zeros_like(dov))
            s = jnp.where(allowed, nt(kv, qm), NEGATIVE)
            p = jnp.exp(s - lse[head : head + 1, rows])
            ds = (p * (nt(vv, dom) - rows_t[head : head + 1, rows])).astype(BF16)
            dv_sum = dv_sum + nn(p.astype(BF16), dom)
            dk_sum = dk_sum + nn(ds, qm)
            dqt[band, rows] = dqt[band, rows] + nn(kt[band, krows], ds)
        dkk[krows, :] = dk_sum
        dvv[krows, :] = dv_sum

    def unit_of(t):
        return jnp.where(home == 0, blocks - 1 - t, t)

    def finish(o):
        rows = pl.ds(pl.multiple_of(o * BLOCK, BLOCK), BLOCK)
        cos_v, sin_v = turns(table[rows, :], cols)
        dq = dqt[:, rows].T * (1.0 / math.sqrt(HEAD))
        d3[rows, :cols] = (dq * cos_v - half_swap(dq) * sin_v).astype(BF16)
        dk = dkk[rows, :]
        d3[rows, cols : 2 * cols] = (dk * cos_v - half_swap(dk) * sin_v).astype(BF16)
        d3[rows, 2 * cols :] = (0.5 * dvv[rows, :]).astype(BF16)
        dh = nt(d3[rows, :], wqkv[...])
        xv = part[o].astype(F32)
        rstd = lax.rsqrt(jnp.mean(xv * xv, axis=1, keepdims=True) + EPSILON)
        xhat = xv * rstd
        h1 = (xhat * gain[...]).astype(BF16)
        u = dh * gain[...]
        part[o] = (rstd * (u - xhat * jnp.mean(u * xhat, axis=1, keepdims=True))).astype(BF16)
        dg[0:1, :] = dg[0:1, :] + jnp.sum(dh * xhat, axis=0, keepdims=True)
        gw_full[...] = gw_full[...] + tn(h1, d3[rows, :])

    def give(t):
        o = unit_of(t)
        slot = t // 2
        plan.send(
            part.at[o], other.at[slot], sib_out.at[slot], sib_sem.at[slot], sibling,
            lax.rem(o, 2) != core,
        )

    def pair_unit(i):
        return jnp.where(home == 0, blocks - 2 - 2 * i, 2 * i) + core

    def add_unit(o, src):
        def body(t, carry):
            at = pl.ds(pl.multiple_of(t * 32, 32), 32)
            part[o, at, :] = (part[o, at, :].astype(F32) + src[at, :].astype(F32)).astype(BF16)
            return carry

        lax.fori_loop(0, BLOCK // 32, body, 0)

    def sum_pair(i):
        plan.arrive(other.at[i], sib_sem.at[i])
        if not plan.draining:
            add_unit(pair_unit(i), other.at[i])

    def pass_pair(i, hears):
        o = pair_unit(i)
        j = o // per
        top = jnp.minimum(j, high)
        bottom = jnp.maximum(j, low)
        from_below = both(c > low, c <= top)
        from_above = both(c < high, c >= bottom)
        now = jnp.logical_or(from_below, from_above) == hears
        spot = jnp.where(j == c, pairs, i)
        if hears and not plan.draining:

            @pl.when(from_below)
            def _():
                plan.arrive(chain.at[i], chain_sem.at[i])
                add_unit(o, chain.at[i])

            @pl.when(from_above)
            def _():
                plan.arrive(chain.at[spot], chain_sem.at[spot])
                add_unit(o, chain.at[spot])

        plan.send(
            part.at[o], chain.at[i], chain_out.at[0, i], chain_sem.at[i], (f, c + 1),
            both(now, c < top),
        )
        below = jnp.where(j == c - 1, pairs, i)
        plan.send(
            part.at[o], chain.at[below], chain_out.at[1, i], chain_sem.at[below], (f, c - 1),
            both(now, c > bottom),
        )
        end = jnp.clip(j, low, high)
        mine = both(c == end, j == c, core == home)
        where = lax.rem(o, per)
        dst = folded.at[pl.ds(pl.multiple_of(where * BLOCK, BLOCK), BLOCK), :]
        plan.send(
            part.at[o], dst, end_out.at[i], end_sem.at[where], (line * 2 + home, j),
            both(now, c == end, jnp.logical_not(mine)),
        )
        plan.keep(part.at[o], dst, end_sem.at[where], both(now, mine))

    rank = lax.rem(c + core * half, ctx)

    def give_values(i):
        j = jnp.where(home == 0, ctx - 1 - i, i)
        src = d3.at[pl.ds(pl.multiple_of(j * tokens, tokens), tokens), 2 * cols : 3 * cols]
        dst = vout.at[:, pl.ds(pl.multiple_of(rank * cols, cols), cols)]
        mine = both(core == home, c == j)
        plan.send(
            src, dst, v_out.at[i], v_sem.at[rank], (line * 2 + home, j), jnp.logical_not(mine)
        )
        plan.keep(src, dst, v_sem.at[rank], mine)

    schedule = {}
    schedule_first = []
    schedule_last = []

    def at_step(t, act):
        schedule.setdefault(t, []).append(act)

    scale = blocks // 8
    for kind, which, place in REDUCE_STEPS:
        pairs_of = getattr(reduction, which)
        if place < 0:
            schedule_first.append(functools.partial(getattr(reduction, kind), pairs_of))
            continue
        if kind != "step_pass":
            at_step(place * scale, functools.partial(getattr(reduction, kind), pairs_of))
            continue
        for hop in range(1, ctx - 1):
            act = functools.partial(reduction.step_pass, pairs_of, hop)
            when = place + PASS_GAP * (hop - 1)
            if when < 8 and hop < 3:
                at_step(when * scale, act)
            else:
                schedule_last.append(act)
    for i in range(pairs - 1):
        at_step(2 * i + 1, lambda i=i: give_values(i))
        at_step(2 * i + 2, lambda i=i: sum_pair(i))
        at_step(2 * i + 2, lambda i=i: pass_pair(i, False))
        if i < pairs - 2:
            at_step(2 * i + 4, lambda i=i: pass_pair(i, True))
    at_step(blocks - 1, lambda: give_values(pairs - 1))

    def step(t, carry):
        o = unit_of(t)

        def inner(i, carry2):
            tile(jnp.where(home == 0, i, o), jnp.where(home == 0, o, o + i))
            return carry2

        lax.fori_loop(0, blocks - t, inner, 0)
        finish(o)
        give(t)
        for s in sorted(schedule):

            @pl.when(t == s)
            def _(s=s):
                for act in schedule[s]:
                    act()

        return carry

    for act in schedule_first:
        act()
    kept = plan.started
    plan.started = []
    lax.fori_loop(0, blocks, step, 0)
    plan.started = kept

    for hop in range(1, fsdp):
        dev = (lax.rem(f + hop, fsdp), c)
        plan.send(dg, dg_near.at[f], dn_out.at[hop - 1], dn_sem.at[f], dev)
    plan.keep(dg, dg_near.at[f], dn_sem.at[f])

    sum_pair(pairs - 1)
    pass_pair(pairs - 1, False)
    shard = depth // fsdp
    rows_each = BLOCK // shard

    def weight(b, carry):
        at = pl.ds(pl.multiple_of(b * BLOCK, BLOCK), BLOCK)
        val = gw_full[at, :].astype(BF16)
        for r in range(rows_each):
            gw[b * (rows_each // 2) + r // 2, r % 2] = val[r * shard : (r + 1) * shard]
        return carry

    lax.fori_loop(0, depth // BLOCK, weight, 0)
    for i in range(3):
        for hop in range(1, lines):
            to = lax.rem(line + hop, lines)
            plan.send(
                gw.at[to, :, :, pl.ds(i * cols, cols)],
                gw_near.at[hop - 1, :, :, pl.ds(i * cols, cols)],
                gw_out.at[i, hop - 1], gw_sem.at[i, hop - 1], (to * 2 + core, c),
            )
    pass_pair(pairs - 2, True)
    pass_pair(pairs - 1, True)

    for at in range(fsdp):
        plan.arrive(dg_near.at[at], dn_sem.at[at])
    total = dg_near[0]
    for at in range(1, fsdp):
        total = total + dg_near[at]
    dg_sum[...] = total
    for hop in range(1, ctx):
        plan.send(
            dg_sum, dg_last.at[c], dl_out.at[hop - 1], dl_sem.at[c], (f, lax.rem(c + hop, ctx))
        )
    plan.keep(dg_sum, dg_last.at[c], dl_sem.at[c])

    plane = jnp.where(core == 0, c, lax.rem(c + half, ctx))
    for i in range(3):
        band = pl.ds(i * cols, cols)
        for hop in range(1, lines):
            plan.arrive(gw_near.at[hop - 1, :, :, band], gw_sem.at[i, hop - 1])
        for kk in range(2):
            add_rows(
                gw_sum.at[kk, :, band],
                [gw.at[line, kk, :, band]]
                + [gw_near.at[hop - 1, kk, :, band] for hop in range(1, lines)],
            )
            mine = both(core == 0, kk == 0)
            src, dst = gw_sum.at[kk, :, band], gw_last.at[core, :, band]
            plan.send(
                src, dst, gl_out.at[kk, i], gl_sem.at[core, i], (line * 2 + kk, plane),
                jnp.logical_not(mine),
            )
            plan.keep(src, dst, gl_sem.at[core, i], mine)

    for act in schedule_last:
        act()
    reduction.finish()
    for at in range(ctx):
        plan.arrive(dg_last.at[at], dl_sem.at[at])
    total = dg_last[0]
    for at in range(1, ctx):
        total = total + dg_last[at]
    dg_all[...] = total
    for kk in range(2):
        for i in range(3):
            plan.arrive(gw_last.at[kk, :, pl.ds(i * cols, cols)], gl_sem.at[kk, i])
    add_rows(g_qkv, [gw_last.at[0], gw_last.at[1]])
    for at in range(per):
        plan.arrive(folded.at[pl.ds(at * BLOCK, BLOCK), :], end_sem.at[at])
    for at in range(ctx):
        plan.arrive(vout.at[:, pl.ds(at * cols, cols)], v_sem.at[at])
    plan.drain()
    plan.draining = True
    for t in range(blocks):
        give(t)
    for s in sorted(schedule):
        for act in schedule[s]:
            act()


PASS_GAP = 1
REDUCE_STEPS = (
    ("step_near", "second_set", 0),
    ("step_next", "first_set", 0),
    ("step_near", "third_set", 1),
    ("step_next", "second_set", 2),
    ("step_pass", "first_set", 2),
    ("step_next", "third_set", 3),
    ("step_pass", "second_set", 4),
    ("step_pass", "third_set", 6),
)


def backward(mesh, d_out, x, q, k, vm, kt, att, lse, wqkv, gain, table, start, dg_two, sums):
    fsdp, ctx = mesh.shape["fsdp"], mesh.shape["ctx"]
    group, depth = x.shape
    cols = vm.shape[1]
    tokens = group // ctx
    blocks = group // BLOCK
    x = x.reshape(blocks, BLOCK, depth)
    pairs = blocks // 2
    half = ctx // 2
    lines = fsdp // 2
    side = math.isqrt(lines)
    shard = depth // fsdp
    s_wo, s_gu, s_wd, _ = sums
    shapes = (
        (s_wo.shape[1], s_wo.shape[2] // ctx),
        (s_gu.shape[2], s_gu.shape[3]),
        (s_wd.shape[1], s_wd.shape[2] // ctx),
    )
    anywhere = pl.BlockSpec(memory_space=pl.ANY)
    vmem = pl.BlockSpec(memory_space=pltpu.VMEM)
    dma = pltpu.SemaphoreType.DMA
    hops = max(side - 1, 1)

    def low(*shape):
        return pltpu.VMEM(shape, BF16)

    def full(*shape):
        return pltpu.VMEM(shape, F32)

    return pl.pallas_call(
        functools.partial(backward_kernel, fsdp, ctx),
        out_shape=(
            jax.ShapeDtypeStruct((tokens, depth), BF16),
            jax.ShapeDtypeStruct((tokens, depth), BF16),
            jax.ShapeDtypeStruct(shapes[0], F32),
            jax.ShapeDtypeStruct(shapes[1], F32),
            jax.ShapeDtypeStruct(shapes[2], F32),
            jax.ShapeDtypeStruct((shard, 3 * cols), F32),
            jax.ShapeDtypeStruct((8, depth), F32),
        ),
        in_specs=[anywhere] * 7 + [vmem, anywhere, vmem] + [anywhere] + [vmem] * 2 + [anywhere] * 4,
        out_specs=[anywhere] * 2 + [vmem] * 5,
        scratch_shapes=[
            low(blocks, BLOCK, depth), low(group, cols), low(group, cols), low(group, cols),
            low(cols, group), full(group, cols), low(ctx, tokens, cols), low(depth, 3 * cols),
            full(group, table.shape[1]),
            full(cols, group), full(group, cols), full(group, cols),
            full(8, group), low(group, 3 * cols), full(depth, 3 * cols), low(lines, 2, shard, 3 * cols),
            low(pairs, BLOCK, depth), low(pairs + 1, BLOCK, depth),
            low(max(lines - 1, 1), 2, shard, 3 * cols), low(2, shard, 3 * cols),
            low(2, shard, 3 * cols),
            full(8, depth), full(fsdp, 8, depth), full(8, depth), full(ctx, 8, depth),
        ]
        + [low(ctx, side, *shape) for shape in shapes]
        + [low(ctx, hops, side, *shape) for shape in shapes]
        + [low(ctx, hops, *shape) for shape in shapes]
        + [low(ctx + 1, *shape) for shape in shapes]
        + [
            dma((8,)), dma((ctx,)), dma((ctx,)), dma((ctx,)), dma((ctx,)),
            dma((pairs,)), dma((pairs,)), dma((pairs + 1,)), dma((2, pairs)),
            dma((tokens // BLOCK,)), dma((pairs,)),
            dma((3, lines)), dma((3, lines)), dma((2, 3)), dma((2, 3)),
            dma((fsdp,)), dma((fsdp,)), dma((ctx,)), dma((ctx,)),
            dma((3, ctx, side)), dma((3, ctx, hops, side)), dma((3, ctx, hops, side)),
            dma((3, ctx, hops)), dma((3, ctx, hops)), dma((3, ctx + 1)), dma((3, ctx)),
        ],
        compiler_params=pltpu.CompilerParams(
            collective_id=3, has_side_effects=True, vmem_limit_bytes=BACKWARD_LIMIT
        ),
        name="backward",
    )(d_out, x, q, k, vm, kt, att, lse, wqkv, gain, table, start, dg_two, *sums)


def layer(
    mesh, tokens, value_first, lengths, w_query, w_key, w_value, w_out, w_gate, w_up, w_down,
    gain_attn, gain_ffn, out_grad, value_grad,
):
    fsdp, ctx = mesh.shape["fsdp"], mesh.shape["ctx"]
    count, depth = tokens.shape
    group = count * ctx
    cols = depth // ctx
    rows = depth // fsdp
    f, c = lax.axis_index("fsdp"), lax.axis_index("ctx")
    small = jnp.stack([gain_attn, gain_ffn]).astype(BF16).astype(F32)
    small = lax.dynamic_update_slice(
        jnp.zeros((8, depth), F32), small, (jnp.int32(0), (f * rows).astype(jnp.int32))
    )
    small = lax.dynamic_update_slice(small, lengths.astype(F32), (2, 0))
    (
        attended, wos, gus, wds, xs, q, k, vm, kt, att, wq, lse, table, first, gains
    ) = forward(
        mesh, tokens, value_first, (w_query, w_key, w_value, w_out, w_gate, w_up, w_down), small
    )
    gain_one, gain_two = gains[0:1], gains[1:2]
    wq = wq.reshape(depth, 3 * cols)
    result, dx2, d_out, dg_two, *sums = feed_forward(
        mesh, attended, tokens, out_grad, wos.reshape(depth, depth), gain_two,
        gus.reshape(ctx, depth, -1), wds.reshape(-1, depth),
    )
    folded, dvr, g_wo, g_gu, g_wd, g_qkv, gain_grads = backward(
        mesh, d_out, xs.reshape(group, depth), q, k, vm, kt, att, lse, wq, gain_one, table, first, dg_two,
        sums,
    )
    gain_grads = lax.dynamic_slice(
        gain_grads, (jnp.int32(0), (f * rows).astype(jnp.int32)), (2, rows)
    )
    ff = w_gate.shape[1]
    return (
        result,
        dx2 + folded.astype(F32),
        value_grad + dvr.astype(F32),
        g_qkv[:, :cols],
        g_qkv[:, cols : 2 * cols],
        g_qkv[:, 2 * cols :],
        g_wo,
        g_gu[:, :ff],
        g_gu[:, ff:],
        g_wd,
        gain_grads[0],
        gain_grads[1],
    )


def solution(mesh):
    rows = P(("fsdp", "ctx"), None)
    shard = P("fsdp", "ctx")
    return jax.shard_map(
        functools.partial(layer, mesh),
        mesh=mesh,
        in_specs=(rows, rows, P("fsdp", None)) + (shard,) * 7 + (P("fsdp"),) * 2 + (rows, rows),
        out_specs=(rows, rows, rows) + (shard,) * 7 + (P("fsdp"),) * 2,
        check_vma=False,
    )
```
